128 devices in a mesh: dp: 64 (over x, y, z_lo, core), expert: 2 (over z_hi).
Axes of the slice: x: 4, y: 4, z: 4 (z_hi: 2, z_lo: 2; z = z_hi * 2 + z_lo), core: 2. Of those that a mesh axis runs over, the one named last changes fastest.
Arguments:
- inputs: bfloat16 [49152, 1536], P(('dp', 'expert')), may hold values from -6 to 6
- cotangent: bfloat16 [49152, 1536], P(('dp', 'expert')), may hold values from -24 to 24
- norm_one: float32 [1536], replicated, may hold values from 0.5 to 1.5
- kv_weight: bfloat16 [1536, 1024], replicated, may hold values from -0.15625 to 0.15625
- attn_router: bfloat16 [1536, 8], replicated, may hold values from -0.109375 to 0.109375
- query_experts: bfloat16 [8, 1536, 512], P('expert'), may hold values from -0.15625 to 0.15625
- out_experts: bfloat16 [8, 512, 1536], P('expert'), may hold values from -2 to 2
- norm_two: float32 [1536], replicated, may hold values from 0.5 to 1.5
- mlp_router: bfloat16 [1536, 8], replicated, may hold values from -0.109375 to 0.109375
- gate_experts: bfloat16 [8, 1536, 512], P('expert'), may hold values from -0.15625 to 0.15625
- up_experts: bfloat16 [8, 1536, 512], P('expert'), may hold values from -0.15625 to 0.15625
- down_experts: bfloat16 [8, 512, 1536], P('expert'), may hold values from -0.25 to 0.25
- attn_routes: int32 [64, 2, 384, 2], P('dp'), may hold values from 0 to 7, all different within a row
- mlp_routes: int32 [64, 2, 384, 2], P('dp'), may hold values from 0 to 7, all different within a row
- slot_order: int32 [64, 2, 2, 768], P('dp'), may hold values from 0 to 767, each once within a row
- seg_lengths: int32 [64, 2, 13], P('dp'), may hold values from 12 to 240, as said below
- seg_parents: int32 [64, 2, 13], P('dp'), may hold values from 0 to 4, as said below
Outputs:
- output: bfloat16 [49152, 1536], P(('dp', 'expert'))
- input_grad: bfloat16 [49152, 1536], P(('dp', 'expert'))
- norm_one_grad: float32 [1536], P(('dp', 'expert'))
- kv_weight_grad: float32 [1536, 1024], P(('dp', 'expert'))
- attn_router_grad: float32 [1536, 8], P(('dp', 'expert'))
- query_grad: float32 [8, 1536, 512], P('expert', 'dp')
- out_grad: float32 [8, 512, 1536], P('expert', 'dp')
- norm_two_grad: float32 [1536], P(('dp', 'expert'))
- mlp_router_grad: float32 [1536, 8], P(('dp', 'expert'))
- gate_grad: float32 [8, 1536, 512], P('expert', 'dp')
- up_grad: float32 [8, 1536, 512], P('expert', 'dp')
- down_grad: float32 [8, 512, 1536], P('expert', 'dp')
The draws below stay inside these ranges and needn't reach their ends.
Inputs may be any that keep to these rules, and one draw needn't show every extreme that they name: `attn_routes`: each token names 2 different experts. `mlp_routes`: each token names 2 different experts. `slot_order`: for each tree and sub-layer, every pair index appears once. `seg_lengths`: a tree's 13 lengths sum to 384; segment 0, the trunk, is the longest. `seg_parents`: segment 0 is its own parent; segments 1 to 4 have parent 0; each of them is the parent of exactly two of segments 5 to 12.
All inputs are finite; a program needn't handle non-finite values.
Results may differ from the reference program's by a relative error of at most 0.015.
Values may be sent and summed in bfloat16 or wider, within the bound.
A program may use at most 256 MiB of HBM per device.

```python
import math
import jax
import jax.numpy as jnp
from jax import lax

D = 1536
HD = 64
KVH = 8
FF = 512
QW = 512
EA = 8
EM = 8
TOPK = 2
NSEG = 13
TOK_DEV = 384
CAP = 120
GROUPS = 64
MEMBERS = 2
TOKENS = 49152
DEVICES = 128


def draw_seg_lengths(key, part):
    key = jax.random.fold_in(key, 11)
    lowest = TOK_DEV // 32
    highest = TOK_DEV // 16 + 1
    others = jax.random.randint(key, (GROUPS, MEMBERS, NSEG - 1), lowest, highest)
    tree_count = GROUPS * MEMBERS
    chosen_tree = jax.random.randint(jax.random.fold_in(key, 5), (), 0, tree_count)
    tree_index = jnp.arange(tree_count, dtype=jnp.int32).reshape(GROUPS, MEMBERS, 1)
    others = jnp.where(tree_index == chosen_tree, lowest, others)
    trunk_length = TOK_DEV - jnp.sum(others, axis=-1, keepdims=True)
    return jnp.concatenate([trunk_length, others], axis=-1).astype(jnp.int32)


def draw_seg_parents(key, part):
    key = jax.random.fold_in(key, 23)
    tree_count = GROUPS * MEMBERS
    split_keys = jax.random.split(key, tree_count)
    leaf_base = jnp.array([1, 1, 2, 2, 3, 3, 4, 4], jnp.int32)
    leaves = jax.vmap(lambda subkey: jax.random.permutation(subkey, leaf_base))(split_keys)
    root_part = jnp.zeros((tree_count, 5), jnp.int32)
    return jnp.concatenate([root_part, leaves], axis=1).reshape(GROUPS, MEMBERS, NSEG).astype(jnp.int32)


def spiked(drawn, stream_key, source, target, parts, factor):
    def block_of(axis_at):
        return (jnp.arange(drawn.shape[axis_at]) // (drawn.shape[axis_at] // parts)).reshape((-1,) + (1,) * (drawn.ndim - 1 - axis_at))

    near = jax.random.permutation(stream_key, parts)[block_of(target)]
    far = (block_of(target) + parts // 2) % parts
    return jnp.where((block_of(source) == near) | (block_of(source) == far), factor * drawn, drawn)


def block_levels(key, shape, shards, low, high):
    factor_of = 1.0
    for dim, shards_of in shards:
        heights = jax.random.uniform(jax.random.fold_in(jax.random.fold_in(key, 6), dim), (shards_of,), jnp.float32, low / len(shards), high / len(shards))
        factor_of = factor_of * jnp.repeat(jnp.exp(heights), shape[dim] // shards_of).reshape((-1,) + (1,) * (len(shape) - 1 - dim))
    return factor_of


def choose_distinct(own_key, rows, number_of, top, lift):
    ranking = jax.random.permutation(jax.random.fold_in(own_key, 1), number_of)
    boost = ranking
    for power in range(3):
        boost = boost * boost // number_of
    boost = boost * lift // number_of
    lots = jax.random.randint(jax.random.fold_in(own_key, 2), (rows, number_of), 0, 4096) + boost
    sure = jax.random.permutation(jax.random.fold_in(own_key, 3), rows)[jnp.arange(number_of) % rows]
    lots = jnp.where(jnp.arange(rows)[:, None] == sure[None, :], 1 << 14, lots)
    merit = lots * number_of + jnp.arange(number_of)
    return lax.top_k(merit.astype(jnp.int32), top)[1].astype(jnp.int32)


def gaussian(key, dims, scale, reach, pieces=(), held_as=jnp.bfloat16):
    values = jax.random.normal(key, dims, jnp.float32) * scale
    if len(pieces) > 0:
        values = block_levels(key, dims, pieces, -0.22, 0.18) * values
    return jnp.clip(values, min=-reach, max=reach).astype(held_as)


def gaussian_with(stream_key, extent, deviation, bound, cuts, heavy, kind=jnp.bfloat16):
    entries = deviation * jax.random.normal(stream_key, extent, jnp.float32)
    if cuts:
        entries = entries * block_levels(stream_key, extent, cuts, -0.22, 0.18)
    return jnp.clip(spiked(entries, jax.random.fold_in(stream_key, 3), *heavy), -bound, bound).astype(kind)


def setup_inputs(seed: int = 0) -> dict:
    key_list = jax.random.split(jax.random.key(seed), 18)
    inputs = gaussian(key_list[0], (TOKENS, D), 1.0, 6.0, ((0, 128),))
    cotangent = gaussian_with(key_list[1], (TOKENS, D), 1.0, 24.0, ((0, 128),), (0, 1, 128, 5.5))
    norm_one = jnp.clip(1.0 + 0.1 * jax.random.normal(key_list[2], (D,), jnp.float32), 0.5, 1.5)
    kv_weight = gaussian(key_list[3], (D, 2 * QW), D ** -0.5, 0.15625)
    attn_router = gaussian(key_list[4], (D, EA), (2 * D) ** -0.5, 0.109375)
    query_experts = gaussian(key_list[5], (EA, D, QW), D ** -0.5, 0.15625, ((0, 2),))
    out_experts = gaussian(key_list[6], (EA, QW, D), (max(1, QW // 64)) ** -0.5, 2.0, ((0, 2),))
    norm_two = jnp.clip(1.0 + 0.1 * jax.random.normal(key_list[7], (D,), jnp.float32), 0.5, 1.5)
    mlp_router = gaussian(key_list[8], (D, EM), (2 * D) ** -0.5, 0.109375)
    gate_experts = gaussian(key_list[9], (EM, D, FF), D ** -0.5, 0.15625, ((0, 2),))
    up_experts = gaussian(key_list[10], (EM, D, FF), D ** -0.5, 0.15625, ((0, 2),))
    down_experts = gaussian(key_list[11], (EM, FF, D), FF ** -0.5, 0.25, ((0, 2),))
    attn_routes = choose_distinct(key_list[12], GROUPS * MEMBERS * TOK_DEV, EA, TOPK, 2048).reshape((GROUPS, MEMBERS, TOK_DEV, TOPK))
    mlp_routes = choose_distinct(key_list[13], GROUPS * MEMBERS * TOK_DEV, EM, TOPK, 2048).reshape((GROUPS, MEMBERS, TOK_DEV, TOPK))
    slot_order = jax.vmap(lambda own: jax.random.permutation(own, TOPK * TOK_DEV))(jax.random.split(key_list[14], GROUPS * MEMBERS * 2)).reshape((GROUPS, MEMBERS, 2, TOPK * TOK_DEV)).astype(jnp.int32)
    seg_lengths = draw_seg_lengths(jax.random.fold_in(key_list[17], 71), 0)
    seg_parents = draw_seg_parents(jax.random.fold_in(key_list[17], 71), 0)
    return {"inputs": inputs, "cotangent": cotangent, "norm_one": norm_one, "kv_weight": kv_weight, "attn_router": attn_router, "query_experts": query_experts, "out_experts": out_experts, "norm_two": norm_two, "mlp_router": mlp_router, "gate_experts": gate_experts, "up_experts": up_experts, "down_experts": down_experts, "attn_routes": attn_routes, "mlp_routes": mlp_routes, "slot_order": slot_order, "seg_lengths": seg_lengths, "seg_parents": seg_parents}


@jax.custom_vjp
def low(v):
    return lax.optimization_barrier(v.astype(jnp.bfloat16)).astype(jnp.float32)

@jax.custom_vjp
def low_back(v):
    return v

def low_keep(v):
    return (low(v), None)

def low_pass(kept, grad):
    return (grad,)

def back_keep(v):
    return (v, None)

def back_low(kept, grad):
    return (low(grad),)
low.defvjp(low_keep, low_pass)
low_back.defvjp(back_keep, back_low)
epsilon = 1e-06
precise = lax.Precision.HIGHEST

def mean_square_scale(values, gain_vector):
    return values * lax.rsqrt(lax.optimization_barrier(jnp.mean(values * values, axis=-1, keepdims=True)) + epsilon) * gain_vector

def rotary(values, position, direction):
    row_total = values.shape[0]
    halves = values.reshape(row_total, KVH, 2, HD // 2)
    frequency = 10000.0 ** (-2.0 * jnp.arange(HD // 2).astype(jnp.float32) / HD)
    angles = position.astype(jnp.float32)[:, None] * frequency[None, :]
    cosine = jnp.cos(angles)[:, None, :]
    sine_term = direction * jnp.sin(angles)[:, None, :]
    first_half = halves[:, :, 0] * cosine - halves[:, :, 1] * sine_term
    second_half = halves[:, :, 1] * cosine + halves[:, :, 0] * sine_term
    return jnp.stack([first_half, second_half], axis=2).reshape(row_total, KVH * HD)

def tree_tables(lengths, parents):
    token_ids = jnp.arange(TOK_DEV, dtype=jnp.int32)
    starts = jnp.cumsum(lengths) - lengths
    segment = lax.optimization_barrier(jnp.sum((token_ids[:, None] >= starts[None, :]).astype(jnp.int32), axis=1)) - 1
    seg_ids = jnp.arange(NSEG, dtype=jnp.int32)
    grand_parents = lax.optimization_barrier(jnp.sum(jnp.where(parents[:, None] == seg_ids[None, :], parents[None, :], 0), axis=1))
    ancestor = (seg_ids[:, None] == seg_ids[None, :]) | (parents[:, None] == seg_ids[None, :]) | (grand_parents[:, None] == seg_ids[None, :])
    member = (segment[:, None] == seg_ids[None, :]).astype(jnp.int32)
    reachable = jnp.dot(jnp.dot(member, ancestor.astype(jnp.int32)), member.T)
    allowed = (reachable > 0) & (token_ids[None, :] <= token_ids[:, None])
    position = lax.optimization_barrier(jnp.sum(allowed.astype(jnp.int32), axis=1)) - 1
    return (allowed, position)

def slot_table(routes, priority, expert_count):
    pair_expert = routes.reshape(-1)
    ordered = jnp.take(pair_expert, priority)
    onehot = (ordered[:, None] == jnp.arange(expert_count, dtype=jnp.int32)[None, :]).astype(jnp.int32)
    earlier = jnp.cumsum(onehot, axis=0) - onehot
    ranked = lax.optimization_barrier(jnp.sum(earlier * onehot, axis=1))
    slot_index = jnp.zeros_like(ranked).at[priority].set(ranked)
    flat_slot = jnp.where(slot_index < CAP, pair_expert * CAP + slot_index, expert_count * CAP)
    owner_pair = jnp.full((expert_count * CAP,), TOPK * TOK_DEV, jnp.int32).at[flat_slot].set(jnp.arange(TOPK * TOK_DEV, dtype=jnp.int32), mode='drop')
    return (flat_slot, owner_pair)

def pick_gates(logits, routes, expert_count):
    choose = (routes[:, :, None] == jnp.arange(expert_count, dtype=jnp.int32)[None, None, :]).astype(logits.dtype)
    picked = lax.optimization_barrier(jnp.sum(choose * logits[:, None, :], axis=-1))
    return jax.nn.softmax(picked, axis=-1)

def attend(queries, key_rows, value_rows, row_mask):
    query_heads = queries.reshape(-1, KVH, HD)
    scores = jnp.einsum('rhd,thd->hrt', query_heads, key_rows.reshape(-1, KVH, HD), precision=precise) * HD ** (-0.5)
    scores = jnp.where(row_mask[None], low_back(scores), -1e+30)
    probability = low(jax.nn.softmax(scores, axis=-1))
    attended = jnp.einsum('hrt,thd->rhd', probability, value_rows.reshape(-1, KVH, HD), precision=precise)
    return low_back(low(attended.reshape(-1, QW)))

def tree_layer(inputs, params, attn_routes, mlp_routes, priority, lengths, parents):
    norm_one, kv_weight, attn_router, query_experts, out_experts, norm_two, mlp_router, gate_experts, up_experts, down_experts = params
    allowed, position = tree_tables(lengths, parents)
    empty_row = jnp.zeros((1, D), inputs.dtype)
    normed = low(mean_square_scale(inputs, norm_one))
    key_value = jnp.dot(normed, kv_weight, precision=precise)
    key_rows = low(rotary(low_back(key_value[:, :QW]), position, 1.0))
    value_rows = low(low_back(key_value[:, QW:]))
    attn_gates = pick_gates(low_back(jnp.dot(normed, attn_router, precision=precise)), attn_routes, EA)
    flat_slot, owner_pair = slot_table(attn_routes, priority[0], EA)
    owner_token = owner_pair // TOPK
    expert_rows = low_back(jnp.take(jnp.concatenate([normed, empty_row]), owner_token, axis=0).reshape(EA, CAP, D))
    query_pre = low_back(jnp.einsum('ecd,edq->ecq', expert_rows, query_experts, precision=precise))
    row_token = jnp.where(owner_token < TOK_DEV, owner_token, 0)
    queries = low(rotary(query_pre.reshape(EA * CAP, QW), jnp.take(position, row_token), 1.0))
    attended = attend(queries, key_rows, value_rows, jnp.take(allowed, row_token, axis=0))
    out_rows = low_back(low(jnp.einsum('ecq,eqd->ecd', attended.reshape(EA, CAP, QW), out_experts, precision=precise)))
    pair_rows = jnp.take(jnp.concatenate([out_rows.reshape(EA * CAP, D), empty_row]), flat_slot, axis=0).reshape(TOK_DEV, TOPK, D)
    middle = inputs + lax.optimization_barrier(jnp.sum(attn_gates[:, :, None] * pair_rows, axis=1))
    normed_two = low(mean_square_scale(middle, norm_two))
    mlp_gates = pick_gates(low_back(jnp.dot(normed_two, mlp_router, precision=precise)), mlp_routes, EM)
    flat_slot, owner_pair = slot_table(mlp_routes, priority[1], EM)
    expert_rows = low_back(jnp.take(jnp.concatenate([normed_two, empty_row]), owner_pair // TOPK, axis=0).reshape(EM, CAP, D))
    gate_pre = low_back(jnp.einsum('ecd,edf->ecf', expert_rows, gate_experts, precision=precise))
    up_pre = low_back(jnp.einsum('ecd,edf->ecf', expert_rows, up_experts, precision=precise))
    hidden = low(jax.nn.silu(gate_pre) * up_pre)
    out_rows = low_back(low(jnp.einsum('ecf,efd->ecd', hidden, down_experts, precision=precise)))
    pair_rows = jnp.take(jnp.concatenate([out_rows.reshape(EM * CAP, D), empty_row]), flat_slot, axis=0).reshape(TOK_DEV, TOPK, D)
    return middle + lax.optimization_barrier(jnp.sum(mlp_gates[:, :, None] * pair_rows, axis=1))

def reference(inputs, cotangent, norm_one, kv_weight, attn_router, query_experts, out_experts, norm_two, mlp_router, gate_experts, up_experts, down_experts, attn_routes, mlp_routes, slot_order, seg_lengths, seg_parents):
    per_step = math.gcd(DEVICES, max(1, 4096 // TOK_DEV))
    step_count = DEVICES // per_step

    def shaped(stacked):
        return stacked.reshape((step_count, per_step) + stacked.shape[2:])
    integers = (shaped(attn_routes), shaped(mlp_routes), shaped(slot_order), shaped(seg_lengths), shaped(seg_parents))
    params = tuple((weight.astype(jnp.float32) for weight in (norm_one, kv_weight, attn_router, query_experts, out_experts, norm_two, mlp_router, gate_experts, up_experts, down_experts)))

    def forward(input_float, weights):

        def one_step(carried, tree_block):
            result = jax.vmap(tree_layer, in_axes=(0, None, 0, 0, 0, 0, 0))(tree_block[0], weights, tree_block[1], tree_block[2], tree_block[3], tree_block[4], tree_block[5])
            return (carried, result)
        unused, outputs = lax.scan(jax.checkpoint(one_step), jnp.zeros((), jnp.float32), (input_float,) + integers)
        return outputs
    input_float = inputs.astype(jnp.float32).reshape(step_count, per_step, TOK_DEV, D)
    outputs, pullback = jax.vjp(forward, input_float, params)
    input_grad, grads = pullback(cotangent.astype(jnp.float32).reshape(step_count, per_step, TOK_DEV, D))
    return (outputs.reshape(TOKENS, D).astype(jnp.bfloat16), input_grad.reshape(TOKENS, D).astype(jnp.bfloat16), grads[0], grads[1], grads[2], grads[3], grads[4], grads[5], grads[6], grads[7], grads[8], grads[9])
```

```python
from functools import partial
import math

import jax
import jax.numpy as jnp
from jax import lax
from jax.experimental import pallas as pl
from jax.experimental.pallas import tpu as pltpu
from jax.sharding import Mesh, PartitionSpec as P

D = 1536
HD = 64
KVH = 8
FF = 512
QW = 512
NSEG = 13
TOK = 384
CAP = 120
PAD = 128
PAIRS = 2 * TOK
EPS = 1e-06
MIB = 1 << 20
F32 = jnp.float32
BF16 = jnp.bfloat16
I32 = jnp.int32

NT = (((1,), (1,)), ((), ()))
NN = (((1,), (0,)), ((), ()))
TN = (((0,), (0,)), ((), ()))


def mm(a, b, dims=NN):
    return lax.dot_general(a, b, dims, preferred_element_type=F32)


def iota(shape, dim):
    return lax.broadcasted_iota(I32, shape, dim)


def params(mib):
    return pltpu.CompilerParams(vmem_limit_bytes=mib * MIB)


VSPEC = pl.BlockSpec(memory_space=pltpu.VMEM)
SSPEC = pl.BlockSpec(memory_space=pltpu.SMEM)
ANY = pl.BlockSpec(memory_space=pl.ANY)


def make_meta(tree, len_ref, par_ref, order_ref, routes, out_ref):
    token = iota((PAIRS, TOK), 1)
    eye = iota((PAIRS, PAIRS), 0) == iota((PAIRS, PAIRS), 1)
    lane = iota((PAIRS, PAD), 1)
    tri = (iota((PAIRS, PAIRS), 0) > iota((PAIRS, PAIRS), 1)).astype(F32).astype(BF16)
    for sub in range(2):
        order = order_ref[0, tree, sub : sub + 1].astype(F32)
        order = jnp.sum(jnp.where(eye, order, 0.0), axis=1, keepdims=True).astype(I32)
        hit = [order == 2 * token + k for k in range(2)]
        named = routes[sub][0, tree].astype(F32)
        expert = jnp.zeros((PAIRS, 1), F32)
        for k in range(2):
            expert = expert + jnp.sum(
                jnp.where(hit[k], named[k : k + 1], 0.0), axis=1, keepdims=True
            )
        onehot = (expert == lane.astype(F32)).astype(F32)
        earlier = mm(tri, onehot.astype(BF16))
        rank = jnp.sum(earlier * onehot, axis=1, keepdims=True)
        code = expert * 1024.0 + rank
        for k in range(2):
            row = jnp.sum(jnp.where(hit[k], code, 0.0), axis=0, keepdims=True)
            out_ref[2 * sub + k : 2 * sub + k + 1] = row.astype(I32)

    def segments(place):
        seg = jnp.full(place.shape, -1, I32)
        start = jnp.int32(0)
        for s in range(NSEG):
            seg = seg + (place >= start).astype(I32)
            start = start + len_ref[0, tree, s]
        parent = jnp.zeros(place.shape, I32)
        for s in range(NSEG):
            parent = jnp.where(seg == s, par_ref[0, tree, s], parent)
        grand = jnp.zeros(place.shape, I32)
        for s in range(NSEG):
            grand = jnp.where(parent == s, par_ref[0, tree, s], grand)
        return seg, parent, grand

    seg, parent, grand = segments(iota((1, TOK), 1))
    key_seg, _, _ = segments(iota((TOK, 1), 0))
    allowed = ((key_seg == seg) | (key_seg == parent) | (key_seg == grand)) & (
        iota((TOK, TOK), 0) <= iota((TOK, TOK), 1)
    )
    depth = jnp.sum(allowed.astype(F32), axis=0, keepdims=True) - 1.0
    out_ref[4:5] = seg
    out_ref[5:6] = parent
    out_ref[6:7] = grand
    out_ref[7:8] = depth.astype(I32)


def sine_cosine(angle):
    turns = jnp.floor(angle * (2.0 / math.pi) + 0.5)
    rest = (angle - turns * 1.5703125) - turns * 4.838267948966e-4
    square = rest * rest
    sine = rest + rest * square * (
        -1.6666654611e-1 + square * (8.3321608736e-3 + square * -1.9515295891e-4)
    )
    cosine = (1.0 - 0.5 * square) + square * square * (
        4.166664568298827e-2 + square * (-1.388731625493765e-3 + square * 2.443315711809948e-5)
    )
    quarter = turns.astype(I32) & 3
    odd = (quarter & 1) == 1
    first, second = jnp.where(odd, cosine, sine), jnp.where(odd, sine, cosine)
    first = jnp.where(quarter >= 2, -first, first)
    second = jnp.where((quarter == 1) | (quarter == 2), -second, second)
    return first, second


def turn(values, place, sign):
    rows = values.shape[0]
    lane = iota((1, 128), 1)
    frequency = jnp.exp((lane % 32).astype(F32) * (-math.log(10000.0) / 32.0))
    angle = place * frequency
    sine, cosine = sine_cosine(angle)
    sine = sine * sign
    first = (iota((rows, 128), 1) % 64) < 32
    sine = jnp.where(first, -sine, sine)
    parts = []
    for b in range(QW // 128):
        v = values[:, 128 * b : 128 * b + 128]
        other = jnp.where(first, pltpu.roll(v, 96, 1), pltpu.roll(v, 32, 1))
        parts.append(v * cosine + other * sine)
    return jnp.concatenate(parts, axis=1)


def as_column(row):
    eye = iota((TOK, TOK), 0) == iota((TOK, TOK), 1)
    return jnp.sum(jnp.where(eye, row, 0.0), axis=1, keepdims=True)


def hits(meta, sub, expert):
    slot = iota((PAD, 1), 0)
    target = jnp.where(slot < CAP, expert * 1024 + slot, -1)
    return (meta[2 * sub : 2 * sub + 1] == target), (meta[2 * sub + 1 : 2 * sub + 2] == target)


def places(meta, sub, base):
    both = []
    for e in range(2):
        first, second = hits(meta, sub, base + e)
        both.append((first | second).astype(F32))
    return jnp.concatenate(both, axis=0).astype(BF16)


def weighted_places(meta, gates, sub, base):
    both = []
    for e in range(2):
        first, second = hits(meta, sub, base + e)
        both.append(jnp.where(first, gates[0:1], 0.0) + jnp.where(second, gates[1:2], 0.0))
    return jnp.concatenate(both, axis=0).astype(BF16)


def slot_gate(meta, gates, sub, expert):
    first, second = hits(meta, sub, expert)
    weighted = jnp.where(first, gates[0:1], 0.0) + jnp.where(second, gates[1:2], 0.0)
    return jnp.sum(weighted, axis=1, keepdims=True)


def token_sums(meta, sub, expert, column):
    first, second = hits(meta, sub, expert)
    return jnp.concatenate(
        [
            jnp.sum(jnp.where(first, column, 0.0), axis=0, keepdims=True),
            jnp.sum(jnp.where(second, column, 0.0), axis=0, keepdims=True),
        ],
        axis=0,
    )


def pair_gates(meta, sub, logits):
    row = iota((8, TOK), 0)
    picked = [
        jnp.sum(
            jnp.where(row == meta[2 * sub + k : 2 * sub + k + 1] // 1024, logits, 0.0),
            axis=0,
            keepdims=True,
        )
        for k in range(2)
    ]
    top = jnp.maximum(picked[0], picked[1])
    raised = [jnp.exp(p - top) for p in picked]
    total = raised[0] + raised[1]
    return jnp.concatenate([raised[0] / total, raised[1] / total], axis=0)


def slot_depth(meta, expert):
    first, second = hits(meta, 0, expert)
    return jnp.sum(jnp.where(first | second, meta[7:8].astype(F32), 0.0), axis=1, keepdims=True)


def slot_mask(columns, expert):
    slot = iota((1, PAD), 1)
    target = jnp.where(slot < CAP, expert * 1024 + slot, -1).astype(F32)
    hit = (columns[:, 0:1] == target) | (columns[:, 1:2] == target)

    def row(column):
        return jnp.sum(jnp.where(hit, column, 0.0), axis=0, keepdims=True)

    key = iota((TOK, 1), 0).astype(F32)
    seg = columns[:, 4:5]
    return (
        (seg == row(seg)) | (seg == row(columns[:, 5:6])) | (seg == row(columns[:, 6:7]))
    ) & (key <= row(key))


def two_heads(rows, masks):
    return jnp.concatenate([rows * masks[0], rows * masks[1]], axis=0)


def softmax_keys(scores, allowed):
    probs = []
    for h in range(2):
        one = jnp.where(allowed, scores[:, PAD * h : PAD * h + PAD] * HD ** (-0.5), -1e30)
        raised = jnp.exp(one - jnp.max(one, axis=0, keepdims=True))
        probs.append(raised * (1.0 / jnp.sum(raised, axis=0, keepdims=True)))
    return probs


def own_lanes(both):
    return jnp.concatenate([both[0:64, 0:PAD], both[64:128, PAD:]], axis=0).T


def logit_grads(meta, sub, gates, grads):
    inner = gates[0:1] * grads[0:1] + gates[1:2] * grads[1:2]
    row = iota((8, TOK), 0)
    total = jnp.zeros((8, TOK), F32)
    for k in range(2):
        picked = gates[k : k + 1] * (grads[k : k + 1] - inner)
        total = total + jnp.where(
            row == meta[2 * sub + k : 2 * sub + k + 1] // 1024, picked, 0.0
        )
    return total.astype(BF16)


def head_masks():
    lane = iota((1, 128), 1)
    return (lane < 64).astype(F32).astype(BF16), (lane >= 64).astype(F32).astype(BF16)


def fetch(pairs, sems):
    copies = []
    for n, (source, target) in enumerate(pairs):
        copy = pltpu.make_async_copy(source, target, sems.at[n])
        copy.start()
        copies.append(copy)
    return copies


MESH = pl.DeviceIdType.MESH
CH = 128
CHUNKS = TOK // CH


class Link:
    def __init__(self, send, recv):
        self.send, self.recv, self.count = send, recv, 0

    def copy(self, source, target, device):
        n = self.count
        self.count += 1
        copy = pltpu.make_async_remote_copy(
            src_ref=source,
            dst_ref=target,
            send_sem=self.send.at[n],
            recv_sem=self.recv.at[n],
            device_id=device,
            device_id_type=MESH,
        )
        copy.start()
        return copy


def around(axes):
    devices = []
    for axis in axes:
        n = lax.axis_size(axis)
        if n > 1:
            me = lax.axis_index(axis)
            devices += [{axis: lax.rem(me + 1, n)}, {axis: lax.rem(me + n - 1, n)}]
    return devices


def flip(*axes):
    return {axis: 1 - lax.axis_index(axis) for axis in axes}


def first_expert():
    local = 2 * lax.axis_index("c")
    return 4 * lax.axis_index("zh") + local, local


def greet(devices):
    barrier = pltpu.get_barrier_semaphore()
    for device in devices:
        pl.semaphore_signal(barrier, inc=1, device_id=device, device_id_type=MESH)
    pl.semaphore_wait(barrier, len(devices))


def part(j):
    return slice(CH * j, CH * j + CH)


class Collect:
    def __init__(self, link, own, mate, far, far_mate, abuf, bbuf, fbuf, rbuf):
        self.link, self.fbuf, self.rbuf, self.abuf, self.bbuf = link, fbuf, rbuf, abuf, bbuf
        self.own, self.mate, self.far, self.far_mate = own, mate, far, far_mate

    def send_far_mate(self):
        self.a = [
            self.link.copy(self.far_mate.at[part(j)], self.abuf.at[part(j)], flip("c"))
            for j in range(CHUNKS)
        ]

    def send_mate(self):
        self.b = [
            self.link.copy(self.mate.at[part(j)], self.bbuf.at[part(j)], flip("c"))
            for j in range(CHUNKS)
        ]

    def forward(self):
        self.f = []
        for j in range(CHUNKS):
            self.a[j].wait_recv()
            total = self.far[part(j)].astype(F32) + self.abuf[part(j)].astype(F32)
            self.fbuf[part(j)] = total.astype(BF16)
            self.f.append(
                self.link.copy(self.fbuf.at[part(j)], self.rbuf.at[part(j)], flip("zl", "zh"))
            )

    def total(self, j):
        self.b[j].wait_recv()
        self.f[j].wait_recv()
        return (
            self.own[part(j)].astype(F32)
            + self.bbuf[part(j)].astype(F32)
            + self.rbuf[part(j)].astype(F32)
        )

    def close(self):
        for copy in self.a + self.b + self.f:
            copy.wait_send()


class Spread:
    def __init__(self, link, own, landed, target, sems):
        self.link, self.own, self.landed, self.target, self.sems = link, own, landed, target, sems
        self.far, self.mate, self.local, self.relayed = [], [], [], []

    def keep(self, source, tree, j):
        local = pltpu.make_async_copy(
            source, self.target.at[tree, part(j)], self.sems.at[len(self.local)]
        )
        local.start()
        self.local.append(local)

    def send(self, j):
        source = self.own.at[part(j)]
        self.far.append(self.link.copy(source, self.landed.at[part(j)], flip("zl", "zh")))
        self.mate.append(self.link.copy(source, self.target.at[1, part(j)], flip("c")))
        self.keep(source, 0, j)

    def relay(self, j):
        self.far[j].wait_recv()
        source = self.landed.at[part(j)]
        self.relayed.append(self.link.copy(source, self.target.at[3, part(j)], flip("c")))
        self.keep(source, 2, j)

    def close(self):
        for copy in self.mate + self.relayed:
            copy.wait_recv()
        for copy in self.far + self.mate + self.relayed:
            copy.wait_send()
        for copy in self.local:
            copy.wait()


class Pairs:
    def __init__(self, link, keep, give, buf, mid, far):
        self.link, self.keep, self.buf, self.mid, self.far = link, keep, buf, mid, far
        self.first = link.copy(give, buf, flip("c"))

    def forward(self):
        self.first.wait_recv()
        self.mid[...] = self.keep[1] + self.buf[1]
        self.second = self.link.copy(self.mid, self.far, flip("zl", "zh"))

    def total(self):
        self.second.wait_recv()
        return self.keep[0] + self.buf[0] + self.far[...]

    def close(self):
        self.first.wait_send()
        self.second.wait_send()


class Ring:
    def __init__(self, link, axis, view, buf0, buf1):
        self.link, self.axis, self.view, self.buf0, self.buf1 = link, axis, view, buf0, buf1
        self.n = lax.axis_size(axis)
        me = lax.axis_index(axis)
        self.at = lambda step: lax.rem(me + step + self.n, self.n)

    def start(self):
        if self.n == 1:
            return
        right, left = {self.axis: self.at(1)}, {self.axis: self.at(-1)}
        self.c0 = self.link.copy(self.view(self.at(2), 0), self.buf0.at[0], right)
        self.c1 = self.link.copy(self.view(self.at(2), 1), self.buf1.at[0], left)
        self.c2 = self.link.copy(self.view(self.at(1), 1), self.buf1.at[1], right)
        self.c3 = self.link.copy(self.view(self.at(-1), 0), self.buf0.at[2], left)

    def middle(self):
        if self.n == 1:
            return
        right, left = {self.axis: self.at(1)}, {self.axis: self.at(-1)}
        self.c0.wait_recv()
        held = self.view(self.at(1), 0)
        held[...] = (held[...].astype(F32) + self.buf0[0].astype(F32)).astype(BF16)
        self.c4 = self.link.copy(held, self.buf0.at[1], right)
        self.c1.wait_recv()
        held = self.view(self.at(-1), 1)
        held[...] = (held[...].astype(F32) + self.buf1[0].astype(F32)).astype(BF16)
        self.c5 = self.link.copy(held, self.buf1.at[2], left)

    def end(self, store):
        if self.n == 1:
            for h in range(2):
                store(h, self.view(0, h)[...].astype(F32))
            return
        for h, waits, buf in ((0, (self.c4, self.c3), self.buf0), (1, (self.c2, self.c5), self.buf1)):
            for copy in waits:
                copy.wait_recv()
            store(
                h,
                self.view(self.at(0), h)[...].astype(F32) + buf[1].astype(F32) + buf[2].astype(F32),
            )

    def close(self):
        if self.n > 1:
            for copy in (self.c0, self.c1, self.c2, self.c3, self.c4, self.c5):
                copy.wait_send()


def split(rows):
    first = (rows // 2 + 15) // 16 * 16
    return slice(0, first), slice(first, rows)


def ring_buffers(lead, rows):
    return [pltpu.VMEM((3,) + lead + (s.stop - s.start, 512), BF16) for s in split(rows)]


def remote_params(mib, ident):
    return pltpu.CompilerParams(
        vmem_limit_bytes=mib * MIB, collective_id=ident, has_side_effects=True
    )


ROWS_BUF = pltpu.VMEM((TOK, D), BF16)


class Gather:
    def __init__(self, link, source, target):
        self.link, self.source, self.target = link, source, target

    def send(self):
        self.far = [
            self.link.copy(self.source.at[part(j)], self.target.at[1, part(j)], flip("zl", "zh"))
            for j in range(CHUNKS)
        ]
        self.mate = self.link.copy(self.source, self.target.at[0], flip("c"))
        self.relayed = []

    def relay(self, j):
        self.far[j].wait_recv()
        self.relayed.append(
            self.link.copy(self.target.at[1, part(j)], self.target.at[2, part(j)], flip("c"))
        )

    def close(self):
        for copy in self.far + [self.mate] + self.relayed:
            copy.wait_send()


def forward_kernel(*refs):
    (
        len_ref, par_ref, order_ref, routes_one, routes_two, x_ref, gain_ref, gain_two_ref, router_ref,
        cot_ref, kv_hbm, wq_hbm, wo_hbm,
        n_hbm, k_hbm, v_hbm, r_hbm, q_hbm, a_hbm, n2_hbm, cots_hbm, gate_ref, meta_ref, middle_ref,
        xb, nb, kb, vb, vt, columns, rb, qb, ab, obuf, pb, kv, wq, wo, mbuf, abuf, bbuf, fbuf, rbuf, own,
        landed, cb, wsem, osem, sems, ssem, rsem,
    ) = refs
    base, local = first_expert()
    link = Link(ssem, rsem)
    load = fetch(
        [(kv_hbm, kv), (wq_hbm.at[pl.ds(local, 2)], wq), (wo_hbm.at[pl.ds(local, 2)], wo)], wsem
    )
    saved = []

    def save(source, target):
        copy = pltpu.make_async_copy(source, target, osem.at[len(saved)])
        copy.start()
        saved.append(copy)

    far, mate = flip("zl", "zh"), flip("c")
    greet([mate, far])
    inputs = Gather(link, x_ref, xb)
    cots = Gather(link, cot_ref, cb)
    collect = Collect(link, pb.at[0], pb.at[1], pb.at[2], pb.at[3], abuf, bbuf, fbuf, rbuf)
    spread = Spread(link, own, landed, n2_hbm, sems)
    inputs.send()
    make_meta(
        lax.axis_index("zh"), len_ref, par_ref, order_ref, (routes_one, routes_two), mbuf.at[0]
    )
    meta_far = link.copy(mbuf.at[0], mbuf.at[2], far)
    meta_mate = link.copy(mbuf.at[0], mbuf.at[1], mate)
    gate_ref[...] = jnp.zeros_like(gate_ref)

    def tree(s, source):
        meta = mbuf[s]
        x = source[...].astype(F32)
        inverse = lax.rsqrt(jnp.mean(x * x, axis=-1, keepdims=True) + EPS)
        normed = (x * inverse * gain_ref[...].reshape(1, D)).astype(BF16)
        nb[s] = normed
        save(nb.at[s], n_hbm.at[s])
        depth = as_column(meta[7:8].astype(F32))
        kb[s] = turn(mm(normed, kv[:, :QW]), depth, 1.0).astype(BF16)
        save(kb.at[s], k_hbm.at[s])
        value = mm(normed, kv[:, QW:])
        vb[s] = value.astype(BF16)
        save(vb.at[s], v_hbm.at[s])
        vt[s] = value.T.astype(BF16)
        columns[s] = meta.astype(F32).T
        moved = mm(places(meta, 0, base), normed).astype(BF16)
        for e in range(2):
            rb[e, PAD * s : PAD * s + PAD] = moved[PAD * e : PAD * e + PAD]
            save(rb.at[e, pl.ds(PAD * s, PAD)], r_hbm.at[e, pl.ds(PAD * s, PAD)])
        gate_ref[s, 0:2] = pair_gates(meta, 0, mm(router_ref[...], normed, NT))

    masks = head_masks()

    def attend(first, between=None):
        group = slice(PAD * first, PAD * first + 2 * PAD)
        for e in range(2):
            depth = jnp.concatenate(
                [slot_depth(mbuf[first + n], base + e) for n in range(2)], axis=0
            )
            qb[e, group] = turn(mm(rb[e, group], wq[e]), depth, 1.0).astype(BF16)

        def block(n, carry):
            e, s = n // 2, first + n % 2
            allowed = slot_mask(columns[s], base + e)
            start = pl.multiple_of(s * PAD, PAD)
            for pair in range(4):
                cols = slice(128 * pair, 128 * pair + 128)
                q = two_heads(qb[e, pl.ds(start, PAD), cols], masks)
                probs = softmax_keys(mm(kb[s, :, cols], q, NT), allowed)
                probs = jnp.concatenate([p.astype(BF16) for p in probs], axis=1)
                ab[e, pl.ds(start, PAD), cols] = own_lanes(mm(vt[s, cols], probs)).astype(BF16)
            return carry

        lax.fori_loop(0, 4, block, 0)
        if between is not None:
            between()
        for e in range(2):
            save(qb.at[e, pl.ds(PAD * first, 2 * PAD)], q_hbm.at[e, pl.ds(PAD * first, 2 * PAD)])
            save(ab.at[e, pl.ds(PAD * first, 2 * PAD)], a_hbm.at[e, pl.ds(PAD * first, 2 * PAD)])
            obuf[e] = mm(ab[e, group], wo[e]).astype(BF16)
        for n in (1, 0):
            s = first + n
            pb[s] = mm(
                weighted_places(mbuf[s], gate_ref[s], 0, base),
                jnp.concatenate([obuf[e, PAD * n : PAD * n + PAD] for e in range(2)], axis=0),
                TN,
            ).astype(BF16)
            if s == 3:
                collect.send_far_mate()
            if s == 1:
                collect.send_mate()

    load[0].wait()
    tree(0, x_ref)
    meta_far.wait_recv()
    meta_on = link.copy(mbuf.at[2], mbuf.at[3], mate)
    meta_mate.wait_recv()
    inputs.relay(0)
    inputs.mate.wait_recv()
    tree(1, xb.at[0])
    load[1].wait()
    load[2].wait()
    attend(0, lambda: inputs.relay(1))
    inputs.relay(2)
    cots.send()
    tree(2, xb.at[1])
    for copy in inputs.relayed:
        copy.wait_recv()
    meta_on.wait_recv()
    tree(3, xb.at[2])
    attend(2)
    meta_ref[...] = mbuf[...]
    collect.forward()
    for j in range(CHUNKS):
        middle = x_ref[part(j)].astype(F32) + collect.total(j)
        middle_ref[part(j)] = middle
        inverse = lax.rsqrt(jnp.mean(middle * middle, axis=-1, keepdims=True) + EPS)
        own[part(j)] = (middle * inverse * gain_two_ref[...].reshape(1, D)).astype(BF16)
        spread.send(j)
    for j in range(CHUNKS):
        cots.relay(j)
    cots.mate.wait_recv()
    save(cb.at[pl.ds(0, 2)], cots_hbm.at[pl.ds(0, 2)])
    for j in range(CHUNKS):
        spread.relay(j)
    for copy in cots.relayed:
        copy.wait_recv()
    save(cb.at[2], cots_hbm.at[2])
    for copy in (meta_far, meta_mate, meta_on):
        copy.wait_send()
    inputs.close()
    cots.close()
    collect.close()
    spread.close()
    for copy in saved:
        copy.wait()


def forward_call(*operands):
    rows = jax.ShapeDtypeStruct((4, TOK, D), BF16)
    heads = jax.ShapeDtypeStruct((4, TOK, QW), BF16)
    slots = jax.ShapeDtypeStruct((2, 4 * PAD, QW), BF16)
    copies = 2 * (2 * CHUNKS + 1) + 3 + 6 * CHUNKS
    return pl.pallas_call(
        forward_kernel,
        out_shape=(
            rows,
            heads,
            heads,
            jax.ShapeDtypeStruct((2, 4 * PAD, D), BF16),
            slots,
            slots,
            rows,
            jax.ShapeDtypeStruct((3, TOK, D), BF16),
            jax.ShapeDtypeStruct((4, 8, TOK), F32),
            jax.ShapeDtypeStruct((4, 8, TOK), I32),
            jax.ShapeDtypeStruct((TOK, D), F32),
        ),
        in_specs=[SSPEC] * 2 + [VSPEC] * 8 + [ANY] * 3,
        out_specs=(ANY,) * 8 + (VSPEC,) * 3,
        scratch_shapes=[
            pltpu.VMEM((3, TOK, D), BF16),
            pltpu.VMEM((4, TOK, D), BF16),
            pltpu.VMEM((4, TOK, QW), BF16),
            pltpu.VMEM((4, TOK, QW), BF16),
            pltpu.VMEM((4, QW, TOK), BF16),
            pltpu.VMEM((4, TOK, 8), F32),
            pltpu.VMEM((2, 4 * PAD, D), BF16),
            pltpu.VMEM((2, 4 * PAD, QW), BF16),
            pltpu.VMEM((2, 4 * PAD, QW), BF16),
            pltpu.VMEM((2, 2 * PAD, D), BF16),
            pltpu.VMEM((4, TOK, D), BF16),
            pltpu.VMEM((D, 2 * QW), BF16),
            pltpu.VMEM((2, D, QW), BF16),
            pltpu.VMEM((2, QW, D), BF16),
            pltpu.VMEM((4, 8, TOK), I32),
        ]
        + [ROWS_BUF] * 6
        + [
            pltpu.VMEM((3, TOK, D), BF16),
            pltpu.SemaphoreType.DMA((3,)),
            pltpu.SemaphoreType.DMA((30,)),
            pltpu.SemaphoreType.DMA((2 * CHUNKS,)),
            pltpu.SemaphoreType.DMA((copies,)),
            pltpu.SemaphoreType.DMA((copies,)),
        ],
        compiler_params=remote_params(60, 1),
        cost_estimate=pl.CostEstimate(flops=10**9, bytes_accessed=300 * 10**6, transcendentals=0),
        name="attention_forward",
    )(*operands)


def expert_block(nx, ny):
    return D // (nx * ny), FF // (nx * ny)


def mlp_kernel(nx, ny, *refs):
    (
        mbuf, router_ref, gain_ref, n4_hbm, cot_hbm, cots_hbm, middle_hbm, wg_hbm, wu_hbm, wd_hbm,
        dm_ref, gain_grad_ref, router_grad_ref, sa_ref, sb_ref, dm4_ref, keep_out, give_out,
    ) = refs[:18]
    (
        pbuf, gb, mr, gr, dgu, hg, obuf, dbuf, big, middle, cot, normed, own, landed, abuf, bbuf, fbuf, rbuf,
        gates, dgk, dgg, gpair, gmid, gfar, a0, a1, b0, b1, c0, c1, d0, d1, sems, lsem, osem, ssem, rsem,
    ) = refs[18:]
    base, local = first_expert()
    r, rq = expert_block(nx, ny)
    half = (2 * r + 3 * rq) // 2
    halves = split(half)
    link = Link(ssem, rsem)
    load = fetch(
        [(n4_hbm.at[pl.ds(2, 2)], pbuf.at[pl.ds(2, 2)]), (cots_hbm.at[pl.ds(1, 2)], gb.at[pl.ds(2, 2)])]
        + [(wg_hbm.at[pl.ds(local, 2)], big.at[:, :, :, 0:r])]
        + [(wu_hbm.at[pl.ds(local, 2)], big.at[:, :, :, r : 2 * r])]
        + [
            (
                wd_hbm.at[pl.ds(local, 2), :, :, :, pl.ds(512 * k, 512)],
                big.at[:, :, :, 2 * r + rq * k : 2 * r + rq * k + rq],
            )
            for k in range(3)
        ]
        + [(n4_hbm.at[pl.ds(0, 2)], pbuf.at[pl.ds(0, 2)])]
        + [(cot_hbm, gb.at[0]), (cots_hbm.at[0], gb.at[1])]
        + [(n4_hbm.at[0], normed), (cot_hbm, cot), (middle_hbm, middle)],
        lsem,
    )
    greet([flip("c"), flip("zl", "zh")] + around(("x", "y")))
    dgk[...] = jnp.zeros_like(dgk)
    dgg[...] = jnp.zeros_like(dgg)
    collect = Collect(
        link, pbuf.at[0], pbuf.at[1], pbuf.at[2], pbuf.at[3], abuf, bbuf, fbuf, rbuf
    )
    spread = Spread(link, own, landed, dm4_ref, sems)
    saved = []

    def save(source, target):
        copy = pltpu.make_async_copy(source, target, osem.at[len(saved)])
        copy.start()
        saved.append(copy)

    def to_slots(s):
        gates[s] = pair_gates(mbuf[s], 1, mm(router_ref[...], pbuf[s], NT))
        hot = places(mbuf[s], 1, base)
        rows = slice(PAD * s, PAD * s + PAD)
        for source, target in ((pbuf, mr), (gb, gr)):
            moved = mm(hot, source[s]).astype(BF16)
            target[0, rows] = moved[:PAD]
            target[1, rows] = moved[PAD:]

    def weight(e, k):
        if k < 2:
            return big[e, :, :, r * k : r * k + r].reshape(D, FF)
        first = 2 * r + rq * (k - 2)
        return big[e, :, :, first : first + rq].reshape(FF, 512)

    def experts(first, e):
        rows = slice(PAD * first, PAD * first + 2 * PAD)
        x, grads = mr[e, rows], gr[e, rows]
        gate_pre, up_pre = mm(x, weight(e, 0)), mm(x, weight(e, 1))
        sigmoid = 1.0 / (1.0 + jnp.exp(-gate_pre))
        silu = gate_pre * sigmoid
        hidden = (silu * up_pre).astype(BF16)
        grad = sum(
            mm(grads[:, 512 * k : 512 * k + 512], weight(e, 2 + k), NT) for k in range(3)
        )
        for k in range(3):
            obuf[e, :, 512 * k : 512 * k + 512] = mm(hidden, weight(e, 2 + k)).astype(BF16)
        hidden = hidden.astype(F32)
        grad_gate = jnp.sum(hidden * grad, axis=1, keepdims=True)
        gate = jnp.concatenate(
            [slot_gate(mbuf[first + n], gates[first + n], 1, base + e) for n in range(2)], axis=0
        )
        for n in range(2):
            s = first + n
            (dgg if s % 2 else dgk)[s // 2, 0:2] += token_sums(
                mbuf[s], 1, base + e, grad_gate[PAD * n : PAD * n + PAD]
            )
        hg[e, rows] = (gate * hidden).astype(BF16)
        grad = gate * grad
        grad_gate_pre = (grad * up_pre * sigmoid * (1.0 + gate_pre * (1.0 - sigmoid))).astype(BF16)
        grad_up_pre = (grad * silu).astype(BF16)
        dgu[e, rows, 0:FF] = grad_gate_pre
        dgu[e, rows, FF:] = grad_up_pre
        dbuf[e] = (
            mm(grad_gate_pre, weight(e, 0), NT) + mm(grad_up_pre, weight(e, 1), NT)
        ).astype(BF16)

    def sums(first):
        for n in (1, 0):
            s = first + n
            pbuf[s] = mm(
                places(mbuf[s], 1, base),
                jnp.concatenate([dbuf[e, PAD * n : PAD * n + PAD] for e in range(2)], axis=0),
                TN,
            ).astype(BF16)
            if s == 3:
                collect.send_far_mate()
            if s == 1:
                collect.send_mate()

    def results(first):
        for n in range(2):
            s = first + n
            gb[s] = mm(
                weighted_places(mbuf[s], gates[s], 1, base),
                jnp.concatenate([obuf[e, PAD * n : PAD * n + PAD] for e in range(2)], axis=0),
                TN,
            ).astype(BF16)
            save(gb.at[s], (give_out if s % 2 else keep_out).at[s // 2])

    for copy in load[:2]:
        copy.wait()
    to_slots(2)
    to_slots(3)
    for copy in load[2:7]:
        copy.wait()
    experts(2, 0)
    experts(2, 1)
    sums(2)
    collect.forward()
    results(2)
    for copy in load[7:10]:
        copy.wait()
    to_slots(0)
    to_slots(1)
    later = [slice(half + s.start, half + s.stop) for s in halves]
    rings = [
        [
            Ring(link, "x", lambda i, h: big.at[0, i, :, halves[h]], a0, a1),
            Ring(link, "y", lambda i, h: big.at[0, :, i, later[h]], b0, b1),
        ],
        [
            Ring(link, "x", lambda i, h: big.at[1, i, :, halves[h]], c0, c1),
            Ring(link, "y", lambda i, h: big.at[1, :, i, later[h]], d0, d1),
        ],
    ]
    wide, narrow = D // nx, FF // nx
    for e in range(2):
        experts(0, e)
        for t in range(nx):
            block = mm(mr[e, :, wide * t : wide * t + wide], dgu[e], TN).astype(BF16)
            for k in range(2):
                big[e, t, :, r * k : r * k + r] = block[:, FF * k : FF * k + FF].reshape(ny, r, FF)
            block = mm(hg[e, :, narrow * t : narrow * t + narrow], gr[e], TN).astype(BF16)
            for k in range(3):
                first = 2 * r + rq * k
                big[e, t, :, first : first + rq] = block[:, 512 * k : 512 * k + 512].reshape(
                    ny, rq, 512
                )
        for ring in rings[e]:
            ring.start()
    sums(0)
    for ring in rings[0]:
        ring.middle()
    pairs = Pairs(link, dgk, dgg, gpair, gmid, gfar)
    results(0)
    pairs.forward()
    for copy in load[10:]:
        copy.wait()
    logits = logit_grads(mbuf[0], 1, gates[0], pairs.total())
    router_grad_ref[...] = mm(logits, normed[...])
    gain_grad_ref[...] = jnp.zeros_like(gain_grad_ref)
    for j in range(CHUNKS):
        if j == 1:
            for ring in rings[1]:
                ring.middle()
        grad = collect.total(j) + mm(logits[:, part(j)], router_ref[...], TN)
        mid = middle[part(j)]
        inverse = lax.rsqrt(jnp.mean(mid * mid, axis=-1, keepdims=True) + EPS)
        gain_grad_ref[...] += jnp.sum(grad * (mid * inverse), axis=0, keepdims=True)
        weighted = grad * gain_ref[...].reshape(1, D)
        inner = jnp.mean(weighted * mid, axis=-1, keepdims=True)
        result = (
            cot[part(j)].astype(F32)
            + inverse * weighted
            - mid * (inverse * inverse * inverse * inner)
        )
        own[part(j)] = result.astype(BF16)
        spread.send(j)
        dm_ref[part(j)] = result
    for j in range(CHUNKS):
        spread.relay(j)
    for e in range(2):
        for ring, out in zip(rings[e], (sa_ref, sb_ref)):
            ring.end(keeper(out.at[e], halves))
            ring.close()
    pairs.close()
    collect.close()
    spread.close()
    for copy in saved:
        copy.wait()


def mlp_call(nx, ny, *operands):
    r, rq = expert_block(nx, ny)
    block = 2 * r + 3 * rq
    copies = 6 * CHUNKS + 2 + 24
    part_shape = jax.ShapeDtypeStruct((2, TOK, D), BF16)
    return pl.pallas_call(
        partial(mlp_kernel, nx, ny),
        out_shape=(
            jax.ShapeDtypeStruct((TOK, D), F32),
            jax.ShapeDtypeStruct((1, D), F32),
            jax.ShapeDtypeStruct((8, D), F32),
            jax.ShapeDtypeStruct((2, ny, block // 2, 512), BF16),
            jax.ShapeDtypeStruct((2, nx, block // 2, 512), BF16),
            jax.ShapeDtypeStruct((4, TOK, D), BF16),
            part_shape,
            part_shape,
        ),
        in_specs=[VSPEC] * 3 + [ANY] * 7,
        out_specs=(VSPEC,) * 5 + (ANY,) * 3,
        scratch_shapes=[
            pltpu.VMEM((4, TOK, D), BF16),
            pltpu.VMEM((4, TOK, D), BF16),
            pltpu.VMEM((2, 4 * PAD, D), BF16),
            pltpu.VMEM((2, 4 * PAD, D), BF16),
            pltpu.VMEM((2, 4 * PAD, 2 * FF), BF16),
            pltpu.VMEM((2, 4 * PAD, FF), BF16),
            pltpu.VMEM((2, 2 * PAD, D), BF16),
            pltpu.VMEM((2, 2 * PAD, D), BF16),
            pltpu.VMEM((2, nx, ny, block, 512), BF16),
            pltpu.VMEM((TOK, D), F32),
        ]
        + [ROWS_BUF] * 8
        + [
            pltpu.VMEM((4, 2, TOK), F32),
            pltpu.VMEM((2, 8, TOK), F32),
            pltpu.VMEM((2, 8, TOK), F32),
            pltpu.VMEM((2, 8, TOK), F32),
            pltpu.VMEM((8, TOK), F32),
            pltpu.VMEM((8, TOK), F32),
        ]
        + (ring_buffers((ny,), block // 2) + ring_buffers((nx,), block // 2)) * 2
        + [
            pltpu.SemaphoreType.DMA((2 * CHUNKS,)),
            pltpu.SemaphoreType.DMA((13,)),
            pltpu.SemaphoreType.DMA((4,)),
            pltpu.SemaphoreType.DMA((copies,)),
            pltpu.SemaphoreType.DMA((copies,)),
        ],
        compiler_params=remote_params(63, 2),
        cost_estimate=pl.CostEstimate(flops=10**9, bytes_accessed=250 * 10**6, transcendentals=0),
        name="feed_forward",
    )(*operands)


def of_half(source, index, first, count, side):
    half = count // 2
    return source[index, pl.ds(pl.multiple_of(first + side * half, 8), half)]


def halves_to_send(fields, zsend, zl):
    for e in range(2):
        offset = 0
        for source, first, count in fields:
            zsend[e, offset : offset + count // 2] = of_half(source, e, first, count, 1 - zl).astype(BF16)
            offset += count // 2


def add_halves(fields, zrecv, y, zl):
    for e in range(2):
        offset = 0
        for source, first, count in fields:
            rows = slice(offset, offset + count // 2)
            y[e, rows] = of_half(source, e, first, count, zl) + zrecv[e, rows].astype(F32)
            offset += count // 2


def quarters_to_send(fields, y, csend, core):
    for e in range(2):
        offset = 0
        for _, _, count in fields:
            csend[e, offset // 2 : offset // 2 + count // 4] = of_half(y, e, offset, count // 2, 1 - core)
            offset += count // 2


def place_quarters(fields, targets, y, crecv, core):
    for e in range(2):
        offset = 0
        for (_, _, count), (target, k) in zip(fields, targets):
            n = count // 4
            columns = slice(None) if k is None else slice(512 * k, 512 * k + 512)
            target[core * 2 + e, :, columns] = of_half(y, e, offset, count // 2, core)
            target[(1 - core) * 2 + e, :, columns] = crecv[e, offset // 2 : offset // 2 + n]
            offset += count // 2


def keeper(target, cut, index=None):
    def store(h, value):
        if index is None:
            target[:, cut[h]] = value.astype(target.dtype)
        else:
            target[index, cut[h]] = value.astype(target.dtype)

    return store


def attn_back_kernel(nx, ny, *refs):
    (
        mbuf, gbuf, router_ref, gain_ref, sa_ref, sb_ref, x_hbm, dm_hbm, n_hbm, grads_hbm,
        k_hbm, v_hbm, q_hbm, a_hbm, wq_hbm, wo_hbm, kv_hbm, r_hbm,
    ) = refs[:18]
    gain_grad_ref, router_grad_ref, dkv_ref, tm, oa_ref, ob_ref, input_grad_hbm = refs[18:25]
    (
        input_grad, pbuf, kbuf, vbuf, kt, qbuf, abuf_, wq, wo, kv, dr, ag, da, dq, dk, dv, x, dm, normed,
        moved, abuf, bbuf, fbuf, rbuf, dgk, dgg, gpair, gmid, gfar, ogrid, a0, a1, b0, b1, qa0, qa1, qb0,
        qb1, ma0, ma1, mb0, mb1, mc0, mc1, md0, md1, lsem, ssem, rsem,
    ) = refs[25:]
    base, local = first_expert()
    r, rq = expert_block(nx, ny)
    mlp_half = (2 * r + 3 * rq) // 2
    mlp_halves, halves = split(mlp_half), split(r)
    mlp_later = [slice(mlp_half + s.start, mlp_half + s.stop) for s in mlp_halves]
    link = Link(ssem, rsem)
    load = fetch(
        [(grads_hbm.at[pl.ds(2, 2)], pbuf.at[pl.ds(2, 2)])]
        + [
            (
                wo_hbm.at[pl.ds(local, 2), :, :, :, pl.ds(512 * k, 512)],
                wo.at[:, :, :, rq * k : rq * k + rq],
            )
            for k in range(3)
        ]
        + [(a_hbm, abuf_), (q_hbm, qbuf), (k_hbm, kbuf), (v_hbm, vbuf)]
        + [(wq_hbm.at[pl.ds(local, 2)], wq), (kv_hbm, kv)]
        + [(grads_hbm.at[pl.ds(0, 2)], pbuf.at[pl.ds(0, 2)])]
        + [(n_hbm.at[0], normed), (x_hbm, x), (dm_hbm, dm)],
        lsem,
    )
    greet([flip("c"), flip("zl", "zh")] + around(("x", "y")))
    mlp_rings = [
        Ring(link, "y", lambda i, h: sa_ref.at[0, i, mlp_halves[h]], ma0, ma1),
        Ring(link, "x", lambda i, h: sb_ref.at[0, i, mlp_halves[h]], mb0, mb1),
        Ring(link, "y", lambda i, h: sa_ref.at[1, i, mlp_halves[h]], mc0, mc1),
        Ring(link, "x", lambda i, h: sb_ref.at[1, i, mlp_halves[h]], md0, md1),
    ]
    for ring in mlp_rings:
        ring.start()
    dgk[...] = jnp.zeros_like(dgk)
    dgg[...] = jnp.zeros_like(dgg)

    def spread(s):
        rows = slice(PAD * s, PAD * s + PAD)
        spread_rows = mm(places(mbuf[s], 0, base), pbuf[s]).astype(BF16)
        dr[0, rows] = spread_rows[:PAD]
        dr[1, rows] = spread_rows[PAD:]

    def outward(first):
        group = slice(PAD * first, PAD * first + 2 * PAD)
        for e in range(2):
            grad = sum(
                mm(
                    dr[e, group, 512 * k : 512 * k + 512],
                    wo[e, :, :, rq * k : rq * k + rq].reshape(FF, 512),
                    NT,
                )
                for k in range(3)
            )
            attended = abuf_[e, group].astype(F32)
            grad_gate = jnp.sum(attended * grad, axis=1, keepdims=True)
            gate = jnp.concatenate(
                [slot_gate(mbuf[first + n], gbuf[first + n], 0, base + e) for n in range(2)], axis=0
            )
            for n in range(2):
                s = first + n
                (dgg if s % 2 else dgk)[s // 2, 0:2] += token_sums(
                    mbuf[s], 0, base + e, grad_gate[PAD * n : PAD * n + PAD]
                )
            ag[e, group] = (gate * attended).astype(BF16)
            da[e, group] = (gate * grad).astype(BF16)

    masks = head_masks()
    scale = HD ** (-0.5)
    collect = Collect(
        link, pbuf.at[0], pbuf.at[1], pbuf.at[2], pbuf.at[3], abuf, bbuf, fbuf, rbuf
    )

    def scores_back(s):
        rows = slice(PAD * s, PAD * s + PAD)
        dk[...] = jnp.zeros_like(dk)
        dv[...] = jnp.zeros_like(dv)
        columns = mbuf[s].astype(F32).T
        for pair in range(4):
            cols = slice(128 * pair, 128 * pair + 128)
            kt[cols] = kbuf[s, :, cols].astype(F32).T.astype(BF16)

        def block(e, carry):
            allowed = slot_mask(columns, base + e)
            turned = []
            for pair in range(4):
                cols = slice(128 * pair, 128 * pair + 128)
                q = two_heads(qbuf[e, rows, cols], masks)
                grad = two_heads(da[e, rows, cols], masks)
                probs = softmax_keys(mm(kbuf[s, :, cols], q, NT), allowed)
                grad_probs = mm(vbuf[s, :, cols], grad, NT)
                grad_scores = []
                for h in range(2):
                    gp = grad_probs[:, PAD * h : PAD * h + PAD]
                    inner = jnp.sum(gp * probs[h], axis=0, keepdims=True)
                    grad_scores.append((probs[h] * (gp - inner)).astype(BF16))
                probs = jnp.concatenate([p.astype(BF16) for p in probs], axis=1)
                grad_scores = jnp.concatenate(grad_scores, axis=1)
                dv[:, cols] += mm(probs, grad)
                dk[:, cols] += mm(grad_scores, q)
                turned.append(own_lanes(mm(kt[cols], grad_scores)) * scale)
            depth = slot_depth(mbuf[s], base + e)
            dq[e, rows] = turn(jnp.concatenate(turned, axis=1), depth, -1.0).astype(BF16)
            return carry

        lax.fori_loop(0, 2, block, 0)
        depth = as_column(mbuf[s, 7:8].astype(F32))
        tokens = slice(TOK * s, TOK * s + TOK)
        dkv_ref[tokens, 0:QW] = turn(dk[...] * scale, depth, -1.0).astype(BF16)
        dkv_ref[tokens, QW:] = dv[...].astype(BF16)

    def rows_back(first):
        group = slice(PAD * first, PAD * first + 2 * PAD)
        for e in range(2):
            moved[e] = mm(dq[e, group], wq[e], NT).astype(BF16)
        for n in (1, 0):
            s = first + n
            both = jnp.concatenate([moved[e, PAD * n : PAD * n + PAD] for e in range(2)], axis=0)
            total = mm(places(mbuf[s], 0, base), both, TN)
            tokens = slice(TOK * s, TOK * s + TOK)
            pbuf[s] = (total + mm(dkv_ref[tokens], kv[...], NT)).astype(BF16)
            if s == 3:
                collect.send_far_mate()
            if s == 1:
                collect.send_mate()

    for copy in load[:5]:
        copy.wait()
    spread(3)
    spread(2)
    outward(2)
    for copy in load[5:10]:
        copy.wait()
    scores_back(3)
    for ring in mlp_rings:
        ring.middle()
    scores_back(2)
    rows_back(2)
    collect.forward()

    load[10].wait()
    spread(1)
    spread(0)
    outward(0)
    pairs = Pairs(link, dgk, dgg, gpair, gmid, gfar)
    o_rings = [
        Ring(link, "x", lambda i, h: ogrid.at[0, i, :, halves[h]], a0, a1),
        Ring(link, "y", lambda i, h: ogrid.at[1, :, i, halves[h]], b0, b1),
    ]
    q_rings = [
        Ring(link, "x", lambda i, h: wo.at[0, i, :, halves[h]], qa0, qa1),
        Ring(link, "y", lambda i, h: wo.at[1, :, i, halves[h]], qb0, qb1),
    ]
    wide, narrow = D // nx, FF // nx
    for e in range(2):
        for t in range(nx):
            block = mm(ag[e, :, narrow * t : narrow * t + narrow], dr[e], TN).astype(BF16)
            for k in range(3):
                ogrid[e, t, :, rq * k : rq * k + rq] = block[:, 512 * k : 512 * k + 512].reshape(
                    ny, rq, 512
                )
        o_rings[e].start()
    rows_load = pltpu.make_async_copy(r_hbm, dr, lsem.at[14])
    rows_load.start()
    pairs.forward()
    scores_back(1)
    for n, ring in enumerate(mlp_rings):
        ring.end(keeper(tm, (mlp_halves, mlp_later)[n % 2], n // 2))
    for ring in o_rings:
        ring.middle()
    scores_back(0)
    rows_back(0)

    rows_load.wait()
    for e in range(2):
        for t in range(nx):
            block = mm(dr[e, :, wide * t : wide * t + wide], dq[e], TN)
            wo[e, t] = block.astype(BF16).reshape(ny, r, QW)
        q_rings[e].start()
    o_halves = [slice(r + s.start, r + s.stop) for s in halves]
    for ring, out in zip(o_rings, (oa_ref, ob_ref)):
        ring.end(keeper(out, o_halves))

    for copy in load[11:]:
        copy.wait()
    logits = logit_grads(mbuf[0], 0, gbuf[0], pairs.total())
    router_grad_ref[...] = mm(logits, normed[...])
    gain_grad_ref[...] = jnp.zeros_like(gain_grad_ref)
    for j in range(CHUNKS):
        if j == CHUNKS - 1:
            for ring in q_rings:
                ring.middle()
        grad = collect.total(j) + mm(logits[:, part(j)], router_ref[...], TN)
        own = x[part(j)].astype(F32)
        inverse = lax.rsqrt(jnp.mean(own * own, axis=-1, keepdims=True) + EPS)
        gain_grad_ref[...] += jnp.sum(grad * (own * inverse), axis=0, keepdims=True)
        weighted = grad * gain_ref[...].reshape(1, D)
        inner = jnp.mean(weighted * own, axis=-1, keepdims=True)
        input_grad[part(j)] = (
            dm[part(j)] + inverse * weighted - own * (inverse * inverse * inverse * inner)
        ).astype(BF16)
    saved = pltpu.make_async_copy(input_grad, input_grad_hbm, lsem.at[15])
    saved.start()
    for ring, out in zip(q_rings, (oa_ref, ob_ref)):
        ring.end(keeper(out, halves))
    pairs.close()
    collect.close()
    for ring in mlp_rings + o_rings + q_rings:
        ring.close()
    saved.wait()


def attn_back_call(nx, ny, *operands):
    r, rq = expert_block(nx, ny)
    mlp_block, block = 2 * r + 3 * rq, r
    copies = 4 * CHUNKS + 2 + 8 * 6
    narrow = pltpu.VMEM((2, 4 * PAD, QW), BF16)
    grid = pltpu.VMEM((2, nx, ny, block, 512), BF16)
    return pl.pallas_call(
        partial(attn_back_kernel, nx, ny),
        out_shape=(
            jax.ShapeDtypeStruct((1, D), F32),
            jax.ShapeDtypeStruct((8, D), F32),
            jax.ShapeDtypeStruct((4 * TOK, 2 * QW), BF16),
            jax.ShapeDtypeStruct((2, mlp_block, 512), F32),
            jax.ShapeDtypeStruct((ny, r + 3 * rq, 512), BF16),
            jax.ShapeDtypeStruct((nx, r + 3 * rq, 512), BF16),
            jax.ShapeDtypeStruct((TOK, D), BF16),
        ),
        in_specs=[VSPEC] * 6 + [ANY] * 12,
        out_specs=(VSPEC,) * 6 + (ANY,),
        scratch_shapes=[
            ROWS_BUF,
            pltpu.VMEM((4, TOK, D), BF16),
            pltpu.VMEM((4, TOK, QW), BF16),
            pltpu.VMEM((4, TOK, QW), BF16),
            pltpu.VMEM((QW, TOK), BF16),
            narrow,
            narrow,
            pltpu.VMEM((2, D, QW), BF16),
            grid,
            pltpu.VMEM((D, 2 * QW), BF16),
            pltpu.VMEM((2, 4 * PAD, D), BF16),
            narrow,
            narrow,
            narrow,
            pltpu.VMEM((TOK, QW), F32),
            pltpu.VMEM((TOK, QW), F32),
            ROWS_BUF,
            pltpu.VMEM((TOK, D), F32),
            ROWS_BUF,
            pltpu.VMEM((2, 2 * PAD, D), BF16),
        ]
        + [ROWS_BUF] * 4
        + [
            pltpu.VMEM((2, 8, TOK), F32),
            pltpu.VMEM((2, 8, TOK), F32),
            pltpu.VMEM((2, 8, TOK), F32),
            pltpu.VMEM((8, TOK), F32),
            pltpu.VMEM((8, TOK), F32),
            grid,
        ]
        + (ring_buffers((ny,), block) + ring_buffers((nx,), block)) * 2
        + ring_buffers((), mlp_block // 2) * 4
        + [
            pltpu.SemaphoreType.DMA((16,)),
            pltpu.SemaphoreType.DMA((copies,)),
            pltpu.SemaphoreType.DMA((copies,)),
        ],
        compiler_params=remote_params(63, 3),
        cost_estimate=pl.CostEstimate(flops=10**9, bytes_accessed=300 * 10**6, transcendentals=0),
        name="attention_backward",
    )(*operands)


def last_kernel(nx, ny, *refs):
    (
        small_a, small_b, small_c, small_d, middle_ref, tm, sa_ref, sb_ref, keep_hbm, give_hbm, n_hbm,
        dkv_hbm,
    ) = refs[:12]
    outs = refs[12:22]
    (
        output_ref, kv_ref, first_ref, second_ref, norm_ref, gate_ref, up_ref, down_ref, query_ref, out_ref,
        nb, dkv, ga, gb, kf, ko, la, lb, fb, lr, kgrid, kgive, kback, sgrid,
        ka0, ka1, kb0, kb1, s0, s1, tka, tkb, ts,
        aa0, aa1, ab0, ab1, kka0, kka1, kkb0, kkb1, ss0, ss1, tt, tk, tsm,
        zsend, zrecv, ksend, krecv, msend, mrecv, y, csend, crecv, kcsend, kcrecv, mcsend, mcrecv,
        wsend, wrecv, lsem, osem, ssem, rsem,
    ) = refs[22:]
    zl, core, zh = lax.axis_index("zl"), lax.axis_index("c"), lax.axis_index("zh")
    r, rq = expert_block(nx, ny)
    halves, k_halves, s_halves = split(r + 3 * rq), split(r // 2), split(r)
    link = Link(ssem, rsem)
    load = fetch(
        [(give_hbm.at[1], ga), (give_hbm.at[0], gb), (n_hbm, nb), (dkv_hbm, dkv)]
        + [(keep_hbm.at[1], kf), (keep_hbm.at[0], ko)],
        lsem,
    )
    saved = []

    def save(*numbers):
        for n in numbers:
            copy = pltpu.make_async_copy(refs[22 + n], outs[n], osem.at[n])
            copy.start()
            saved.append(copy)

    mate, far = flip("c"), flip("zl", "zh")
    greet([mate, far, flip("zl"), flip("zh")] + around(("x", "y")))
    seconds = [
        Ring(link, "y", lambda i, h: sa_ref.at[i, halves[h]], aa0, aa1),
        Ring(link, "x", lambda i, h: sb_ref.at[i, halves[h]], ab0, ab1),
    ]
    k_rings = [
        Ring(link, "x", lambda i, h: kgrid.at[0, i, :, k_halves[h]], ka0, ka1),
        Ring(link, "y", lambda i, h: kgrid.at[1, :, i, k_halves[h]], kb0, kb1),
    ]
    s_ring = Ring(link, "x", lambda i, h: sgrid.at[i, :, s_halves[h]], s0, s1)
    for ring in seconds:
        ring.start()
    load[0].wait()
    load[1].wait()
    late_first = link.copy(ga, la, mate)
    late_second = link.copy(gb, lb, mate)
    row = iota((8, 1), 0)
    norms = jnp.where(row == 0, small_c[...], jnp.where(row == 1, small_d[...], 0.0))
    small = jnp.concatenate(
        [small_a[...], small_b[...], norms, jnp.zeros((104, D), F32)], axis=0
    ).T
    sgrid[...] = small.astype(BF16).reshape(nx, ny, r, 128)
    s_ring.start()
    for copy in load[2:5]:
        copy.wait()
    late_first.wait_recv()
    fb[...] = (kf[...].astype(F32) + la[...].astype(F32)).astype(BF16)
    late_third = link.copy(fb, lr, far)

    wide = D // nx

    def project(side, target):
        columns = pl.ds(pl.multiple_of(side * QW, QW), QW)
        for t in range(nx):
            block = sum(
                mm(nb[s, :, wide * t : wide * t + wide], dkv[TOK * s : TOK * s + TOK, columns], TN)
                for s in range(4)
            )
            block = block.astype(BF16).reshape(ny, 2, r // 2, QW)
            for h in range(2):
                target[h, t] = block[:, h]

    project(1 - core, kgive)
    k_copy = link.copy(kgive, kback, mate)
    for ring in seconds:
        ring.middle()
    s_ring.middle()
    project(core, kgrid)
    k_copy.wait_recv()
    kgrid[...] = (kgrid[...].astype(F32) + kback[...].astype(F32)).astype(BF16)
    for ring in k_rings:
        ring.start()
    for e in range(2):
        seconds[e].end(keeper(tt, halves, e))

    fields = [(tm, 0, r), (tm, r, r)] + [(tm, 2 * r + rq * k, rq) for k in range(3)]
    fields += [(tt, 0, r)] + [(tt, r + rq * k, rq) for k in range(3)]
    to_zl = flip("zl")
    halves_to_send(fields, zsend, zl)
    z_copy = link.copy(zsend, zrecv, to_zl)
    s_ring.end(keeper(ts, s_halves))
    s_second = Ring(link, "y", lambda i, h: ts.at[i, s_halves[h]], ss0, ss1)
    s_second.start()
    for ring in k_rings:
        ring.middle()
    z_copy.wait_recv()
    add_halves(fields, zrecv, y, zl)
    quarters_to_send(fields, y, csend, core)
    c_copy = link.copy(csend, crecv, mate)
    s_second.middle()
    k_seconds = [
        Ring(link, "y", lambda i, h: tka.at[i, k_halves[h]], kka0, kka1),
        Ring(link, "x", lambda i, h: tkb.at[i, k_halves[h]], kkb0, kkb1),
    ]
    for e in range(2):
        k_rings[e].end(keeper((tka, tkb)[e], k_halves))
        k_seconds[e].start()
    c_copy.wait_recv()
    targets = [(gate_ref, None), (up_ref, None)] + [(down_ref, k) for k in range(3)]
    targets += [(query_ref, None)] + [(out_ref, k) for k in range(3)]
    place_quarters(fields, targets, y, crecv, core)
    save(5, 6, 7, 8, 9)
    for ring in k_seconds:
        ring.middle()

    def store_small(h, value):
        tsm[s_halves[h]] = value

    s_second.end(store_small)
    for e in range(2):
        k_seconds[e].end(keeper(tk, k_halves, e))
    ksend[...] = tk[1 - zl].astype(BF16)
    msend[...] = tsm[pl.ds(pl.multiple_of((1 - zl) * (r // 2), 8), r // 2)].astype(BF16)
    k_copies = [link.copy(a, b, to_zl) for a, b in ((ksend, krecv), (msend, mrecv))]
    for copy in k_copies:
        copy.wait_recv()
    k_own = tk[zl] + krecv[...].astype(F32)
    m_own = tsm[pl.ds(pl.multiple_of(zl * (r // 2), 8), r // 2)] + mrecv[...].astype(F32)
    tk[0] = k_own
    tsm[0 : r // 2] = m_own

    quarter = r // 4
    kcsend[...] = tk[0, pl.ds(pl.multiple_of((1 - core) * quarter, 8), quarter)]
    mcsend[...] = tsm[pl.ds(pl.multiple_of((1 - core) * quarter, 8), quarter)]
    m_copies = [link.copy(a, b, mate) for a, b in ((kcsend, kcrecv), (mcsend, mcrecv))]
    for copy in m_copies:
        copy.wait_recv()
    k_own = tk[0, pl.ds(pl.multiple_of(core * quarter, 8), quarter)]
    k_other = kcrecv[...]
    first = core == 0
    wsend[:, 0:QW] = jnp.where(first, k_own, k_other)
    wsend[:, QW : 2 * QW] = jnp.where(first, k_other, k_own)
    wsend[:, 2 * QW :] = tsm[pl.ds(pl.multiple_of(core * quarter, 8), quarter)] + mcrecv[...]
    w_copy = link.copy(wsend, wrecv, flip("zh"))
    load[5].wait()
    late_second.wait_recv()
    late_third.wait_recv()
    for j in range(CHUNKS):
        output_ref[part(j)] = (
            middle_ref[part(j)]
            + ko[part(j)].astype(F32)
            + lb[part(j)].astype(F32)
            + lr[part(j)].astype(F32)
        ).astype(BF16)
    save(0)
    w_copy.wait_recv()
    total = wsend[...] + wrecv[...]
    total = jnp.where(zh == 0, total[0 : r // 8], total[r // 8 :])
    kv_ref[...] = total[:, 0 : 2 * QW]
    first_ref[...] = total[:, 2 * QW : 2 * QW + 8]
    second_ref[...] = total[:, 2 * QW + 8 : 2 * QW + 16]
    norm_ref[...] = total[:, 2 * QW : 2 * QW + 128].T[16:24]
    save(1, 2, 3, 4)
    for ring in seconds + k_rings + [s_ring] + k_seconds + [s_second]:
        ring.close()
    for copy in [late_first, late_second, late_third, k_copy, z_copy, c_copy, w_copy] + k_copies + m_copies:
        copy.wait_send()
    for copy in saved:
        copy.wait()


def last_call(nx, ny, *operands):
    r, rq = expert_block(nx, ny)
    block, mlp_block, k_block = r + 3 * rq, 2 * r + 3 * rq, r // 2
    zrows = (block + mlp_block) // 2

    def small_buffers(lead):
        return [pltpu.VMEM((3,) + lead + (s.stop - s.start, 128), BF16) for s in split(r)]

    copies = 4 * 12 + 11
    results = [
        ((TOK, D), BF16),
        ((r // 8, 2 * QW), F32),
        ((r // 8, 8), F32),
        ((r // 8, 8), F32),
        ((8, r // 8), F32),
        ((4, r // 4, FF), F32),
        ((4, r // 4, FF), F32),
        ((4, rq // 4, D), F32),
        ((4, r // 4, QW), F32),
        ((4, rq // 4, D), F32),
    ]
    return pl.pallas_call(
        partial(last_kernel, nx, ny),
        out_shape=tuple(jax.ShapeDtypeStruct(*a) for a in results),
        in_specs=[VSPEC] * 8 + [ANY] * 4,
        out_specs=(ANY,) * len(results),
        scratch_shapes=[pltpu.VMEM(*a) for a in results]
        + [
            pltpu.VMEM((4, TOK, D), BF16),
            pltpu.VMEM((4 * TOK, 2 * QW), BF16),
        ]
        + [ROWS_BUF] * 8
        + [
            pltpu.VMEM((2, nx, ny, k_block, 512), BF16),
            pltpu.VMEM((2, nx, ny, k_block, 512), BF16),
            pltpu.VMEM((2, nx, ny, k_block, 512), BF16),
            pltpu.VMEM((nx, ny, r, 128), BF16),
        ]
        + ring_buffers((ny,), k_block)
        + ring_buffers((nx,), k_block)
        + small_buffers((ny,))
        + [
            pltpu.VMEM((ny, k_block, 512), BF16),
            pltpu.VMEM((nx, k_block, 512), BF16),
            pltpu.VMEM((ny, r, 128), BF16),
        ]
        + ring_buffers((), block) * 2
        + ring_buffers((), k_block) * 2
        + small_buffers(())
        + [
            pltpu.VMEM((2, block, 512), F32),
            pltpu.VMEM((2, k_block, 512), F32),
            pltpu.VMEM((r, 128), F32),
            pltpu.VMEM((2, zrows, 512), BF16),
            pltpu.VMEM((2, zrows, 512), BF16),
            pltpu.VMEM((k_block, 512), BF16),
            pltpu.VMEM((k_block, 512), BF16),
            pltpu.VMEM((r // 2, 128), BF16),
            pltpu.VMEM((r // 2, 128), BF16),
            pltpu.VMEM((2, zrows, 512), F32),
            pltpu.VMEM((2, zrows // 2, 512), F32),
            pltpu.VMEM((2, zrows // 2, 512), F32),
            pltpu.VMEM((r // 4, 512), F32),
            pltpu.VMEM((r // 4, 512), F32),
            pltpu.VMEM((r // 4, 128), F32),
            pltpu.VMEM((r // 4, 128), F32),
            pltpu.VMEM((r // 4, 2 * QW + 128), F32),
            pltpu.VMEM((r // 4, 2 * QW + 128), F32),
            pltpu.SemaphoreType.DMA((6,)),
            pltpu.SemaphoreType.DMA((len(results),)),
            pltpu.SemaphoreType.DMA((copies,)),
            pltpu.SemaphoreType.DMA((copies,)),
        ],
        compiler_params=remote_params(60, 4),
        cost_estimate=pl.CostEstimate(flops=10**9, bytes_accessed=150 * 10**6, transcendentals=0),
        name="last_sums",
    )(*operands)


def copy_kernel(norms_ref, *refs):
    n = (len(refs) - 4) // 3
    sources, targets, (first, second), bufs = refs[:n], refs[n : 2 * n], refs[2 * n : 2 * n + 2], refs[2 * n + 2 : -2]
    came = fetch(list(zip(sources, bufs)), refs[-2])
    first[...] = norms_ref[1]
    second[...] = norms_ref[0]
    left = []
    for k in range(n):
        came[k].wait()
        copy = pltpu.make_async_copy(bufs[k], targets[k], refs[-1].at[k])
        copy.start()
        left.append(copy)
    for copy in left:
        copy.wait()


def copy_call(norms, *arrays):
    count, n = norms.shape[1], len(arrays)
    return pl.pallas_call(
        copy_kernel,
        out_shape=tuple(jax.ShapeDtypeStruct(a.shape, a.dtype) for a in arrays)
        + (jax.ShapeDtypeStruct((count,), F32),) * 2,
        in_specs=[VSPEC] + [ANY] * n,
        out_specs=(ANY,) * n + (VSPEC,) * 2,
        scratch_shapes=[pltpu.VMEM(a.shape, a.dtype) for a in arrays]
        + [pltpu.SemaphoreType.DMA((n,)), pltpu.SemaphoreType.DMA((n,))],
        compiler_params=params(60),
        name="results",
    )(norms, *arrays)


def per_device(
    inputs, cotangent, norm_one, kv_weight, attn_router, query_experts, out_experts, norm_two,
    mlp_router, gate_experts, up_experts, down_experts, attn_routes, mlp_routes, slot_order,
    seg_lengths, seg_parents,
):
    nx, ny = lax.axis_size("x"), lax.axis_size("y")
    router_one, router_two = attn_router.T, mlp_router.T
    normed, keys, values, rows, q, attended, normed_twos, cots, gates, metas, middle = forward_call(
        seg_lengths, seg_parents, slot_order, jnp.swapaxes(attn_routes, 2, 3),
        jnp.swapaxes(mlp_routes, 2, 3), inputs, norm_one, norm_two,
        router_one, cotangent, kv_weight, query_experts, out_experts,
    )
    r, rq = expert_block(nx, ny)
    grad_middle, grad_norm_two, grad_router_two, sums_a, sums_b, grads_in, keep_out, give_out = mlp_call(
        nx, ny, metas, router_two, norm_two, normed_twos, cotangent, cots, middle,
        gate_experts.reshape(4, nx, ny, r, FF), up_experts.reshape(4, nx, ny, r, FF),
        down_experts.reshape(4, nx, ny, rq, D),
    )
    grad_norm_one, grad_router_one, grad_kv, sums_mlp, sums_a, sums_b, input_grad = attn_back_call(
        nx, ny, metas, gates, router_one, norm_one, sums_a, sums_b, inputs, grad_middle, normed,
        grads_in, keys, values, q, attended, query_experts, out_experts.reshape(4, nx, ny, rq, D),
        kv_weight, rows,
    )
    output, kv, router_one_grad, router_two_grad, norms, gate, up, down, query, out = last_call(
        nx, ny, grad_router_one, grad_router_two, grad_norm_two, grad_norm_one, middle, sums_mlp, sums_a,
        sums_b, keep_out, give_out, normed, grad_kv,
    )
    (
        output, input_grad, kv, router_one_grad, query, out, router_two_grad, gate, up, down, norm_one_grad,
        norm_two_grad,
    ) = copy_call(
        norms, output, input_grad, kv, router_one_grad, query, out, router_two_grad, gate, up, down
    )
    return (
        output, input_grad, norm_one_grad, kv, router_one_grad, query, out, norm_two_grad,
        router_two_grad, gate, up, down,
    )


def solution(mesh):
    total = mesh.devices.size
    grid = mesh.devices.reshape(4, total // 32, 2, 2, 2)
    fine = Mesh(grid, ("x", "y", "zl", "c", "zh"))
    copies = ("x", "y", "zl", "c")
    every = copies + ("zh",)
    weight = P("zh", None, None)
    placed = (
        P(every, None),
        P(every, None),
        P(),
        P(),
        P(),
        weight,
        weight,
        P(),
        P(),
        weight,
        weight,
        weight,
        P(copies, None, None, None),
        P(copies, None, None, None),
        P(copies, None, None, None),
        P(copies, None, None),
        P(copies, None, None),
    )
    grad = P("zh", copies, None)
    return jax.shard_map(
        per_device,
        mesh=fine,
        in_specs=placed,
        out_specs=(
            P(every, None),
            P(every, None),
            P(every),
            P(every, None),
            P(every, None),
            grad,
            grad,
            P(every),
            P(every, None),
            grad,
            grad,
            grad,
        ),
        check_vma=False,
    )
```

```python
from functools import partial
import math

import jax
import jax.numpy as jnp
from jax import lax
from jax.experimental import pallas as pl
from jax.experimental.pallas import tpu as pltpu
from jax.sharding import Mesh, PartitionSpec as P

D = 1536
HD = 64
KVH = 8
FF = 512
QW = 512
NSEG = 13
TOK = 384
CAP = 120
PAD = 128
PAIRS = 2 * TOK
EPS = 1e-06
MIB = 1 << 20
F32 = jnp.float32
BF16 = jnp.bfloat16
I32 = jnp.int32

NT = (((1,), (1,)), ((), ()))
NN = (((1,), (0,)), ((), ()))
TN = (((0,), (0,)), ((), ()))


def mm(a, b, dims=NN):
    return lax.dot_general(a, b, dims, preferred_element_type=F32)


def iota(shape, dim):
    return lax.broadcasted_iota(I32, shape, dim)


def params(mib):
    return pltpu.CompilerParams(vmem_limit_bytes=mib * MIB)


VSPEC = pl.BlockSpec(memory_space=pltpu.VMEM)
SSPEC = pl.BlockSpec(memory_space=pltpu.SMEM)
ANY = pl.BlockSpec(memory_space=pl.ANY)


def make_meta(tree, len_ref, par_ref, order_ref, routes, out_ref):
    token = iota((PAIRS, TOK), 1)
    eye = iota((PAIRS, PAIRS), 0) == iota((PAIRS, PAIRS), 1)
    lane = iota((PAIRS, PAD), 1)
    tri = (iota((PAIRS, PAIRS), 0) > iota((PAIRS, PAIRS), 1)).astype(F32).astype(BF16)
    for sub in range(2):
        order = order_ref[0, tree, sub : sub + 1].astype(F32)
        order = jnp.sum(jnp.where(eye, order, 0.0), axis=1, keepdims=True).astype(I32)
        hit = [order == 2 * token + k for k in range(2)]
        named = routes[sub][0, tree].astype(F32)
        expert = jnp.zeros((PAIRS, 1), F32)
        for k in range(2):
            expert = expert + jnp.sum(
                jnp.where(hit[k], named[k : k + 1], 0.0), axis=1, keepdims=True
            )
        onehot = (expert == lane.astype(F32)).astype(F32)
        earlier = mm(tri, onehot.astype(BF16))
        rank = jnp.sum(earlier * onehot, axis=1, keepdims=True)
        code = expert * 1024.0 + rank
        for k in range(2):
            row = jnp.sum(jnp.where(hit[k], code, 0.0), axis=0, keepdims=True)
            out_ref[2 * sub + k : 2 * sub + k + 1] = row.astype(I32)

    def segments(place):
        seg = jnp.full(place.shape, -1, I32)
        start = jnp.int32(0)
        for s in range(NSEG):
            seg = seg + (place >= start).astype(I32)
            start = start + len_ref[0, tree, s]
        parent = jnp.zeros(place.shape, I32)
        for s in range(NSEG):
            parent = jnp.where(seg == s, par_ref[0, tree, s], parent)
        grand = jnp.zeros(place.shape, I32)
        for s in range(NSEG):
            grand = jnp.where(parent == s, par_ref[0, tree, s], grand)
        return seg, parent, grand

    seg, parent, grand = segments(iota((1, TOK), 1))
    key_seg, _, _ = segments(iota((TOK, 1), 0))
    allowed = ((key_seg == seg) | (key_seg == parent) | (key_seg == grand)) & (
        iota((TOK, TOK), 0) <= iota((TOK, TOK), 1)
    )
    depth = jnp.sum(allowed.astype(F32), axis=0, keepdims=True) - 1.0
    out_ref[4:5] = seg
    out_ref[5:6] = parent
    out_ref[6:7] = grand
    out_ref[7:8] = depth.astype(I32)


def sine_cosine(angle):
    turns = jnp.floor(angle * (2.0 / math.pi) + 0.5)
    rest = (angle - turns * 1.5703125) - turns * 4.838267948966e-4
    square = rest * rest
    sine = rest + rest * square * (
        -1.6666654611e-1 + square * (8.3321608736e-3 + square * -1.9515295891e-4)
    )
    cosine = (1.0 - 0.5 * square) + square * square * (
        4.166664568298827e-2 + square * (-1.388731625493765e-3 + square * 2.443315711809948e-5)
    )
    quarter = turns.astype(I32) & 3
    odd = (quarter & 1) == 1
    first, second = jnp.where(odd, cosine, sine), jnp.where(odd, sine, cosine)
    first = jnp.where(quarter >= 2, -first, first)
    second = jnp.where((quarter == 1) | (quarter == 2), -second, second)
    return first, second


def turn(values, place, sign):
    rows = values.shape[0]
    lane = iota((1, 128), 1)
    frequency = jnp.exp((lane % 32).astype(F32) * (-math.log(10000.0) / 32.0))
    angle = place * frequency
    sine, cosine = sine_cosine(angle)
    sine = sine * sign
    first = (iota((rows, 128), 1) % 64) < 32
    sine = jnp.where(first, -sine, sine)
    parts = []
    for b in range(QW // 128):
        v = values[:, 128 * b : 128 * b + 128]
        other = jnp.where(first, pltpu.roll(v, 96, 1), pltpu.roll(v, 32, 1))
        parts.append(v * cosine + other * sine)
    return jnp.concatenate(parts, axis=1)


def as_column(row):
    eye = iota((TOK, TOK), 0) == iota((TOK, TOK), 1)
    return jnp.sum(jnp.where(eye, row, 0.0), axis=1, keepdims=True)


def hits(meta, sub, expert):
    slot = iota((PAD, 1), 0)
    target = jnp.where(slot < CAP, expert * 1024 + slot, -1)
    return (meta[2 * sub : 2 * sub + 1] == target), (meta[2 * sub + 1 : 2 * sub + 2] == target)


def places(meta, sub, base):
    both = []
    for e in range(2):
        first, second = hits(meta, sub, base + e)
        both.append((first | second).astype(F32))
    return jnp.concatenate(both, axis=0).astype(BF16)


def weighted_places(meta, gates, sub, base):
    both = []
    for e in range(2):
        first, second = hits(meta, sub, base + e)
        both.append(jnp.where(first, gates[0:1], 0.0) + jnp.where(second, gates[1:2], 0.0))
    return jnp.concatenate(both, axis=0).astype(BF16)


def slot_gate(meta, gates, sub, expert):
    first, second = hits(meta, sub, expert)
    weighted = jnp.where(first, gates[0:1], 0.0) + jnp.where(second, gates[1:2], 0.0)
    return jnp.sum(weighted, axis=1, keepdims=True)


def token_sums(meta, sub, expert, column):
    first, second = hits(meta, sub, expert)
    return jnp.concatenate(
        [
            jnp.sum(jnp.where(first, column, 0.0), axis=0, keepdims=True),
            jnp.sum(jnp.where(second, column, 0.0), axis=0, keepdims=True),
        ],
        axis=0,
    )


def pair_gates(meta, sub, logits):
    row = iota((8, TOK), 0)
    picked = [
        jnp.sum(
            jnp.where(row == meta[2 * sub + k : 2 * sub + k + 1] // 1024, logits, 0.0),
            axis=0,
            keepdims=True,
        )
        for k in range(2)
    ]
    top = jnp.maximum(picked[0], picked[1])
    raised = [jnp.exp(p - top) for p in picked]
    total = raised[0] + raised[1]
    return jnp.concatenate([raised[0] / total, raised[1] / total], axis=0)


def slot_depth(meta, expert):
    first, second = hits(meta, 0, expert)
    return jnp.sum(jnp.where(first | second, meta[7:8].astype(F32), 0.0), axis=1, keepdims=True)


def slot_mask(columns, expert):
    slot = iota((1, PAD), 1)
    target = jnp.where(slot < CAP, expert * 1024 + slot, -1).astype(F32)
    hit = (columns[:, 0:1] == target) | (columns[:, 1:2] == target)

    def row(column):
        return jnp.sum(jnp.where(hit, column, 0.0), axis=0, keepdims=True)

    key = iota((TOK, 1), 0).astype(F32)
    seg = columns[:, 4:5]
    return (
        (seg == row(seg)) | (seg == row(columns[:, 5:6])) | (seg == row(columns[:, 6:7]))
    ) & (key <= row(key))


def two_heads(rows, masks):
    return jnp.concatenate([rows * masks[0], rows * masks[1]], axis=0)


def masked(scores, allowed, h):
    return jnp.where(allowed, scores[:, PAD * h : PAD * h + PAD], -1e30)


def own_lanes(both):
    return jnp.concatenate([both[0:64, 0:PAD], both[64:128, PAD:]], axis=0).T


def logit_grads(meta, sub, gates, grads):
    inner = gates[0:1] * grads[0:1] + gates[1:2] * grads[1:2]
    row = iota((8, TOK), 0)
    total = jnp.zeros((8, TOK), F32)
    for k in range(2):
        picked = gates[k : k + 1] * (grads[k : k + 1] - inner)
        total = total + jnp.where(
            row == meta[2 * sub + k : 2 * sub + k + 1] // 1024, picked, 0.0
        )
    return total.astype(BF16)


def head_masks(weight=1.0):
    lane = iota((1, 128), 1)
    return [jnp.where(half, weight, 0.0).astype(BF16) for half in (lane < 64, lane >= 64)]


def fetch(pairs, sems):
    copies = []
    for n, (source, target) in enumerate(pairs):
        copy = pltpu.make_async_copy(source, target, sems.at[n])
        copy.start()
        copies.append(copy)
    return copies


MESH = pl.DeviceIdType.MESH
CH = 128
CHUNKS = TOK // CH


class Link:
    def __init__(self, send, recv):
        self.send, self.recv, self.count = send, recv, 0

    def copy(self, source, target, device):
        n = self.count
        self.count += 1
        copy = pltpu.make_async_remote_copy(
            src_ref=source,
            dst_ref=target,
            send_sem=self.send.at[n],
            recv_sem=self.recv.at[n],
            device_id=device,
            device_id_type=MESH,
        )
        copy.start()
        return copy


def around(axes):
    devices = []
    for axis in axes:
        n = lax.axis_size(axis)
        if n > 1:
            me = lax.axis_index(axis)
            devices += [{axis: lax.rem(me + 1, n)}, {axis: lax.rem(me + n - 1, n)}]
    return devices


def flip(*axes):
    return {axis: 1 - lax.axis_index(axis) for axis in axes}


def first_expert():
    local = 2 * lax.axis_index("c")
    return 4 * lax.axis_index("zh") + local, local


def greet(devices):
    barrier = pltpu.get_barrier_semaphore()
    for device in devices:
        pl.semaphore_signal(barrier, inc=1, device_id=device, device_id_type=MESH)
    pl.semaphore_wait(barrier, len(devices))


def part(j):
    return slice(CH * j, CH * j + CH)


class Collect:
    def __init__(self, link, own, mate, far, far_mate, abuf, bbuf, fbuf, rbuf):
        self.link, self.fbuf, self.rbuf, self.abuf, self.bbuf = link, fbuf, rbuf, abuf, bbuf
        self.own, self.mate, self.far, self.far_mate = own, mate, far, far_mate

    def send_far_mate(self):
        self.a = [
            self.link.copy(self.far_mate.at[part(j)], self.abuf.at[part(j)], flip("c"))
            for j in range(CHUNKS)
        ]

    def send_mate(self):
        self.b = [
            self.link.copy(self.mate.at[part(j)], self.bbuf.at[part(j)], flip("c"))
            for j in range(CHUNKS)
        ]

    def forward(self):
        self.f = []
        for j in range(CHUNKS):
            self.a[j].wait_recv()
            total = self.far[part(j)].astype(F32) + self.abuf[part(j)].astype(F32)
            self.fbuf[part(j)] = total.astype(BF16)
            self.f.append(
                self.link.copy(self.fbuf.at[part(j)], self.rbuf.at[part(j)], flip("zl", "zh"))
            )

    def total(self, j):
        self.b[j].wait_recv()
        self.f[j].wait_recv()
        return (
            self.own[part(j)].astype(F32)
            + self.bbuf[part(j)].astype(F32)
            + self.rbuf[part(j)].astype(F32)
        )

    def close(self):
        for copy in self.a + self.b + self.f:
            copy.wait_send()


class Spread:
    def __init__(self, link, own, landed, target, sems):
        self.link, self.own, self.landed, self.target, self.sems = link, own, landed, target, sems
        self.far, self.mate, self.local, self.relayed = [], [], [], []

    def keep(self, source, tree, j):
        local = pltpu.make_async_copy(
            source, self.target.at[tree, part(j)], self.sems.at[len(self.local)]
        )
        local.start()
        self.local.append(local)

    def send(self, j):
        source = self.own.at[part(j)]
        self.far.append(self.link.copy(source, self.landed.at[part(j)], flip("zl", "zh")))
        self.mate.append(self.link.copy(source, self.target.at[1, part(j)], flip("c")))
        self.keep(source, 0, j)

    def relay(self, j):
        self.far[j].wait_recv()
        source = self.landed.at[part(j)]
        self.relayed.append(self.link.copy(source, self.target.at[3, part(j)], flip("c")))
        self.keep(source, 2, j)

    def close(self):
        for copy in self.mate + self.relayed:
            copy.wait_recv()
        for copy in self.far + self.mate + self.relayed:
            copy.wait_send()
        for copy in self.local:
            copy.wait()


class Pairs:
    def __init__(self, link, keep, give, buf, mid, far):
        self.link, self.keep, self.buf, self.mid, self.far = link, keep, buf, mid, far
        self.first = link.copy(give, buf, flip("c"))

    def forward(self):
        self.first.wait_recv()
        self.mid[...] = self.keep[1] + self.buf[1]
        self.second = self.link.copy(self.mid, self.far, flip("zl", "zh"))

    def total(self):
        self.second.wait_recv()
        return self.keep[0] + self.buf[0] + self.far[...]

    def close(self):
        self.first.wait_send()
        self.second.wait_send()


class Ring:
    def __init__(self, link, axis, view, buf0, buf1):
        self.link, self.axis, self.view, self.buf0, self.buf1 = link, axis, view, buf0, buf1
        self.n = lax.axis_size(axis)
        me = lax.axis_index(axis)
        self.at = lambda step: lax.rem(me + step + self.n, self.n)

    def start(self):
        if self.n == 1:
            return
        right, left = {self.axis: self.at(1)}, {self.axis: self.at(-1)}
        self.c0 = self.link.copy(self.view(self.at(2), 0), self.buf0.at[0], right)
        self.c1 = self.link.copy(self.view(self.at(2), 1), self.buf1.at[0], left)
        self.c2 = self.link.copy(self.view(self.at(1), 1), self.buf1.at[1], right)
        self.c3 = self.link.copy(self.view(self.at(-1), 0), self.buf0.at[2], left)

    def middle(self):
        if self.n == 1:
            return
        right, left = {self.axis: self.at(1)}, {self.axis: self.at(-1)}
        self.c0.wait_recv()
        held = self.view(self.at(1), 0)
        held[...] = (held[...].astype(F32) + self.buf0[0].astype(F32)).astype(BF16)
        self.c4 = self.link.copy(held, self.buf0.at[1], right)
        self.c1.wait_recv()
        held = self.view(self.at(-1), 1)
        held[...] = (held[...].astype(F32) + self.buf1[0].astype(F32)).astype(BF16)
        self.c5 = self.link.copy(held, self.buf1.at[2], left)

    def end(self, store):
        if self.n == 1:
            for h in range(2):
                store(h, self.view(0, h)[...].astype(F32))
            return
        for h, waits, buf in ((0, (self.c4, self.c3), self.buf0), (1, (self.c2, self.c5), self.buf1)):
            for copy in waits:
                copy.wait_recv()
            store(
                h,
                self.view(self.at(0), h)[...].astype(F32) + buf[1].astype(F32) + buf[2].astype(F32),
            )

    def close(self):
        if self.n > 1:
            for copy in (self.c0, self.c1, self.c2, self.c3, self.c4, self.c5):
                copy.wait_send()


def split(rows):
    first = (rows // 2 + 15) // 16 * 16
    return slice(0, first), slice(first, rows)


def ring_buffers(lead, rows):
    return [pltpu.VMEM((3,) + lead + (s.stop - s.start, 512), BF16) for s in split(rows)]


def remote_params(mib, ident):
    return pltpu.CompilerParams(
        vmem_limit_bytes=mib * MIB, collective_id=ident, has_side_effects=True
    )


ROWS_BUF = pltpu.VMEM((TOK, D), BF16)


class Gather:
    def __init__(self, link, source, target):
        self.link, self.source, self.target = link, source, target

    def send(self):
        self.far = [
            self.link.copy(self.source.at[part(j)], self.target.at[1, part(j)], flip("zl", "zh"))
            for j in range(CHUNKS)
        ]
        self.mate = self.link.copy(self.source, self.target.at[0], flip("c"))
        self.relayed = []

    def relay(self, j):
        self.far[j].wait_recv()
        self.relayed.append(
            self.link.copy(self.target.at[1, part(j)], self.target.at[2, part(j)], flip("c"))
        )

    def close(self):
        for copy in self.far + [self.mate] + self.relayed:
            copy.wait_send()


def forward_kernel(*refs):
    (
        len_ref, par_ref, order_ref, routes_one, routes_two, x_ref, gain_ref, gain_two_ref, router_ref,
        cot_ref, kv_hbm, wq_hbm, wo_hbm,
        n_hbm, k_hbm, v_hbm, r_hbm, q_hbm, a_hbm, n2_hbm, cots_hbm, gate_ref, meta_ref, middle_ref, lse_ref,
        xb, nb, kb, vb, vt, columns, rb, qb, ab, obuf, pb, kv, wq, wo, mbuf, abuf, bbuf, fbuf, rbuf, own,
        landed, cb, wsem, osem, sems, ssem, rsem,
    ) = refs
    base, local = first_expert()
    link = Link(ssem, rsem)
    load = fetch(
        [(kv_hbm, kv), (wq_hbm.at[pl.ds(local, 2)], wq), (wo_hbm.at[pl.ds(local, 2)], wo)], wsem
    )
    saved = []

    def save(source, target):
        copy = pltpu.make_async_copy(source, target, osem.at[len(saved)])
        copy.start()
        saved.append(copy)

    far, mate = flip("zl", "zh"), flip("c")
    greet([mate, far])
    inputs = Gather(link, x_ref, xb)
    cots = Gather(link, cot_ref, cb)
    collect = Collect(link, pb.at[0], pb.at[1], pb.at[2], pb.at[3], abuf, bbuf, fbuf, rbuf)
    spread = Spread(link, own, landed, n2_hbm, sems)
    inputs.send()
    make_meta(
        lax.axis_index("zh"), len_ref, par_ref, order_ref, (routes_one, routes_two), mbuf.at[0]
    )
    meta_far = link.copy(mbuf.at[0], mbuf.at[2], far)
    meta_mate = link.copy(mbuf.at[0], mbuf.at[1], mate)
    gate_ref[...] = jnp.zeros_like(gate_ref)

    def tree(s, source):
        meta = mbuf[s]
        x = source[...].astype(F32)
        inverse = lax.rsqrt(jnp.mean(x * x, axis=-1, keepdims=True) + EPS)
        normed = (x * inverse * gain_ref[...].reshape(1, D)).astype(BF16)
        nb[s] = normed
        save(nb.at[s], n_hbm.at[s])
        depth = as_column(meta[7:8].astype(F32))
        kb[s] = turn(mm(normed, kv[:, :QW]), depth, 1.0).astype(BF16)
        save(kb.at[s], k_hbm.at[s])
        value = mm(normed, kv[:, QW:])
        vb[s] = value.astype(BF16)
        save(vb.at[s], v_hbm.at[s])
        vt[s] = value.T.astype(BF16)
        columns[s] = meta.astype(F32).T
        moved = mm(places(meta, 0, base), normed).astype(BF16)
        for e in range(2):
            rb[e, PAD * s : PAD * s + PAD] = moved[PAD * e : PAD * e + PAD]
            save(rb.at[e, pl.ds(PAD * s, PAD)], r_hbm.at[e, pl.ds(PAD * s, PAD)])
        gate_ref[s, 0:2] = pair_gates(meta, 0, mm(router_ref[...], normed, NT))

    masks = head_masks(HD ** (-0.5))

    def attend(first, between=None):
        group = slice(PAD * first, PAD * first + 2 * PAD)
        for e in range(2):
            depth = jnp.concatenate(
                [slot_depth(mbuf[first + n], base + e) for n in range(2)], axis=0
            )
            qb[e, group] = turn(mm(rb[e, group], wq[e]), depth, 1.0).astype(BF16)

        def block(n, carry):
            e, s = n // 2, first + n % 2
            allowed = slot_mask(columns[s], base + e)
            start = pl.multiple_of(s * PAD, PAD)
            for pair in range(4):
                cols = slice(128 * pair, 128 * pair + 128)
                q = two_heads(qb[e, pl.ds(start, PAD), cols], masks)
                scores = mm(kb[s, :, cols], q, NT)
                probs = []
                for h in range(2):
                    one = masked(scores, allowed, h)
                    top = jnp.max(one, axis=0, keepdims=True)
                    raised = jnp.exp(one - top)
                    total = jnp.sum(raised, axis=0, keepdims=True)
                    lse_ref[e, s, 2 * pair + h : 2 * pair + h + 1] = top + jnp.log(total)
                    probs.append((raised * (1.0 / total)).astype(BF16))
                probs = jnp.concatenate(probs, axis=1)
                ab[e, pl.ds(start, PAD), cols] = own_lanes(mm(vt[s, cols], probs)).astype(BF16)
            return carry

        lax.fori_loop(0, 4, block, 0)
        if between is not None:
            between()
        for e in range(2):
            save(qb.at[e, pl.ds(PAD * first, 2 * PAD)], q_hbm.at[e, pl.ds(PAD * first, 2 * PAD)])
            save(ab.at[e, pl.ds(PAD * first, 2 * PAD)], a_hbm.at[e, pl.ds(PAD * first, 2 * PAD)])
            obuf[e] = mm(ab[e, group], wo[e]).astype(BF16)
        for n in (1, 0):
            s = first + n
            pb[s] = mm(
                weighted_places(mbuf[s], gate_ref[s], 0, base),
                jnp.concatenate([obuf[e, PAD * n : PAD * n + PAD] for e in range(2)], axis=0),
                TN,
            ).astype(BF16)
            if s == 3:
                collect.send_far_mate()
            if s == 1:
                collect.send_mate()

    load[0].wait()
    tree(0, x_ref)
    meta_far.wait_recv()
    meta_on = link.copy(mbuf.at[2], mbuf.at[3], mate)
    meta_mate.wait_recv()
    inputs.relay(0)
    inputs.mate.wait_recv()
    tree(1, xb.at[0])
    load[1].wait()
    load[2].wait()
    attend(0, lambda: inputs.relay(1))
    inputs.relay(2)
    cots.send()
    tree(2, xb.at[1])
    for copy in inputs.relayed:
        copy.wait_recv()
    meta_on.wait_recv()
    tree(3, xb.at[2])
    attend(2)
    meta_ref[...] = mbuf[...]
    collect.forward()
    for j in range(CHUNKS):
        middle = x_ref[part(j)].astype(F32) + collect.total(j)
        middle_ref[part(j)] = middle
        inverse = lax.rsqrt(jnp.mean(middle * middle, axis=-1, keepdims=True) + EPS)
        own[part(j)] = (middle * inverse * gain_two_ref[...].reshape(1, D)).astype(BF16)
        spread.send(j)
    for j in range(CHUNKS):
        cots.relay(j)
    cots.mate.wait_recv()
    save(cb.at[pl.ds(0, 2)], cots_hbm.at[pl.ds(0, 2)])
    for j in range(CHUNKS):
        spread.relay(j)
    for copy in cots.relayed:
        copy.wait_recv()
    save(cb.at[2], cots_hbm.at[2])
    for copy in (meta_far, meta_mate, meta_on):
        copy.wait_send()
    inputs.close()
    cots.close()
    collect.close()
    spread.close()
    for copy in saved:
        copy.wait()


def forward_call(*operands):
    rows = jax.ShapeDtypeStruct((4, TOK, D), BF16)
    heads = jax.ShapeDtypeStruct((4, TOK, QW), BF16)
    slots = jax.ShapeDtypeStruct((2, 4 * PAD, QW), BF16)
    copies = 2 * (2 * CHUNKS + 1) + 3 + 6 * CHUNKS
    return pl.pallas_call(
        forward_kernel,
        out_shape=(
            rows,
            heads,
            heads,
            jax.ShapeDtypeStruct((2, 4 * PAD, D), BF16),
            slots,
            slots,
            rows,
            jax.ShapeDtypeStruct((3, TOK, D), BF16),
            jax.ShapeDtypeStruct((4, 8, TOK), F32),
            jax.ShapeDtypeStruct((4, 8, TOK), I32),
            jax.ShapeDtypeStruct((TOK, D), F32),
            jax.ShapeDtypeStruct((2, 4, KVH, PAD), F32),
        ),
        in_specs=[SSPEC] * 2 + [VSPEC] * 8 + [ANY] * 3,
        out_specs=(ANY,) * 8 + (VSPEC,) * 4,
        scratch_shapes=[
            pltpu.VMEM((3, TOK, D), BF16),
            pltpu.VMEM((4, TOK, D), BF16),
            pltpu.VMEM((4, TOK, QW), BF16),
            pltpu.VMEM((4, TOK, QW), BF16),
            pltpu.VMEM((4, QW, TOK), BF16),
            pltpu.VMEM((4, TOK, 8), F32),
            pltpu.VMEM((2, 4 * PAD, D), BF16),
            pltpu.VMEM((2, 4 * PAD, QW), BF16),
            pltpu.VMEM((2, 4 * PAD, QW), BF16),
            pltpu.VMEM((2, 2 * PAD, D), BF16),
            pltpu.VMEM((4, TOK, D), BF16),
            pltpu.VMEM((D, 2 * QW), BF16),
            pltpu.VMEM((2, D, QW), BF16),
            pltpu.VMEM((2, QW, D), BF16),
            pltpu.VMEM((4, 8, TOK), I32),
        ]
        + [ROWS_BUF] * 6
        + [
            pltpu.VMEM((3, TOK, D), BF16),
            pltpu.SemaphoreType.DMA((3,)),
            pltpu.SemaphoreType.DMA((30,)),
            pltpu.SemaphoreType.DMA((2 * CHUNKS,)),
            pltpu.SemaphoreType.DMA((copies,)),
            pltpu.SemaphoreType.DMA((copies,)),
        ],
        compiler_params=remote_params(60, 1),
        cost_estimate=pl.CostEstimate(flops=10**9, bytes_accessed=300 * 10**6, transcendentals=0),
        name="attention_forward",
    )(*operands)


def expert_block(nx, ny):
    return D // (nx * ny), FF // (nx * ny)


def mlp_kernel(nx, ny, *refs):
    (
        mbuf, router_ref, gain_ref, n4_hbm, cot_hbm, cots_hbm, middle_hbm, wg_hbm, wu_hbm, wd_hbm,
        gain_grad_ref, router_grad_ref, sa_ref, sb_ref, dm4_ref, keep_out, give_out, dm_hbm,
    ) = refs[:18]
    (
        pbuf, gb, mr, gr, dgu, hg, obuf, dbuf, big, middle, cot, normed, own, landed, abuf, bbuf, fbuf, rbuf,
        gates, dgk, dgg, gpair, gmid, gfar, dm_ref, a0, a1, b0, b1, c0, c1, d0, d1, sems, lsem, osem, ssem, rsem,
    ) = refs[18:]
    base, local = first_expert()
    r, rq = expert_block(nx, ny)
    half = (2 * r + 3 * rq) // 2
    halves = split(half)
    link = Link(ssem, rsem)
    load = fetch(
        [(n4_hbm.at[pl.ds(2, 2)], pbuf.at[pl.ds(2, 2)]), (cots_hbm.at[pl.ds(1, 2)], gb.at[pl.ds(2, 2)])]
        + [(wg_hbm.at[pl.ds(local, 2)], big.at[:, :, :, 0:r])]
        + [(wu_hbm.at[pl.ds(local, 2)], big.at[:, :, :, r : 2 * r])]
        + [
            (
                wd_hbm.at[pl.ds(local, 2), :, :, :, pl.ds(512 * k, 512)],
                big.at[:, :, :, 2 * r + rq * k : 2 * r + rq * k + rq],
            )
            for k in range(3)
        ]
        + [(n4_hbm.at[pl.ds(0, 2)], pbuf.at[pl.ds(0, 2)])]
        + [(cot_hbm, gb.at[0]), (cots_hbm.at[0], gb.at[1])]
        + [(n4_hbm.at[0], normed), (cot_hbm, cot), (middle_hbm, middle)],
        lsem,
    )
    greet([flip("c"), flip("zl", "zh")] + around(("x", "y")))
    dgk[...] = jnp.zeros_like(dgk)
    dgg[...] = jnp.zeros_like(dgg)
    collect = Collect(
        link, pbuf.at[0], pbuf.at[1], pbuf.at[2], pbuf.at[3], abuf, bbuf, fbuf, rbuf
    )
    spread = Spread(link, own, landed, dm4_ref, sems)
    saved = []

    def save(source, target):
        copy = pltpu.make_async_copy(source, target, osem.at[len(saved)])
        copy.start()
        saved.append(copy)

    def to_slots(s):
        gates[s] = pair_gates(mbuf[s], 1, mm(router_ref[...], pbuf[s], NT))
        hot = places(mbuf[s], 1, base)
        rows = slice(PAD * s, PAD * s + PAD)
        for source, target in ((pbuf, mr), (gb, gr)):
            moved = mm(hot, source[s]).astype(BF16)
            target[0, rows] = moved[:PAD]
            target[1, rows] = moved[PAD:]

    def weight(e, k):
        if k < 2:
            return big[e, :, :, r * k : r * k + r].reshape(D, FF)
        first = 2 * r + rq * (k - 2)
        return big[e, :, :, first : first + rq].reshape(FF, 512)

    def experts(first, e):
        rows = slice(PAD * first, PAD * first + 2 * PAD)
        x, grads = mr[e, rows], gr[e, rows]
        gate_pre, up_pre = mm(x, weight(e, 0)), mm(x, weight(e, 1))
        sigmoid = 1.0 / (1.0 + jnp.exp(-gate_pre))
        silu = gate_pre * sigmoid
        hidden = (silu * up_pre).astype(BF16)
        grad = sum(
            mm(grads[:, 512 * k : 512 * k + 512], weight(e, 2 + k), NT) for k in range(3)
        )
        for k in range(3):
            obuf[e, :, 512 * k : 512 * k + 512] = mm(hidden, weight(e, 2 + k)).astype(BF16)
        hidden = hidden.astype(F32)
        grad_gate = jnp.sum(hidden * grad, axis=1, keepdims=True)
        gate = jnp.concatenate(
            [slot_gate(mbuf[first + n], gates[first + n], 1, base + e) for n in range(2)], axis=0
        )
        for n in range(2):
            s = first + n
            (dgg if s % 2 else dgk)[s // 2, 0:2] += token_sums(
                mbuf[s], 1, base + e, grad_gate[PAD * n : PAD * n + PAD]
            )
        hg[e, rows] = (gate * hidden).astype(BF16)
        grad = gate * grad
        grad_gate_pre = (grad * up_pre * sigmoid * (1.0 + gate_pre * (1.0 - sigmoid))).astype(BF16)
        grad_up_pre = (grad * silu).astype(BF16)
        dgu[e, rows, 0:FF] = grad_gate_pre
        dgu[e, rows, FF:] = grad_up_pre
        dbuf[e] = (
            mm(grad_gate_pre, weight(e, 0), NT) + mm(grad_up_pre, weight(e, 1), NT)
        ).astype(BF16)

    def sums(first):
        for n in (1, 0):
            s = first + n
            pbuf[s] = mm(
                places(mbuf[s], 1, base),
                jnp.concatenate([dbuf[e, PAD * n : PAD * n + PAD] for e in range(2)], axis=0),
                TN,
            ).astype(BF16)
            if s == 3:
                collect.send_far_mate()
            if s == 1:
                collect.send_mate()

    def results(first):
        for n in range(2):
            s = first + n
            gb[s] = mm(
                weighted_places(mbuf[s], gates[s], 1, base),
                jnp.concatenate([obuf[e, PAD * n : PAD * n + PAD] for e in range(2)], axis=0),
                TN,
            ).astype(BF16)
            save(gb.at[s], (give_out if s % 2 else keep_out).at[s // 2])

    for copy in load[:2]:
        copy.wait()
    to_slots(2)
    to_slots(3)
    for copy in load[2:7]:
        copy.wait()
    experts(2, 0)
    experts(2, 1)
    sums(2)
    collect.forward()
    results(2)
    for copy in load[7:10]:
        copy.wait()
    to_slots(0)
    to_slots(1)
    later = [slice(half + s.start, half + s.stop) for s in halves]
    rings = [
        [
            Ring(link, "x", lambda i, h: big.at[0, i, :, halves[h]], a0, a1),
            Ring(link, "y", lambda i, h: big.at[0, :, i, later[h]], b0, b1),
        ],
        [
            Ring(link, "x", lambda i, h: big.at[1, i, :, halves[h]], c0, c1),
            Ring(link, "y", lambda i, h: big.at[1, :, i, later[h]], d0, d1),
        ],
    ]
    wide, narrow = D // nx, FF // nx
    for e in range(2):
        experts(0, e)
        for t in range(nx):
            block = mm(mr[e, :, wide * t : wide * t + wide], dgu[e], TN).astype(BF16)
            for k in range(2):
                big[e, t, :, r * k : r * k + r] = block[:, FF * k : FF * k + FF].reshape(ny, r, FF)
            block = mm(hg[e, :, narrow * t : narrow * t + narrow], gr[e], TN).astype(BF16)
            for k in range(3):
                first = 2 * r + rq * k
                big[e, t, :, first : first + rq] = block[:, 512 * k : 512 * k + 512].reshape(
                    ny, rq, 512
                )
        for ring in rings[e]:
            ring.start()
    sums(0)
    for ring in rings[0]:
        ring.middle()
    pairs = Pairs(link, dgk, dgg, gpair, gmid, gfar)
    results(0)
    pairs.forward()
    for copy in load[10:]:
        copy.wait()
    logits = logit_grads(mbuf[0], 1, gates[0], pairs.total())
    router_grad_ref[...] = mm(logits, normed[...])
    gain_grad_ref[...] = jnp.zeros_like(gain_grad_ref)
    for j in range(CHUNKS):
        if j == 1:
            for ring in rings[1]:
                ring.middle()
        grad = collect.total(j) + mm(logits[:, part(j)], router_ref[...], TN)
        mid = middle[part(j)]
        inverse = lax.rsqrt(jnp.mean(mid * mid, axis=-1, keepdims=True) + EPS)
        gain_grad_ref[...] += jnp.sum(grad * (mid * inverse), axis=0, keepdims=True)
        weighted = grad * gain_ref[...].reshape(1, D)
        inner = jnp.mean(weighted * mid, axis=-1, keepdims=True)
        result = (
            cot[part(j)].astype(F32)
            + inverse * weighted
            - mid * (inverse * inverse * inverse * inner)
        )
        own[part(j)] = result.astype(BF16)
        spread.send(j)
        dm_ref[part(j)] = result
        save(dm_ref.at[part(j)], dm_hbm.at[part(j)])
    for j in range(CHUNKS):
        spread.relay(j)
    for e in range(2):
        for ring, out in zip(rings[e], (sa_ref, sb_ref)):
            ring.end(keeper(out.at[e], halves))
            ring.close()
    pairs.close()
    collect.close()
    spread.close()
    for copy in saved:
        copy.wait()


def mlp_call(nx, ny, *operands):
    r, rq = expert_block(nx, ny)
    block = 2 * r + 3 * rq
    copies = 6 * CHUNKS + 2 + 24
    part_shape = jax.ShapeDtypeStruct((2, TOK, D), BF16)
    return pl.pallas_call(
        partial(mlp_kernel, nx, ny),
        out_shape=(
            jax.ShapeDtypeStruct((1, D), F32),
            jax.ShapeDtypeStruct((8, D), F32),
            jax.ShapeDtypeStruct((2, ny, block // 2, 512), BF16),
            jax.ShapeDtypeStruct((2, nx, block // 2, 512), BF16),
            jax.ShapeDtypeStruct((4, TOK, D), BF16),
            part_shape,
            part_shape,
            jax.ShapeDtypeStruct((TOK, D), F32),
        ),
        in_specs=[VSPEC] * 3 + [ANY] * 7,
        out_specs=(VSPEC,) * 4 + (ANY,) * 4,
        scratch_shapes=[
            pltpu.VMEM((4, TOK, D), BF16),
            pltpu.VMEM((4, TOK, D), BF16),
            pltpu.VMEM((2, 4 * PAD, D), BF16),
            pltpu.VMEM((2, 4 * PAD, D), BF16),
            pltpu.VMEM((2, 4 * PAD, 2 * FF), BF16),
            pltpu.VMEM((2, 4 * PAD, FF), BF16),
            pltpu.VMEM((2, 2 * PAD, D), BF16),
            pltpu.VMEM((2, 2 * PAD, D), BF16),
            pltpu.VMEM((2, nx, ny, block, 512), BF16),
            pltpu.VMEM((TOK, D), F32),
        ]
        + [ROWS_BUF] * 8
        + [
            pltpu.VMEM((4, 2, TOK), F32),
            pltpu.VMEM((2, 8, TOK), F32),
            pltpu.VMEM((2, 8, TOK), F32),
            pltpu.VMEM((2, 8, TOK), F32),
            pltpu.VMEM((8, TOK), F32),
            pltpu.VMEM((8, TOK), F32),
            pltpu.VMEM((TOK, D), F32),
        ]
        + (ring_buffers((ny,), block // 2) + ring_buffers((nx,), block // 2)) * 2
        + [
            pltpu.SemaphoreType.DMA((2 * CHUNKS,)),
            pltpu.SemaphoreType.DMA((13,)),
            pltpu.SemaphoreType.DMA((4 + CHUNKS,)),
            pltpu.SemaphoreType.DMA((copies,)),
            pltpu.SemaphoreType.DMA((copies,)),
        ],
        compiler_params=remote_params(63, 2),
        cost_estimate=pl.CostEstimate(flops=10**9, bytes_accessed=250 * 10**6, transcendentals=0),
        name="feed_forward",
    )(*operands)


def of_half(source, index, first, count, side):
    half = count // 2
    return source[index, pl.ds(pl.multiple_of(first + side * half, 8), half)]


def halves_to_send(fields, zsend, zl):
    for e in range(2):
        offset = 0
        for source, first, count in fields:
            zsend[e, offset : offset + count // 2] = of_half(source, e, first, count, 1 - zl).astype(BF16)
            offset += count // 2


def add_halves(fields, zrecv, y, zl):
    for e in range(2):
        offset = 0
        for source, first, count in fields:
            rows = slice(offset, offset + count // 2)
            y[e, rows] = of_half(source, e, first, count, zl) + zrecv[e, rows].astype(F32)
            offset += count // 2


def quarters_to_send(fields, y, csend, core):
    for e in range(2):
        offset = 0
        for _, _, count in fields:
            csend[e, offset // 2 : offset // 2 + count // 4] = of_half(y, e, offset, count // 2, 1 - core)
            offset += count // 2


def place_quarters(fields, targets, y, crecv, core):
    for e in range(2):
        offset = 0
        for (_, _, count), (target, k) in zip(fields, targets):
            n = count // 4
            columns = slice(None) if k is None else slice(512 * k, 512 * k + 512)
            target[core * 2 + e, :, columns] = of_half(y, e, offset, count // 2, core)
            target[(1 - core) * 2 + e, :, columns] = crecv[e, offset // 2 : offset // 2 + n]
            offset += count // 2


def keeper(target, cut, index=None):
    def store(h, value):
        if index is None:
            target[:, cut[h]] = value.astype(target.dtype)
        else:
            target[index, cut[h]] = value.astype(target.dtype)

    return store


def attn_back_kernel(nx, ny, *refs):
    (
        mbuf, gbuf, lse_ref, router_ref, gain_ref, sa_ref, sb_ref, x_hbm, dm_hbm, n_hbm, grads_hbm,
        k_hbm, v_hbm, q_hbm, a_hbm, wq_hbm, wo_hbm, kv_hbm, r_hbm,
    ) = refs[:19]
    gain_grad_ref, router_grad_ref, oa_ref, ob_ref, dkv_hbm, tm_hbm, input_grad_hbm = refs[19:26]
    (
        dkv_ref, tm, input_grad, pbuf, kbuf, vbuf, kt, qbuf, abuf_, wq, wo, kv, dr, ag, da, dq, dk, dv, x, dm, normed,
        moved, abuf, bbuf, fbuf, rbuf, dgk, dgg, gpair, gmid, gfar, ogrid, a0, a1, b0, b1, qa0, qa1, qb0,
        qb1, ma0, ma1, mb0, mb1, mc0, mc1, md0, md1, lsem, ssem, rsem,
    ) = refs[26:]
    base, local = first_expert()
    r, rq = expert_block(nx, ny)
    mlp_half = (2 * r + 3 * rq) // 2
    mlp_halves, halves = split(mlp_half), split(r)
    mlp_later = [slice(mlp_half + s.start, mlp_half + s.stop) for s in mlp_halves]
    link = Link(ssem, rsem)
    load = fetch(
        [(grads_hbm.at[pl.ds(2, 2)], pbuf.at[pl.ds(2, 2)])]
        + [
            (
                wo_hbm.at[pl.ds(local, 2), :, :, :, pl.ds(512 * k, 512)],
                wo.at[:, :, :, rq * k : rq * k + rq],
            )
            for k in range(3)
        ]
        + [(a_hbm, abuf_), (q_hbm, qbuf), (k_hbm, kbuf), (v_hbm, vbuf)]
        + [(wq_hbm.at[pl.ds(local, 2)], wq), (kv_hbm, kv)]
        + [(grads_hbm.at[pl.ds(0, 2)], pbuf.at[pl.ds(0, 2)])]
        + [(n_hbm.at[0], normed), (x_hbm, x), (dm_hbm, dm)],
        lsem,
    )
    greet([flip("c"), flip("zl", "zh")] + around(("x", "y")))
    mlp_rings = [
        Ring(link, "y", lambda i, h: sa_ref.at[0, i, mlp_halves[h]], ma0, ma1),
        Ring(link, "x", lambda i, h: sb_ref.at[0, i, mlp_halves[h]], mb0, mb1),
        Ring(link, "y", lambda i, h: sa_ref.at[1, i, mlp_halves[h]], mc0, mc1),
        Ring(link, "x", lambda i, h: sb_ref.at[1, i, mlp_halves[h]], md0, md1),
    ]
    for ring in mlp_rings:
        ring.start()
    dgk[...] = jnp.zeros_like(dgk)
    dgg[...] = jnp.zeros_like(dgg)

    def spread(s):
        rows = slice(PAD * s, PAD * s + PAD)
        spread_rows = mm(places(mbuf[s], 0, base), pbuf[s]).astype(BF16)
        dr[0, rows] = spread_rows[:PAD]
        dr[1, rows] = spread_rows[PAD:]

    def outward(first):
        group = slice(PAD * first, PAD * first + 2 * PAD)
        for e in range(2):
            grad = sum(
                mm(
                    dr[e, group, 512 * k : 512 * k + 512],
                    wo[e, :, :, rq * k : rq * k + rq].reshape(FF, 512),
                    NT,
                )
                for k in range(3)
            )
            attended = abuf_[e, group].astype(F32)
            grad_gate = jnp.sum(attended * grad, axis=1, keepdims=True)
            gate = jnp.concatenate(
                [slot_gate(mbuf[first + n], gbuf[first + n], 0, base + e) for n in range(2)], axis=0
            )
            for n in range(2):
                s = first + n
                (dgg if s % 2 else dgk)[s // 2, 0:2] += token_sums(
                    mbuf[s], 0, base + e, grad_gate[PAD * n : PAD * n + PAD]
                )
            ag[e, group] = (gate * attended).astype(BF16)
            da[e, group] = (gate * grad).astype(BF16)

    scale = HD ** (-0.5)
    masks, q_masks = head_masks(), head_masks(scale)
    collect = Collect(
        link, pbuf.at[0], pbuf.at[1], pbuf.at[2], pbuf.at[3], abuf, bbuf, fbuf, rbuf
    )

    def scores_back(s):
        rows = slice(PAD * s, PAD * s + PAD)
        dk[...] = jnp.zeros_like(dk)
        dv[...] = jnp.zeros_like(dv)
        columns = mbuf[s].astype(F32).T
        for pair in range(4):
            cols = slice(128 * pair, 128 * pair + 128)
            kt[cols] = kbuf[s, :, cols].astype(F32).T.astype(BF16)

        def block(e, carry):
            allowed = slot_mask(columns, base + e)
            turned = []
            for pair in range(4):
                cols = slice(128 * pair, 128 * pair + 128)
                q = two_heads(qbuf[e, rows, cols], q_masks)
                grad = two_heads(da[e, rows, cols], masks)
                scores = mm(kbuf[s, :, cols], q, NT)
                probs = [
                    jnp.exp(masked(scores, allowed, h) - lse_ref[e, s, 2 * pair + h : 2 * pair + h + 1])
                    for h in range(2)
                ]
                grad_probs = mm(vbuf[s, :, cols], grad, NT)
                grad_scores = []
                for h in range(2):
                    gp = grad_probs[:, PAD * h : PAD * h + PAD]
                    inner = jnp.sum(gp * probs[h], axis=0, keepdims=True)
                    grad_scores.append((probs[h] * (gp - inner)).astype(BF16))
                probs = jnp.concatenate([p.astype(BF16) for p in probs], axis=1)
                grad_scores = jnp.concatenate(grad_scores, axis=1)
                dv[:, cols] += mm(probs, grad)
                dk[:, cols] += mm(grad_scores, q)
                turned.append(own_lanes(mm(kt[cols], grad_scores)) * scale)
            depth = slot_depth(mbuf[s], base + e)
            dq[e, rows] = turn(jnp.concatenate(turned, axis=1), depth, -1.0).astype(BF16)
            return carry

        lax.fori_loop(0, 2, block, 0)
        depth = as_column(mbuf[s, 7:8].astype(F32))
        tokens = slice(TOK * s, TOK * s + TOK)
        dkv_ref[tokens, 0:QW] = turn(dk[...], depth, -1.0).astype(BF16)
        dkv_ref[tokens, QW:] = dv[...].astype(BF16)

    def rows_back(first):
        group = slice(PAD * first, PAD * first + 2 * PAD)
        for e in range(2):
            moved[e] = mm(dq[e, group], wq[e], NT).astype(BF16)
        for n in (1, 0):
            s = first + n
            both = jnp.concatenate([moved[e, PAD * n : PAD * n + PAD] for e in range(2)], axis=0)
            total = mm(places(mbuf[s], 0, base), both, TN)
            tokens = slice(TOK * s, TOK * s + TOK)
            pbuf[s] = (total + mm(dkv_ref[tokens], kv[...], NT)).astype(BF16)
            if s == 3:
                collect.send_far_mate()
            if s == 1:
                collect.send_mate()

    for copy in load[:5]:
        copy.wait()
    spread(3)
    spread(2)
    outward(2)
    for copy in load[5:10]:
        copy.wait()
    scores_back(3)
    for ring in mlp_rings:
        ring.middle()
    scores_back(2)
    rows_back(2)
    collect.forward()

    load[10].wait()
    spread(1)
    spread(0)
    outward(0)
    pairs = Pairs(link, dgk, dgg, gpair, gmid, gfar)
    o_rings = [
        Ring(link, "x", lambda i, h: ogrid.at[0, i, :, halves[h]], a0, a1),
        Ring(link, "y", lambda i, h: ogrid.at[1, :, i, halves[h]], b0, b1),
    ]
    q_rings = [
        Ring(link, "x", lambda i, h: wo.at[0, i, :, halves[h]], qa0, qa1),
        Ring(link, "y", lambda i, h: wo.at[1, :, i, halves[h]], qb0, qb1),
    ]
    wide, narrow = D // nx, FF // nx
    for e in range(2):
        for t in range(nx):
            block = mm(ag[e, :, narrow * t : narrow * t + narrow], dr[e], TN).astype(BF16)
            for k in range(3):
                ogrid[e, t, :, rq * k : rq * k + rq] = block[:, 512 * k : 512 * k + 512].reshape(
                    ny, rq, 512
                )
        o_rings[e].start()
    saved = []

    def save(source, target):
        copy = pltpu.make_async_copy(source, target, lsem.at[15 + len(saved)])
        copy.start()
        saved.append(copy)

    rows_load = pltpu.make_async_copy(r_hbm, dr, lsem.at[14])
    rows_load.start()
    pairs.forward()
    scores_back(1)
    for n, ring in enumerate(mlp_rings):
        ring.end(keeper(tm, (mlp_halves, mlp_later)[n % 2], n // 2))
    save(tm, tm_hbm)
    for ring in o_rings:
        ring.middle()
    scores_back(0)
    save(dkv_ref, dkv_hbm)
    rows_back(0)

    rows_load.wait()
    for e in range(2):
        for t in range(nx):
            block = mm(dr[e, :, wide * t : wide * t + wide], dq[e], TN)
            wo[e, t] = block.astype(BF16).reshape(ny, r, QW)
        q_rings[e].start()
    o_halves = [slice(r + s.start, r + s.stop) for s in halves]
    for ring, out in zip(o_rings, (oa_ref, ob_ref)):
        ring.end(keeper(out, o_halves))

    for copy in load[11:]:
        copy.wait()
    logits = logit_grads(mbuf[0], 0, gbuf[0], pairs.total())
    router_grad_ref[...] = mm(logits, normed[...])
    gain_grad_ref[...] = jnp.zeros_like(gain_grad_ref)
    for j in range(CHUNKS):
        if j == CHUNKS - 1:
            for ring in q_rings:
                ring.middle()
        grad = collect.total(j) + mm(logits[:, part(j)], router_ref[...], TN)
        own = x[part(j)].astype(F32)
        inverse = lax.rsqrt(jnp.mean(own * own, axis=-1, keepdims=True) + EPS)
        gain_grad_ref[...] += jnp.sum(grad * (own * inverse), axis=0, keepdims=True)
        weighted = grad * gain_ref[...].reshape(1, D)
        inner = jnp.mean(weighted * own, axis=-1, keepdims=True)
        input_grad[part(j)] = (
            dm[part(j)] + inverse * weighted - own * (inverse * inverse * inverse * inner)
        ).astype(BF16)
    save(input_grad, input_grad_hbm)
    for ring, out in zip(q_rings, (oa_ref, ob_ref)):
        ring.end(keeper(out, halves))
    pairs.close()
    collect.close()
    for ring in mlp_rings + o_rings + q_rings:
        ring.close()
    for copy in saved:
        copy.wait()


def attn_back_call(nx, ny, *operands):
    r, rq = expert_block(nx, ny)
    mlp_block, block = 2 * r + 3 * rq, r
    copies = 4 * CHUNKS + 2 + 8 * 6
    narrow = pltpu.VMEM((2, 4 * PAD, QW), BF16)
    grid = pltpu.VMEM((2, nx, ny, block, 512), BF16)
    return pl.pallas_call(
        partial(attn_back_kernel, nx, ny),
        out_shape=(
            jax.ShapeDtypeStruct((1, D), F32),
            jax.ShapeDtypeStruct((8, D), F32),
            jax.ShapeDtypeStruct((ny, r + 3 * rq, 512), BF16),
            jax.ShapeDtypeStruct((nx, r + 3 * rq, 512), BF16),
            jax.ShapeDtypeStruct((4 * TOK, 2 * QW), BF16),
            jax.ShapeDtypeStruct((2, mlp_block, 512), F32),
            jax.ShapeDtypeStruct((TOK, D), BF16),
        ),
        in_specs=[VSPEC] * 7 + [ANY] * 12,
        out_specs=(VSPEC,) * 4 + (ANY,) * 3,
        scratch_shapes=[
            pltpu.VMEM((4 * TOK, 2 * QW), BF16),
            pltpu.VMEM((2, mlp_block, 512), F32),
            ROWS_BUF,
            pltpu.VMEM((4, TOK, D), BF16),
            pltpu.VMEM((4, TOK, QW), BF16),
            pltpu.VMEM((4, TOK, QW), BF16),
            pltpu.VMEM((QW, TOK), BF16),
            narrow,
            narrow,
            pltpu.VMEM((2, D, QW), BF16),
            grid,
            pltpu.VMEM((D, 2 * QW), BF16),
            pltpu.VMEM((2, 4 * PAD, D), BF16),
            narrow,
            narrow,
            narrow,
            pltpu.VMEM((TOK, QW), F32),
            pltpu.VMEM((TOK, QW), F32),
            ROWS_BUF,
            pltpu.VMEM((TOK, D), F32),
            ROWS_BUF,
            pltpu.VMEM((2, 2 * PAD, D), BF16),
        ]
        + [ROWS_BUF] * 4
        + [
            pltpu.VMEM((2, 8, TOK), F32),
            pltpu.VMEM((2, 8, TOK), F32),
            pltpu.VMEM((2, 8, TOK), F32),
            pltpu.VMEM((8, TOK), F32),
            pltpu.VMEM((8, TOK), F32),
            grid,
        ]
        + (ring_buffers((ny,), block) + ring_buffers((nx,), block)) * 2
        + ring_buffers((), mlp_block // 2) * 4
        + [
            pltpu.SemaphoreType.DMA((18,)),
            pltpu.SemaphoreType.DMA((copies,)),
            pltpu.SemaphoreType.DMA((copies,)),
        ],
        compiler_params=remote_params(63, 3),
        cost_estimate=pl.CostEstimate(flops=10**9, bytes_accessed=300 * 10**6, transcendentals=0),
        name="attention_backward",
    )(*operands)


def last_kernel(nx, ny, *refs):
    (
        small_a, small_b, small_c, small_d, sa_ref, sb_ref, tm_hbm, middle_hbm, keep_hbm, give_hbm, n_hbm,
        dkv_hbm,
    ) = refs[:12]
    outs = refs[12:22]
    (
        output_ref, kv_ref, first_ref, second_ref, norm_ref, gate_ref, up_ref, down_ref, query_ref, out_ref,
        nb, dkv, tm, middle_ref, kblock, ga, gb, kf, ko, la, lb, fb, lr, kgrid, kgive, kback, sgrid,
        ka0, ka1, kb0, kb1, s0, s1, tka, tkb, ts,
        aa0, aa1, ab0, ab1, kka0, kka1, kkb0, kkb1, ss0, ss1, tt, tk, tsm,
        zsend, zrecv, ksend, krecv, msend, mrecv, y, csend, crecv, kcsend, kcrecv, mcsend, mcrecv,
        wsend, wrecv, lsem, osem, ssem, rsem,
    ) = refs[22:]
    zl, core, zh = lax.axis_index("zl"), lax.axis_index("c"), lax.axis_index("zh")
    r, rq = expert_block(nx, ny)
    halves, k_halves, s_halves = split(r + 3 * rq), split(r // 2), split(r)
    link = Link(ssem, rsem)
    load = fetch(
        [(give_hbm.at[1], ga), (give_hbm.at[0], gb), (keep_hbm.at[1], kf), (n_hbm, nb), (dkv_hbm, dkv)]
        + [(tm_hbm, tm), (keep_hbm.at[0], ko), (middle_hbm, middle_ref)],
        lsem,
    )
    saved = []

    def save(*numbers):
        for n in numbers:
            copy = pltpu.make_async_copy(refs[22 + n], outs[n], osem.at[n])
            copy.start()
            saved.append(copy)

    mate, far = flip("c"), flip("zl", "zh")
    greet([mate, far, flip("zl"), flip("zh")] + around(("x", "y")))
    seconds = [
        Ring(link, "y", lambda i, h: sa_ref.at[i, halves[h]], aa0, aa1),
        Ring(link, "x", lambda i, h: sb_ref.at[i, halves[h]], ab0, ab1),
    ]
    k_rings = [
        Ring(link, "x", lambda i, h: kgrid.at[0, i, :, k_halves[h]], ka0, ka1),
        Ring(link, "y", lambda i, h: kgrid.at[1, :, i, k_halves[h]], kb0, kb1),
    ]
    s_ring = Ring(link, "x", lambda i, h: sgrid.at[i, :, s_halves[h]], s0, s1)
    for ring in seconds:
        ring.start()
    load[0].wait()
    load[1].wait()
    late_first = link.copy(ga, la, mate)
    late_second = link.copy(gb, lb, mate)
    for copy in load[2:5]:
        copy.wait()

    wide = D // nx

    def project(t):
        kblock[...] = sum(
            mm(nb[s, :, wide * t : wide * t + wide], dkv[TOK * s : TOK * s + TOK], TN)
            for s in range(4)
        ).astype(BF16)
        for side, target in ((1 - core, kgive), (core, kgrid)):
            columns = pl.ds(pl.multiple_of(side * QW, QW), QW)
            block = kblock[:, columns].reshape(ny, 2, r // 2, QW)
            for h in range(2):
                target[h, t] = block[:, h]

    project(0)
    late_first.wait_recv()
    fb[...] = (kf[...].astype(F32) + la[...].astype(F32)).astype(BF16)
    late_third = link.copy(fb, lr, far)
    for t in range(1, nx):
        project(t)
    k_copy = link.copy(kgive, kback, mate)
    for ring in seconds:
        ring.middle()
    row = iota((8, 1), 0)
    norms = jnp.where(row == 0, small_c[...], jnp.where(row == 1, small_d[...], 0.0))
    small = jnp.concatenate(
        [small_a[...], small_b[...], norms, jnp.zeros((104, D), F32)], axis=0
    ).T
    sgrid[...] = small.astype(BF16).reshape(nx, ny, r, 128)
    s_ring.start()
    k_copy.wait_recv()
    kgrid[...] = (kgrid[...].astype(F32) + kback[...].astype(F32)).astype(BF16)
    for ring in k_rings:
        ring.start()
    for e in range(2):
        seconds[e].end(keeper(tt, halves, e))
    s_ring.middle()
    for copy in load[5:]:
        copy.wait()

    fields = [(tm, 0, r), (tm, r, r)] + [(tm, 2 * r + rq * k, rq) for k in range(3)]
    fields += [(tt, 0, r)] + [(tt, r + rq * k, rq) for k in range(3)]
    to_zl = flip("zl")
    halves_to_send(fields, zsend, zl)
    z_copy = link.copy(zsend, zrecv, to_zl)
    s_ring.end(keeper(ts, s_halves))
    s_second = Ring(link, "y", lambda i, h: ts.at[i, s_halves[h]], ss0, ss1)
    s_second.start()
    for ring in k_rings:
        ring.middle()
    z_copy.wait_recv()
    add_halves(fields, zrecv, y, zl)
    quarters_to_send(fields, y, csend, core)
    c_copy = link.copy(csend, crecv, mate)
    s_second.middle()
    k_seconds = [
        Ring(link, "y", lambda i, h: tka.at[i, k_halves[h]], kka0, kka1),
        Ring(link, "x", lambda i, h: tkb.at[i, k_halves[h]], kkb0, kkb1),
    ]
    for e in range(2):
        k_rings[e].end(keeper((tka, tkb)[e], k_halves))
        k_seconds[e].start()
    c_copy.wait_recv()
    targets = [(gate_ref, None), (up_ref, None)] + [(down_ref, k) for k in range(3)]
    targets += [(query_ref, None)] + [(out_ref, k) for k in range(3)]
    place_quarters(fields, targets, y, crecv, core)
    save(5, 6, 7, 8, 9)
    for ring in k_seconds:
        ring.middle()

    def store_small(h, value):
        tsm[s_halves[h]] = value

    s_second.end(store_small)
    for e in range(2):
        k_seconds[e].end(keeper(tk, k_halves, e))
    ksend[...] = tk[1 - zl].astype(BF16)
    msend[...] = tsm[pl.ds(pl.multiple_of((1 - zl) * (r // 2), 8), r // 2)].astype(BF16)
    k_copies = [link.copy(a, b, to_zl) for a, b in ((ksend, krecv), (msend, mrecv))]
    for copy in k_copies:
        copy.wait_recv()
    k_own = tk[zl] + krecv[...].astype(F32)
    m_own = tsm[pl.ds(pl.multiple_of(zl * (r // 2), 8), r // 2)] + mrecv[...].astype(F32)
    tk[0] = k_own
    tsm[0 : r // 2] = m_own

    quarter = r // 4
    kcsend[...] = tk[0, pl.ds(pl.multiple_of((1 - core) * quarter, 8), quarter)]
    mcsend[...] = tsm[pl.ds(pl.multiple_of((1 - core) * quarter, 8), quarter)]
    m_copies = [link.copy(a, b, mate) for a, b in ((kcsend, kcrecv), (mcsend, mcrecv))]
    for copy in m_copies:
        copy.wait_recv()
    k_own = tk[0, pl.ds(pl.multiple_of(core * quarter, 8), quarter)]
    k_other = kcrecv[...]
    first = core == 0
    wsend[:, 0:QW] = jnp.where(first, k_own, k_other)
    wsend[:, QW : 2 * QW] = jnp.where(first, k_other, k_own)
    wsend[:, 2 * QW :] = tsm[pl.ds(pl.multiple_of(core * quarter, 8), quarter)] + mcrecv[...]
    w_copy = link.copy(wsend, wrecv, flip("zh"))
    late_second.wait_recv()
    late_third.wait_recv()
    for j in range(CHUNKS):
        output_ref[part(j)] = (
            middle_ref[part(j)]
            + ko[part(j)].astype(F32)
            + lb[part(j)].astype(F32)
            + lr[part(j)].astype(F32)
        ).astype(BF16)
    save(0)
    w_copy.wait_recv()
    total = wsend[...] + wrecv[...]
    total = jnp.where(zh == 0, total[0 : r // 8], total[r // 8 :])
    kv_ref[...] = total[:, 0 : 2 * QW]
    first_ref[...] = total[:, 2 * QW : 2 * QW + 8]
    second_ref[...] = total[:, 2 * QW + 8 : 2 * QW + 16]
    norm_ref[...] = total[:, 2 * QW : 2 * QW + 128].T[16:24]
    save(1, 2, 3, 4)
    for ring in seconds + k_rings + [s_ring] + k_seconds + [s_second]:
        ring.close()
    for copy in [late_first, late_second, late_third, k_copy, z_copy, c_copy, w_copy] + k_copies + m_copies:
        copy.wait_send()
    for copy in saved:
        copy.wait()


def last_call(nx, ny, *operands):
    r, rq = expert_block(nx, ny)
    block, mlp_block, k_block = r + 3 * rq, 2 * r + 3 * rq, r // 2
    zrows = (block + mlp_block) // 2

    def small_buffers(lead):
        return [pltpu.VMEM((3,) + lead + (s.stop - s.start, 128), BF16) for s in split(r)]

    copies = 4 * 12 + 11
    results = [
        ((TOK, D), BF16),
        ((r // 8, 2 * QW), F32),
        ((r // 8, 8), F32),
        ((r // 8, 8), F32),
        ((8, r // 8), F32),
        ((4, r // 4, FF), F32),
        ((4, r // 4, FF), F32),
        ((4, rq // 4, D), F32),
        ((4, r // 4, QW), F32),
        ((4, rq // 4, D), F32),
    ]
    return pl.pallas_call(
        partial(last_kernel, nx, ny),
        out_shape=tuple(jax.ShapeDtypeStruct(*a) for a in results),
        in_specs=[VSPEC] * 6 + [ANY] * 6,
        out_specs=(ANY,) * len(results),
        scratch_shapes=[pltpu.VMEM(*a) for a in results]
        + [
            pltpu.VMEM((4, TOK, D), BF16),
            pltpu.VMEM((4 * TOK, 2 * QW), BF16),
            pltpu.VMEM((2, mlp_block, 512), F32),
            pltpu.VMEM((TOK, D), F32),
            pltpu.VMEM((D // nx, 2 * QW), BF16),
        ]
        + [ROWS_BUF] * 8
        + [
            pltpu.VMEM((2, nx, ny, k_block, 512), BF16),
            pltpu.VMEM((2, nx, ny, k_block, 512), BF16),
            pltpu.VMEM((2, nx, ny, k_block, 512), BF16),
            pltpu.VMEM((nx, ny, r, 128), BF16),
        ]
        + ring_buffers((ny,), k_block)
        + ring_buffers((nx,), k_block)
        + small_buffers((ny,))
        + [
            pltpu.VMEM((ny, k_block, 512), BF16),
            pltpu.VMEM((nx, k_block, 512), BF16),
            pltpu.VMEM((ny, r, 128), BF16),
        ]
        + ring_buffers((), block) * 2
        + ring_buffers((), k_block) * 2
        + small_buffers(())
        + [
            pltpu.VMEM((2, block, 512), F32),
            pltpu.VMEM((2, k_block, 512), F32),
            pltpu.VMEM((r, 128), F32),
            pltpu.VMEM((2, zrows, 512), BF16),
            pltpu.VMEM((2, zrows, 512), BF16),
            pltpu.VMEM((k_block, 512), BF16),
            pltpu.VMEM((k_block, 512), BF16),
            pltpu.VMEM((r // 2, 128), BF16),
            pltpu.VMEM((r // 2, 128), BF16),
            pltpu.VMEM((2, zrows, 512), F32),
            pltpu.VMEM((2, zrows // 2, 512), F32),
            pltpu.VMEM((2, zrows // 2, 512), F32),
            pltpu.VMEM((r // 4, 512), F32),
            pltpu.VMEM((r // 4, 512), F32),
            pltpu.VMEM((r // 4, 128), F32),
            pltpu.VMEM((r // 4, 128), F32),
            pltpu.VMEM((r // 4, 2 * QW + 128), F32),
            pltpu.VMEM((r // 4, 2 * QW + 128), F32),
            pltpu.SemaphoreType.DMA((8,)),
            pltpu.SemaphoreType.DMA((len(results),)),
            pltpu.SemaphoreType.DMA((copies,)),
            pltpu.SemaphoreType.DMA((copies,)),
        ],
        compiler_params=remote_params(60, 4),
        cost_estimate=pl.CostEstimate(flops=10**9, bytes_accessed=150 * 10**6, transcendentals=0),
        name="last_sums",
    )(*operands)


def copy_kernel(norms_ref, *refs):
    n = (len(refs) - 4) // 3
    sources, targets, (first, second), bufs = refs[:n], refs[n : 2 * n], refs[2 * n : 2 * n + 2], refs[2 * n + 2 : -2]
    came = fetch(list(zip(sources, bufs)), refs[-2])
    first[...] = norms_ref[1]
    second[...] = norms_ref[0]
    left = []
    for k in range(n):
        came[k].wait()
        copy = pltpu.make_async_copy(bufs[k], targets[k], refs[-1].at[k])
        copy.start()
        left.append(copy)
    for copy in left:
        copy.wait()


def copy_call(norms, *arrays):
    count, n = norms.shape[1], len(arrays)
    return pl.pallas_call(
        copy_kernel,
        out_shape=tuple(jax.ShapeDtypeStruct(a.shape, a.dtype) for a in arrays)
        + (jax.ShapeDtypeStruct((count,), F32),) * 2,
        in_specs=[VSPEC] + [ANY] * n,
        out_specs=(ANY,) * n + (VSPEC,) * 2,
        scratch_shapes=[pltpu.VMEM(a.shape, a.dtype) for a in arrays]
        + [pltpu.SemaphoreType.DMA((n,)), pltpu.SemaphoreType.DMA((n,))],
        compiler_params=params(60),
        name="results",
    )(norms, *arrays)


def per_device(
    inputs, cotangent, norm_one, kv_weight, attn_router, query_experts, out_experts, norm_two,
    mlp_router, gate_experts, up_experts, down_experts, attn_routes, mlp_routes, slot_order,
    seg_lengths, seg_parents,
):
    nx, ny = lax.axis_size("x"), lax.axis_size("y")
    router_one, router_two = attn_router.T, mlp_router.T
    normed, keys, values, rows, q, attended, normed_twos, cots, gates, metas, middle, lse = forward_call(
        seg_lengths, seg_parents, slot_order, jnp.swapaxes(attn_routes, 2, 3),
        jnp.swapaxes(mlp_routes, 2, 3), inputs, norm_one, norm_two,
        router_one, cotangent, kv_weight, query_experts, out_experts,
    )
    r, rq = expert_block(nx, ny)
    grad_norm_two, grad_router_two, sums_a, sums_b, grads_in, keep_out, give_out, grad_middle = mlp_call(
        nx, ny, metas, router_two, norm_two, normed_twos, cotangent, cots, middle,
        gate_experts.reshape(4, nx, ny, r, FF), up_experts.reshape(4, nx, ny, r, FF),
        down_experts.reshape(4, nx, ny, rq, D),
    )
    grad_norm_one, grad_router_one, sums_a, sums_b, grad_kv, sums_mlp, input_grad = attn_back_call(
        nx, ny, metas, gates, lse, router_one, norm_one, sums_a, sums_b, inputs, grad_middle, normed,
        grads_in, keys, values, q, attended, query_experts, out_experts.reshape(4, nx, ny, rq, D),
        kv_weight, rows,
    )
    output, kv, router_one_grad, router_two_grad, norms, gate, up, down, query, out = last_call(
        nx, ny, grad_router_one, grad_router_two, grad_norm_two, grad_norm_one, sums_a, sums_b, sums_mlp,
        middle, keep_out, give_out, normed, grad_kv,
    )
    (
        output, input_grad, kv, router_one_grad, query, out, router_two_grad, gate, up, down, norm_one_grad,
        norm_two_grad,
    ) = copy_call(
        norms, output, input_grad, kv, router_one_grad, query, out, router_two_grad, gate, up, down
    )
    return (
        output, input_grad, norm_one_grad, kv, router_one_grad, query, out, norm_two_grad,
        router_two_grad, gate, up, down,
    )


def solution(mesh):
    total = mesh.devices.size
    grid = mesh.devices.reshape(4, total // 32, 2, 2, 2)
    fine = Mesh(grid, ("x", "y", "zl", "c", "zh"))
    copies = ("x", "y", "zl", "c")
    every = copies + ("zh",)
    weight = P("zh", None, None)
    placed = (
        P(every, None),
        P(every, None),
        P(),
        P(),
        P(),
        weight,
        weight,
        P(),
        P(),
        weight,
        weight,
        weight,
        P(copies, None, None, None),
        P(copies, None, None, None),
        P(copies, None, None, None),
        P(copies, None, None),
        P(copies, None, None),
    )
    grad = P("zh", copies, None)
    return jax.shard_map(
        per_device,
        mesh=fine,
        in_specs=placed,
        out_specs=(
            P(every, None),
            P(every, None),
            P(every),
            P(every, None),
            P(every, None),
            grad,
            grad,
            P(every),
            P(every, None),
            grad,
            grad,
            grad,
        ),
        check_vma=False,
    )
```

```python
from functools import partial
import math

import jax
import jax.numpy as jnp
from jax import lax
from jax.experimental import pallas as pl
from jax.experimental.pallas import tpu as pltpu
from jax.sharding import Mesh, PartitionSpec as P

D = 1536
HD = 64
KVH = 8
FF = 512
QW = 512
NSEG = 13
TOK = 384
CAP = 120
PAD = 128
PAIRS = 2 * TOK
EPS = 1e-06
MIB = 1 << 20
F32 = jnp.float32
BF16 = jnp.bfloat16
I32 = jnp.int32

NT = (((1,), (1,)), ((), ()))
NN = (((1,), (0,)), ((), ()))
TN = (((0,), (0,)), ((), ()))


def mm(a, b, dims=NN):
    return lax.dot_general(a, b, dims, preferred_element_type=F32)


def iota(shape, dim):
    return lax.broadcasted_iota(I32, shape, dim)


def params(mib):
    return pltpu.CompilerParams(vmem_limit_bytes=mib * MIB)


VSPEC = pl.BlockSpec(memory_space=pltpu.VMEM)
SSPEC = pl.BlockSpec(memory_space=pltpu.SMEM)
ANY = pl.BlockSpec(memory_space=pl.ANY)


def make_meta(tree, len_ref, par_ref, order_ref, routes, out_ref):
    token = iota((PAIRS, TOK), 1)
    eye = iota((PAIRS, PAIRS), 0) == iota((PAIRS, PAIRS), 1)
    lane = iota((PAIRS, PAD), 1)
    tri = (iota((PAIRS, PAIRS), 0) > iota((PAIRS, PAIRS), 1)).astype(F32).astype(BF16)
    for sub in range(2):
        order = order_ref[0, tree, sub : sub + 1].astype(F32)
        order = jnp.sum(jnp.where(eye, order, 0.0), axis=1, keepdims=True).astype(I32)
        hit = [order == 2 * token + k for k in range(2)]
        named = routes[sub][0, tree].astype(F32)
        expert = jnp.zeros((PAIRS, 1), F32)
        for k in range(2):
            expert = expert + jnp.sum(
                jnp.where(hit[k], named[k : k + 1], 0.0), axis=1, keepdims=True
            )
        onehot = (expert == lane.astype(F32)).astype(F32)
        earlier = mm(tri, onehot.astype(BF16))
        rank = jnp.sum(earlier * onehot, axis=1, keepdims=True)
        code = expert * 1024.0 + rank
        for k in range(2):
            row = jnp.sum(jnp.where(hit[k], code, 0.0), axis=0, keepdims=True)
            out_ref[2 * sub + k : 2 * sub + k + 1] = row.astype(I32)

    def segments(place):
        seg = jnp.full(place.shape, -1, I32)
        start = jnp.int32(0)
        for s in range(NSEG):
            seg = seg + (place >= start).astype(I32)
            start = start + len_ref[0, tree, s]
        parent = jnp.zeros(place.shape, I32)
        for s in range(NSEG):
            parent = jnp.where(seg == s, par_ref[0, tree, s], parent)
        grand = jnp.zeros(place.shape, I32)
        for s in range(NSEG):
            grand = jnp.where(parent == s, par_ref[0, tree, s], grand)
        return seg, parent, grand

    seg, parent, grand = segments(iota((1, TOK), 1))
    key_seg, _, _ = segments(iota((TOK, 1), 0))
    allowed = ((key_seg == seg) | (key_seg == parent) | (key_seg == grand)) & (
        iota((TOK, TOK), 0) <= iota((TOK, TOK), 1)
    )
    depth = jnp.sum(allowed.astype(F32), axis=0, keepdims=True) - 1.0
    out_ref[4:5] = seg
    out_ref[5:6] = parent
    out_ref[6:7] = grand
    out_ref[7:8] = depth.astype(I32)


def sine_cosine(angle):
    turns = jnp.floor(angle * (2.0 / math.pi) + 0.5)
    rest = (angle - turns * 1.5703125) - turns * 4.838267948966e-4
    square = rest * rest
    sine = rest + rest * square * (
        -1.6666654611e-1 + square * (8.3321608736e-3 + square * -1.9515295891e-4)
    )
    cosine = (1.0 - 0.5 * square) + square * square * (
        4.166664568298827e-2 + square * (-1.388731625493765e-3 + square * 2.443315711809948e-5)
    )
    quarter = turns.astype(I32) & 3
    odd = (quarter & 1) == 1
    first, second = jnp.where(odd, cosine, sine), jnp.where(odd, sine, cosine)
    first = jnp.where(quarter >= 2, -first, first)
    second = jnp.where((quarter == 1) | (quarter == 2), -second, second)
    return first, second


def turn(values, place, sign):
    rows = values.shape[0]
    lane = iota((1, 128), 1)
    frequency = jnp.exp((lane % 32).astype(F32) * (-math.log(10000.0) / 32.0))
    angle = place * frequency
    sine, cosine = sine_cosine(angle)
    sine = sine * sign
    first = (iota((rows, 128), 1) % 64) < 32
    sine = jnp.where(first, -sine, sine)
    parts = []
    for b in range(QW // 128):
        v = values[:, 128 * b : 128 * b + 128]
        other = jnp.where(first, pltpu.roll(v, 96, 1), pltpu.roll(v, 32, 1))
        parts.append(v * cosine + other * sine)
    return jnp.concatenate(parts, axis=1)


def as_column(row):
    eye = iota((TOK, TOK), 0) == iota((TOK, TOK), 1)
    return jnp.sum(jnp.where(eye, row, 0.0), axis=1, keepdims=True)


def hits(meta, sub, expert):
    slot = iota((PAD, 1), 0)
    target = jnp.where(slot < CAP, expert * 1024 + slot, -1)
    return (meta[2 * sub : 2 * sub + 1] == target), (meta[2 * sub + 1 : 2 * sub + 2] == target)


def places(meta, sub, base):
    both = []
    for e in range(2):
        first, second = hits(meta, sub, base + e)
        both.append((first | second).astype(F32))
    return jnp.concatenate(both, axis=0).astype(BF16)


def weighted_places(meta, gates, sub, base):
    both = []
    for e in range(2):
        first, second = hits(meta, sub, base + e)
        both.append(jnp.where(first, gates[0:1], 0.0) + jnp.where(second, gates[1:2], 0.0))
    return jnp.concatenate(both, axis=0).astype(BF16)


def slot_gate(meta, gates, sub, expert):
    first, second = hits(meta, sub, expert)
    weighted = jnp.where(first, gates[0:1], 0.0) + jnp.where(second, gates[1:2], 0.0)
    return jnp.sum(weighted, axis=1, keepdims=True)


def token_sums(meta, sub, expert, column):
    first, second = hits(meta, sub, expert)
    return jnp.concatenate(
        [
            jnp.sum(jnp.where(first, column, 0.0), axis=0, keepdims=True),
            jnp.sum(jnp.where(second, column, 0.0), axis=0, keepdims=True),
        ],
        axis=0,
    )


def pair_gates(meta, sub, logits):
    row = iota((8, TOK), 0)
    picked = [
        jnp.sum(
            jnp.where(row == meta[2 * sub + k : 2 * sub + k + 1] // 1024, logits, 0.0),
            axis=0,
            keepdims=True,
        )
        for k in range(2)
    ]
    top = jnp.maximum(picked[0], picked[1])
    raised = [jnp.exp(p - top) for p in picked]
    total = raised[0] + raised[1]
    return jnp.concatenate([raised[0] / total, raised[1] / total], axis=0)


def slot_depth(meta, expert):
    first, second = hits(meta, 0, expert)
    return jnp.sum(jnp.where(first | second, meta[7:8].astype(F32), 0.0), axis=1, keepdims=True)


def slot_mask(columns, expert):
    slot = iota((1, PAD), 1)
    target = jnp.where(slot < CAP, expert * 1024 + slot, -1).astype(F32)
    hit = (columns[:, 0:1] == target) | (columns[:, 1:2] == target)

    def row(column):
        return jnp.sum(jnp.where(hit, column, 0.0), axis=0, keepdims=True)

    key = iota((TOK, 1), 0).astype(F32)
    seg = columns[:, 4:5]
    return (
        (seg == row(seg)) | (seg == row(columns[:, 5:6])) | (seg == row(columns[:, 6:7]))
    ) & (key <= row(key))


def two_heads(rows, masks):
    return jnp.concatenate([rows * masks[0], rows * masks[1]], axis=0)


def masked(scores, allowed, h):
    return jnp.where(allowed, scores[:, PAD * h : PAD * h + PAD], -1e30)


def own_lanes(both):
    return jnp.concatenate([both[0:64, 0:PAD], both[64:128, PAD:]], axis=0).T


def logit_grads(meta, sub, gates, grads):
    inner = gates[0:1] * grads[0:1] + gates[1:2] * grads[1:2]
    row = iota((8, TOK), 0)
    total = jnp.zeros((8, TOK), F32)
    for k in range(2):
        picked = gates[k : k + 1] * (grads[k : k + 1] - inner)
        total = total + jnp.where(
            row == meta[2 * sub + k : 2 * sub + k + 1] // 1024, picked, 0.0
        )
    return total.astype(BF16)


def head_masks(weight=1.0):
    lane = iota((1, 128), 1)
    return [jnp.where(half, weight, 0.0).astype(BF16) for half in (lane < 64, lane >= 64)]


def fetch(pairs, sems):
    copies = []
    for n, (source, target) in enumerate(pairs):
        copy = pltpu.make_async_copy(source, target, sems.at[n])
        copy.start()
        copies.append(copy)
    return copies


MESH = pl.DeviceIdType.MESH
CH = 128
CHUNKS = TOK // CH


class Link:
    def __init__(self, send, recv):
        self.send, self.recv, self.count = send, recv, 0

    def copy(self, source, target, device):
        n = self.count
        self.count += 1
        copy = pltpu.make_async_remote_copy(
            src_ref=source,
            dst_ref=target,
            send_sem=self.send.at[n],
            recv_sem=self.recv.at[n],
            device_id=device,
            device_id_type=MESH,
        )
        copy.start()
        return copy


def around(axes):
    devices = []
    for axis in axes:
        n = lax.axis_size(axis)
        if n > 1:
            me = lax.axis_index(axis)
            devices += [{axis: lax.rem(me + 1, n)}, {axis: lax.rem(me + n - 1, n)}]
    return devices


def flip(*axes):
    return {axis: 1 - lax.axis_index(axis) for axis in axes}


def first_expert():
    local = 2 * lax.axis_index("c")
    return 4 * lax.axis_index("zh") + local, local


def greet(devices):
    barrier = pltpu.get_barrier_semaphore()
    for device in devices:
        pl.semaphore_signal(barrier, inc=1, device_id=device, device_id_type=MESH)
    pl.semaphore_wait(barrier, len(devices))


def part(j):
    return slice(CH * j, CH * j + CH)


class Collect:
    def __init__(self, link, own, mate, far, far_mate, abuf, bbuf, fbuf, rbuf):
        self.link, self.fbuf, self.rbuf, self.abuf, self.bbuf = link, fbuf, rbuf, abuf, bbuf
        self.own, self.mate, self.far, self.far_mate = own, mate, far, far_mate

    def send_far_mate(self):
        self.a = [
            self.link.copy(self.far_mate.at[part(j)], self.abuf.at[part(j)], flip("c"))
            for j in range(CHUNKS)
        ]

    def send_mate(self):
        self.b = [
            self.link.copy(self.mate.at[part(j)], self.bbuf.at[part(j)], flip("c"))
            for j in range(CHUNKS)
        ]

    def forward(self):
        self.f = []
        for j in range(CHUNKS):
            self.a[j].wait_recv()
            total = self.far[part(j)].astype(F32) + self.abuf[part(j)].astype(F32)
            self.fbuf[part(j)] = total.astype(BF16)
            self.f.append(
                self.link.copy(self.fbuf.at[part(j)], self.rbuf.at[part(j)], flip("zl", "zh"))
            )

    def total(self, j):
        self.b[j].wait_recv()
        self.f[j].wait_recv()
        return (
            self.own[part(j)].astype(F32)
            + self.bbuf[part(j)].astype(F32)
            + self.rbuf[part(j)].astype(F32)
        )

    def close(self):
        for copy in self.a + self.b + self.f:
            copy.wait_send()


class Spread:
    def __init__(self, link, own, landed, target, sems):
        self.link, self.own, self.landed, self.target, self.sems = link, own, landed, target, sems
        self.far, self.mate, self.local, self.relayed = [], [], [], []

    def keep(self, source, tree, j):
        local = pltpu.make_async_copy(
            source, self.target.at[tree, part(j)], self.sems.at[len(self.local)]
        )
        local.start()
        self.local.append(local)

    def send(self, j):
        source = self.own.at[part(j)]
        self.far.append(self.link.copy(source, self.landed.at[part(j)], flip("zl", "zh")))
        self.mate.append(self.link.copy(source, self.target.at[1, part(j)], flip("c")))
        self.keep(source, 0, j)

    def relay(self, j):
        self.far[j].wait_recv()
        source = self.landed.at[part(j)]
        self.relayed.append(self.link.copy(source, self.target.at[3, part(j)], flip("c")))
        self.keep(source, 2, j)

    def close(self):
        for copy in self.mate + self.relayed:
            copy.wait_recv()
        for copy in self.far + self.mate + self.relayed:
            copy.wait_send()
        for copy in self.local:
            copy.wait()


class Pairs:
    def __init__(self, link, keep, give, buf, mid, far):
        self.link, self.keep, self.buf, self.mid, self.far = link, keep, buf, mid, far
        self.first = link.copy(give, buf, flip("c"))

    def forward(self):
        self.first.wait_recv()
        self.mid[...] = self.keep[1] + self.buf[1]
        self.second = self.link.copy(self.mid, self.far, flip("zl", "zh"))

    def total(self):
        self.second.wait_recv()
        return self.keep[0] + self.buf[0] + self.far[...]

    def close(self):
        self.first.wait_send()
        self.second.wait_send()


class Ring:
    def __init__(self, link, axis, view, buf0, buf1):
        self.link, self.axis, self.view, self.buf0, self.buf1 = link, axis, view, buf0, buf1
        self.n = lax.axis_size(axis)
        me = lax.axis_index(axis)
        self.at = lambda step: lax.rem(me + step + self.n, self.n)

    def start(self):
        if self.n == 1:
            return
        right, left = {self.axis: self.at(1)}, {self.axis: self.at(-1)}
        self.c0 = self.link.copy(self.view(self.at(2), 0), self.buf0.at[0], right)
        self.c1 = self.link.copy(self.view(self.at(2), 1), self.buf1.at[0], left)
        self.c2 = self.link.copy(self.view(self.at(1), 1), self.buf1.at[1], right)
        self.c3 = self.link.copy(self.view(self.at(-1), 0), self.buf0.at[2], left)

    def middle(self):
        if self.n == 1:
            return
        right, left = {self.axis: self.at(1)}, {self.axis: self.at(-1)}
        self.c0.wait_recv()
        held = self.view(self.at(1), 0)
        held[...] = (held[...].astype(F32) + self.buf0[0].astype(F32)).astype(BF16)
        self.c4 = self.link.copy(held, self.buf0.at[1], right)
        self.c1.wait_recv()
        held = self.view(self.at(-1), 1)
        held[...] = (held[...].astype(F32) + self.buf1[0].astype(F32)).astype(BF16)
        self.c5 = self.link.copy(held, self.buf1.at[2], left)

    def end(self, store):
        if self.n == 1:
            for h in range(2):
                store(h, self.view(0, h)[...].astype(F32))
            return
        for h, waits, buf in ((0, (self.c4, self.c3), self.buf0), (1, (self.c2, self.c5), self.buf1)):
            for copy in waits:
                copy.wait_recv()
            store(
                h,
                self.view(self.at(0), h)[...].astype(F32) + buf[1].astype(F32) + buf[2].astype(F32),
            )

    def close(self):
        if self.n > 1:
            for copy in (self.c0, self.c1, self.c2, self.c3, self.c4, self.c5):
                copy.wait_send()


def split(rows):
    first = (rows // 2 + 15) // 16 * 16
    return slice(0, first), slice(first, rows)


def ring_buffers(lead, rows):
    return [pltpu.VMEM((3,) + lead + (s.stop - s.start, 512), BF16) for s in split(rows)]


def remote_params(mib, ident):
    return pltpu.CompilerParams(
        vmem_limit_bytes=mib * MIB, collective_id=ident, has_side_effects=True
    )


ROWS_BUF = pltpu.VMEM((TOK, D), BF16)


class Gather:
    def __init__(self, link, source, target):
        self.link, self.source, self.target = link, source, target

    def send(self):
        self.far = [
            self.link.copy(self.source.at[part(j)], self.target.at[1, part(j)], flip("zl", "zh"))
            for j in range(CHUNKS)
        ]
        self.mate = self.link.copy(self.source, self.target.at[0], flip("c"))
        self.relayed = []

    def relay(self, j):
        self.far[j].wait_recv()
        self.relayed.append(
            self.link.copy(self.target.at[1, part(j)], self.target.at[2, part(j)], flip("c"))
        )

    def close(self):
        for copy in self.far + [self.mate] + self.relayed:
            copy.wait_send()


def forward_kernel(*refs):
    (
        len_ref, par_ref, order_ref, routes_one, routes_two, x_ref, gain_ref, gain_two_ref, router_ref,
        cot_ref, kv_hbm, wq_hbm, wo_hbm,
        n_hbm, k_hbm, v_hbm, r_hbm, q_hbm, a_hbm, n2_hbm, cots_hbm, gate_ref, meta_ref, middle_ref, lse_ref,
        xb, nb, kb, vb, vt, columns, rb, qb, ab, obuf, pb, kv, wq, wo, mbuf, abuf, bbuf, fbuf, rbuf, own,
        landed, cb, wsem, osem, sems, ssem, rsem,
    ) = refs
    base, local = first_expert()
    link = Link(ssem, rsem)
    load = fetch(
        [(kv_hbm, kv), (wq_hbm.at[pl.ds(local, 2)], wq), (wo_hbm.at[pl.ds(local, 2)], wo)], wsem
    )
    saved = []

    def save(source, target):
        copy = pltpu.make_async_copy(source, target, osem.at[len(saved)])
        copy.start()
        saved.append(copy)

    far, mate = flip("zl", "zh"), flip("c")
    greet([mate, far])
    inputs = Gather(link, x_ref, xb)
    cots = Gather(link, cot_ref, cb)
    collect = Collect(link, pb.at[0], pb.at[1], pb.at[2], pb.at[3], abuf, bbuf, fbuf, rbuf)
    spread = Spread(link, own, landed, n2_hbm, sems)
    inputs.send()
    make_meta(
        lax.axis_index("zh"), len_ref, par_ref, order_ref, (routes_one, routes_two), mbuf.at[0]
    )
    meta_far = link.copy(mbuf.at[0], mbuf.at[2], far)
    meta_mate = link.copy(mbuf.at[0], mbuf.at[1], mate)
    gate_ref[...] = jnp.zeros_like(gate_ref)

    def tree(s, source):
        meta = mbuf[s]
        x = source[...].astype(F32)
        inverse = lax.rsqrt(jnp.mean(x * x, axis=-1, keepdims=True) + EPS)
        normed = (x * inverse * gain_ref[...].reshape(1, D)).astype(BF16)
        nb[s] = normed
        save(nb.at[s], n_hbm.at[s])
        depth = as_column(meta[7:8].astype(F32))
        kb[s] = turn(mm(normed, kv[:, :QW]), depth, 1.0).astype(BF16)
        save(kb.at[s], k_hbm.at[s])
        value = mm(normed, kv[:, QW:])
        vb[s] = value.astype(BF16)
        save(vb.at[s], v_hbm.at[s])
        vt[s] = value.T.astype(BF16)
        columns[s] = meta.astype(F32).T
        moved = mm(places(meta, 0, base), normed).astype(BF16)
        for e in range(2):
            rb[e, PAD * s : PAD * s + PAD] = moved[PAD * e : PAD * e + PAD]
            save(rb.at[e, pl.ds(PAD * s, PAD)], r_hbm.at[e, pl.ds(PAD * s, PAD)])
        gate_ref[s, 0:2] = pair_gates(meta, 0, mm(router_ref[...], normed, NT))

    masks = head_masks(HD ** (-0.5))

    def attend(first, between=None):
        group = slice(PAD * first, PAD * first + 2 * PAD)
        for e in range(2):
            depth = jnp.concatenate(
                [slot_depth(mbuf[first + n], base + e) for n in range(2)], axis=0
            )
            qb[e, group] = turn(mm(rb[e, group], wq[e]), depth, 1.0).astype(BF16)

        def block(n, carry):
            e, s = n // 2, first + n % 2
            allowed = slot_mask(columns[s], base + e)
            start = pl.multiple_of(s * PAD, PAD)
            for pair in range(4):
                cols = slice(128 * pair, 128 * pair + 128)
                q = two_heads(qb[e, pl.ds(start, PAD), cols], masks)
                scores = mm(kb[s, :, cols], q, NT)
                probs = []
                for h in range(2):
                    one = masked(scores, allowed, h)
                    top = jnp.max(one, axis=0, keepdims=True)
                    raised = jnp.exp(one - top)
                    total = jnp.sum(raised, axis=0, keepdims=True)
                    lse_ref[e, s, 2 * pair + h : 2 * pair + h + 1] = top + jnp.log(total)
                    probs.append((raised * (1.0 / total)).astype(BF16))
                probs = jnp.concatenate(probs, axis=1)
                ab[e, pl.ds(start, PAD), cols] = own_lanes(mm(vt[s, cols], probs)).astype(BF16)
            return carry

        lax.fori_loop(0, 4, block, 0)
        if between is not None:
            between()
        for e in range(2):
            save(qb.at[e, pl.ds(PAD * first, 2 * PAD)], q_hbm.at[e, pl.ds(PAD * first, 2 * PAD)])
            save(ab.at[e, pl.ds(PAD * first, 2 * PAD)], a_hbm.at[e, pl.ds(PAD * first, 2 * PAD)])
            obuf[e] = mm(ab[e, group], wo[e]).astype(BF16)
        for n in (1, 0):
            s = first + n
            pb[s] = mm(
                weighted_places(mbuf[s], gate_ref[s], 0, base),
                jnp.concatenate([obuf[e, PAD * n : PAD * n + PAD] for e in range(2)], axis=0),
                TN,
            ).astype(BF16)
            if s == 3:
                collect.send_far_mate()
            if s == 1:
                collect.send_mate()

    load[0].wait()
    tree(0, x_ref)
    meta_far.wait_recv()
    meta_on = link.copy(mbuf.at[2], mbuf.at[3], mate)
    meta_mate.wait_recv()
    inputs.relay(0)
    inputs.mate.wait_recv()
    tree(1, xb.at[0])
    load[1].wait()
    load[2].wait()
    attend(0, lambda: inputs.relay(1))
    inputs.relay(2)
    cots.send()
    tree(2, xb.at[1])
    for copy in inputs.relayed:
        copy.wait_recv()
    meta_on.wait_recv()
    tree(3, xb.at[2])
    attend(2)
    meta_ref[...] = mbuf[...]
    collect.forward()
    for j in range(CHUNKS):
        middle = x_ref[part(j)].astype(F32) + collect.total(j)
        middle_ref[part(j)] = middle
        inverse = lax.rsqrt(jnp.mean(middle * middle, axis=-1, keepdims=True) + EPS)
        own[part(j)] = (middle * inverse * gain_two_ref[...].reshape(1, D)).astype(BF16)
        spread.send(j)
    for j in range(CHUNKS):
        cots.relay(j)
    cots.mate.wait_recv()
    save(cb.at[pl.ds(0, 2)], cots_hbm.at[pl.ds(0, 2)])
    for j in range(CHUNKS):
        spread.relay(j)
    for copy in cots.relayed:
        copy.wait_recv()
    save(cb.at[2], cots_hbm.at[2])
    for copy in (meta_far, meta_mate, meta_on):
        copy.wait_send()
    inputs.close()
    cots.close()
    collect.close()
    spread.close()
    for copy in saved:
        copy.wait()


def forward_call(*operands):
    rows = jax.ShapeDtypeStruct((4, TOK, D), BF16)
    heads = jax.ShapeDtypeStruct((4, TOK, QW), BF16)
    slots = jax.ShapeDtypeStruct((2, 4 * PAD, QW), BF16)
    copies = 2 * (2 * CHUNKS + 1) + 3 + 6 * CHUNKS
    return pl.pallas_call(
        forward_kernel,
        out_shape=(
            rows,
            heads,
            heads,
            jax.ShapeDtypeStruct((2, 4 * PAD, D), BF16),
            slots,
            slots,
            rows,
            jax.ShapeDtypeStruct((3, TOK, D), BF16),
            jax.ShapeDtypeStruct((4, 8, TOK), F32),
            jax.ShapeDtypeStruct((4, 8, TOK), I32),
            jax.ShapeDtypeStruct((TOK, D), F32),
            jax.ShapeDtypeStruct((2, 4, KVH, PAD), F32),
        ),
        in_specs=[SSPEC] * 2 + [VSPEC] * 8 + [ANY] * 3,
        out_specs=(ANY,) * 8 + (VSPEC,) * 4,
        scratch_shapes=[
            pltpu.VMEM((3, TOK, D), BF16),
            pltpu.VMEM((4, TOK, D), BF16),
            pltpu.VMEM((4, TOK, QW), BF16),
            pltpu.VMEM((4, TOK, QW), BF16),
            pltpu.VMEM((4, QW, TOK), BF16),
            pltpu.VMEM((4, TOK, 8), F32),
            pltpu.VMEM((2, 4 * PAD, D), BF16),
            pltpu.VMEM((2, 4 * PAD, QW), BF16),
            pltpu.VMEM((2, 4 * PAD, QW), BF16),
            pltpu.VMEM((2, 2 * PAD, D), BF16),
            pltpu.VMEM((4, TOK, D), BF16),
            pltpu.VMEM((D, 2 * QW), BF16),
            pltpu.VMEM((2, D, QW), BF16),
            pltpu.VMEM((2, QW, D), BF16),
            pltpu.VMEM((4, 8, TOK), I32),
        ]
        + [ROWS_BUF] * 6
        + [
            pltpu.VMEM((3, TOK, D), BF16),
            pltpu.SemaphoreType.DMA((3,)),
            pltpu.SemaphoreType.DMA((30,)),
            pltpu.SemaphoreType.DMA((2 * CHUNKS,)),
            pltpu.SemaphoreType.DMA((copies,)),
            pltpu.SemaphoreType.DMA((copies,)),
        ],
        compiler_params=remote_params(60, 1),
        cost_estimate=pl.CostEstimate(flops=10**9, bytes_accessed=300 * 10**6, transcendentals=0),
        name="attention_forward",
    )(*operands)


def expert_block(nx, ny):
    return D // (nx * ny), FF // (nx * ny)


def mlp_kernel(nx, ny, *refs):
    (
        mbuf, router_ref, gain_ref, n4_hbm, cot_hbm, cots_hbm, middle_hbm, wg_hbm, wu_hbm, wd_hbm,
        gain_grad_ref, router_grad_ref, sa_ref, sb_ref, dm4_ref, keep_out, give_out, dm_hbm,
    ) = refs[:18]
    (
        pbuf, gb, mr, gr, dgu, hg, obuf, dbuf, big, middle, cot, normed, own, landed, abuf, bbuf, fbuf, rbuf,
        gates, dgk, dgg, gpair, gmid, gfar, dm_ref, a0, a1, b0, b1, c0, c1, d0, d1, sems, lsem, osem, ssem, rsem,
    ) = refs[18:]
    base, local = first_expert()
    r, rq = expert_block(nx, ny)
    half = (2 * r + 3 * rq) // 2
    halves = split(half)
    link = Link(ssem, rsem)
    load = fetch(
        [(n4_hbm.at[pl.ds(2, 2)], pbuf.at[pl.ds(2, 2)]), (cots_hbm.at[pl.ds(1, 2)], gb.at[pl.ds(2, 2)])]
        + [(wg_hbm.at[pl.ds(local, 2)], big.at[:, :, :, 0:r])]
        + [(wu_hbm.at[pl.ds(local, 2)], big.at[:, :, :, r : 2 * r])]
        + [
            (
                wd_hbm.at[pl.ds(local, 2), :, :, :, pl.ds(512 * k, 512)],
                big.at[:, :, :, 2 * r + rq * k : 2 * r + rq * k + rq],
            )
            for k in range(3)
        ]
        + [(n4_hbm.at[pl.ds(0, 2)], pbuf.at[pl.ds(0, 2)])]
        + [(cot_hbm, gb.at[0]), (cots_hbm.at[0], gb.at[1])]
        + [(n4_hbm.at[0], normed), (cot_hbm, cot), (middle_hbm, middle)],
        lsem,
    )
    greet([flip("c"), flip("zl", "zh")] + around(("x", "y")))
    dgk[...] = jnp.zeros_like(dgk)
    dgg[...] = jnp.zeros_like(dgg)
    collect = Collect(
        link, pbuf.at[0], pbuf.at[1], pbuf.at[2], pbuf.at[3], abuf, bbuf, fbuf, rbuf
    )
    spread = Spread(link, own, landed, dm4_ref, sems)
    saved = []

    def save(source, target):
        copy = pltpu.make_async_copy(source, target, osem.at[len(saved)])
        copy.start()
        saved.append(copy)

    def to_slots(s):
        gates[s] = pair_gates(mbuf[s], 1, mm(router_ref[...], pbuf[s], NT))
        hot = places(mbuf[s], 1, base)
        rows = slice(PAD * s, PAD * s + PAD)
        for source, target in ((pbuf, mr), (gb, gr)):
            moved = mm(hot, source[s]).astype(BF16)
            target[0, rows] = moved[:PAD]
            target[1, rows] = moved[PAD:]

    def weight(e, k):
        if k < 2:
            return big[e, :, :, r * k : r * k + r].reshape(D, FF)
        first = 2 * r + rq * (k - 2)
        return big[e, :, :, first : first + rq].reshape(FF, 512)

    def experts(first, e):
        rows = slice(PAD * first, PAD * first + 2 * PAD)
        x, grads = mr[e, rows], gr[e, rows]
        gate_pre, up_pre = mm(x, weight(e, 0)), mm(x, weight(e, 1))
        sigmoid = 1.0 / (1.0 + jnp.exp(-gate_pre))
        silu = gate_pre * sigmoid
        hidden = (silu * up_pre).astype(BF16)
        grad = sum(
            mm(grads[:, 512 * k : 512 * k + 512], weight(e, 2 + k), NT) for k in range(3)
        )
        for k in range(3):
            obuf[e, :, 512 * k : 512 * k + 512] = mm(hidden, weight(e, 2 + k)).astype(BF16)
        hidden = hidden.astype(F32)
        grad_gate = jnp.sum(hidden * grad, axis=1, keepdims=True)
        gate = jnp.concatenate(
            [slot_gate(mbuf[first + n], gates[first + n], 1, base + e) for n in range(2)], axis=0
        )
        for n in range(2):
            s = first + n
            (dgg if s % 2 else dgk)[s // 2, 0:2] += token_sums(
                mbuf[s], 1, base + e, grad_gate[PAD * n : PAD * n + PAD]
            )
        hg[e, rows] = (gate * hidden).astype(BF16)
        grad = gate * grad
        grad_gate_pre = (grad * up_pre * sigmoid * (1.0 + gate_pre * (1.0 - sigmoid))).astype(BF16)
        grad_up_pre = (grad * silu).astype(BF16)
        dgu[e, rows, 0:FF] = grad_gate_pre
        dgu[e, rows, FF:] = grad_up_pre
        dbuf[e] = (
            mm(grad_gate_pre, weight(e, 0), NT) + mm(grad_up_pre, weight(e, 1), NT)
        ).astype(BF16)

    def sums(first):
        for n in (1, 0):
            s = first + n
            pbuf[s] = mm(
                places(mbuf[s], 1, base),
                jnp.concatenate([dbuf[e, PAD * n : PAD * n + PAD] for e in range(2)], axis=0),
                TN,
            ).astype(BF16)
            if s == 3:
                collect.send_far_mate()
            if s == 1:
                collect.send_mate()

    def results(first):
        for n in range(2):
            s = first + n
            gb[s] = mm(
                weighted_places(mbuf[s], gates[s], 1, base),
                jnp.concatenate([obuf[e, PAD * n : PAD * n + PAD] for e in range(2)], axis=0),
                TN,
            ).astype(BF16)
            save(gb.at[s], (give_out if s % 2 else keep_out).at[s // 2])

    for copy in load[:2]:
        copy.wait()
    to_slots(2)
    to_slots(3)
    for copy in load[2:7]:
        copy.wait()
    experts(2, 0)
    experts(2, 1)
    sums(2)
    collect.forward()
    results(2)
    for copy in load[7:10]:
        copy.wait()
    to_slots(0)
    to_slots(1)
    later = [slice(half + s.start, half + s.stop) for s in halves]
    rings = [
        [
            Ring(link, "x", lambda i, h: big.at[0, i, :, halves[h]], a0, a1),
            Ring(link, "y", lambda i, h: big.at[0, :, i, later[h]], b0, b1),
        ],
        [
            Ring(link, "x", lambda i, h: big.at[1, i, :, halves[h]], c0, c1),
            Ring(link, "y", lambda i, h: big.at[1, :, i, later[h]], d0, d1),
        ],
    ]
    wide, narrow = D // nx, FF // nx
    for e in range(2):
        experts(0, e)
        for t in range(nx):
            block = mm(mr[e, :, wide * t : wide * t + wide], dgu[e], TN).astype(BF16)
            for k in range(2):
                big[e, t, :, r * k : r * k + r] = block[:, FF * k : FF * k + FF].reshape(ny, r, FF)
            block = mm(hg[e, :, narrow * t : narrow * t + narrow], gr[e], TN).astype(BF16)
            for k in range(3):
                first = 2 * r + rq * k
                big[e, t, :, first : first + rq] = block[:, 512 * k : 512 * k + 512].reshape(
                    ny, rq, 512
                )
        for ring in rings[e]:
            ring.start()
    sums(0)
    for ring in rings[0]:
        ring.middle()
    pairs = Pairs(link, dgk, dgg, gpair, gmid, gfar)
    results(0)
    pairs.forward()
    for copy in load[10:]:
        copy.wait()
    logits = logit_grads(mbuf[0], 1, gates[0], pairs.total())
    router_grad_ref[...] = mm(logits, normed[...])
    gain_grad_ref[...] = jnp.zeros_like(gain_grad_ref)
    for j in range(CHUNKS):
        if j == 1:
            for ring in rings[1]:
                ring.middle()
        grad = collect.total(j) + mm(logits[:, part(j)], router_ref[...], TN)
        mid = middle[part(j)]
        inverse = lax.rsqrt(jnp.mean(mid * mid, axis=-1, keepdims=True) + EPS)
        gain_grad_ref[...] += jnp.sum(grad * (mid * inverse), axis=0, keepdims=True)
        weighted = grad * gain_ref[...].reshape(1, D)
        inner = jnp.mean(weighted * mid, axis=-1, keepdims=True)
        result = (
            cot[part(j)].astype(F32)
            + inverse * weighted
            - mid * (inverse * inverse * inverse * inner)
        )
        own[part(j)] = result.astype(BF16)
        spread.send(j)
        dm_ref[part(j)] = result
        save(dm_ref.at[part(j)], dm_hbm.at[part(j)])
    for j in range(CHUNKS):
        spread.relay(j)
    for e in range(2):
        for ring, out in zip(rings[e], (sa_ref, sb_ref)):
            ring.end(keeper(out.at[e], halves))
            ring.close()
    pairs.close()
    collect.close()
    spread.close()
    for copy in saved:
        copy.wait()


def mlp_call(nx, ny, *operands):
    r, rq = expert_block(nx, ny)
    block = 2 * r + 3 * rq
    copies = 6 * CHUNKS + 2 + 24
    part_shape = jax.ShapeDtypeStruct((2, TOK, D), BF16)
    return pl.pallas_call(
        partial(mlp_kernel, nx, ny),
        out_shape=(
            jax.ShapeDtypeStruct((1, D), F32),
            jax.ShapeDtypeStruct((8, D), F32),
            jax.ShapeDtypeStruct((2, ny, block // 2, 512), BF16),
            jax.ShapeDtypeStruct((2, nx, block // 2, 512), BF16),
            jax.ShapeDtypeStruct((4, TOK, D), BF16),
            part_shape,
            part_shape,
            jax.ShapeDtypeStruct((TOK, D), F32),
        ),
        in_specs=[VSPEC] * 3 + [ANY] * 7,
        out_specs=(VSPEC,) * 4 + (ANY,) * 4,
        scratch_shapes=[
            pltpu.VMEM((4, TOK, D), BF16),
            pltpu.VMEM((4, TOK, D), BF16),
            pltpu.VMEM((2, 4 * PAD, D), BF16),
            pltpu.VMEM((2, 4 * PAD, D), BF16),
            pltpu.VMEM((2, 4 * PAD, 2 * FF), BF16),
            pltpu.VMEM((2, 4 * PAD, FF), BF16),
            pltpu.VMEM((2, 2 * PAD, D), BF16),
            pltpu.VMEM((2, 2 * PAD, D), BF16),
            pltpu.VMEM((2, nx, ny, block, 512), BF16),
            pltpu.VMEM((TOK, D), F32),
        ]
        + [ROWS_BUF] * 8
        + [
            pltpu.VMEM((4, 2, TOK), F32),
            pltpu.VMEM((2, 8, TOK), F32),
            pltpu.VMEM((2, 8, TOK), F32),
            pltpu.VMEM((2, 8, TOK), F32),
            pltpu.VMEM((8, TOK), F32),
            pltpu.VMEM((8, TOK), F32),
            pltpu.VMEM((TOK, D), F32),
        ]
        + (ring_buffers((ny,), block // 2) + ring_buffers((nx,), block // 2)) * 2
        + [
            pltpu.SemaphoreType.DMA((2 * CHUNKS,)),
            pltpu.SemaphoreType.DMA((13,)),
            pltpu.SemaphoreType.DMA((4 + CHUNKS,)),
            pltpu.SemaphoreType.DMA((copies,)),
            pltpu.SemaphoreType.DMA((copies,)),
        ],
        compiler_params=remote_params(63, 2),
        cost_estimate=pl.CostEstimate(flops=10**9, bytes_accessed=250 * 10**6, transcendentals=0),
        name="feed_forward",
    )(*operands)


def of_half(source, index, first, count, side):
    half = count // 2
    return source[index, pl.ds(pl.multiple_of(first + side * half, 8), half)]


def halves_to_send(fields, zsend, zl):
    for e in range(2):
        offset = 0
        for source, first, count in fields:
            zsend[e, offset : offset + count // 2] = of_half(source, e, first, count, 1 - zl).astype(BF16)
            offset += count // 2


def add_halves(fields, zrecv, y, zl):
    for e in range(2):
        offset = 0
        for source, first, count in fields:
            rows = slice(offset, offset + count // 2)
            y[e, rows] = of_half(source, e, first, count, zl) + zrecv[e, rows].astype(F32)
            offset += count // 2


def quarters_to_send(fields, y, csend, core):
    for e in range(2):
        offset = 0
        for _, _, count in fields:
            csend[e, offset // 2 : offset // 2 + count // 4] = of_half(y, e, offset, count // 2, 1 - core)
            offset += count // 2


def place_quarters(fields, targets, y, crecv, core):
    for e in range(2):
        offset = 0
        for (_, _, count), (target, k) in zip(fields, targets):
            n = count // 4
            columns = slice(None) if k is None else slice(512 * k, 512 * k + 512)
            target[core * 2 + e, :, columns] = of_half(y, e, offset, count // 2, core)
            target[(1 - core) * 2 + e, :, columns] = crecv[e, offset // 2 : offset // 2 + n]
            offset += count // 2


def keeper(target, cut, index=None):
    def store(h, value):
        if index is None:
            target[:, cut[h]] = value.astype(target.dtype)
        else:
            target[index, cut[h]] = value.astype(target.dtype)

    return store


def attn_back_kernel(nx, ny, *refs):
    (
        mbuf, gbuf, lse_ref, router_ref, gain_ref, sa_ref, sb_ref, x_hbm, dm_hbm, n_hbm, grads_hbm,
        k_hbm, v_hbm, q_hbm, a_hbm, wq_hbm, wo_hbm, kv_hbm, r_hbm,
    ) = refs[:19]
    gain_grad_ref, router_grad_ref, oa_ref, ob_ref, dkv_hbm, tm_hbm, input_grad_hbm = refs[19:26]
    (
        dkv_ref, tm, input_grad, pbuf, kbuf, vbuf, kt, qbuf, abuf_, wq, wo, kv, dr, ag, da, dq, dk, dv, x, dm, normed,
        moved, abuf, bbuf, fbuf, rbuf, dgk, dgg, gpair, gmid, gfar, ogrid, a0, a1, b0, b1, qa0, qa1, qb0,
        qb1, ma0, ma1, mb0, mb1, mc0, mc1, md0, md1, lsem, ssem, rsem,
    ) = refs[26:]
    base, local = first_expert()
    r, rq = expert_block(nx, ny)
    mlp_half = (2 * r + 3 * rq) // 2
    mlp_halves, halves = split(mlp_half), split(r)
    mlp_later = [slice(mlp_half + s.start, mlp_half + s.stop) for s in mlp_halves]
    link = Link(ssem, rsem)
    load = fetch(
        [(grads_hbm.at[pl.ds(2, 2)], pbuf.at[pl.ds(2, 2)])]
        + [
            (
                wo_hbm.at[pl.ds(local, 2), :, :, :, pl.ds(512 * k, 512)],
                wo.at[:, :, :, rq * k : rq * k + rq],
            )
            for k in range(3)
        ]
        + [(a_hbm, abuf_), (q_hbm, qbuf), (k_hbm, kbuf), (v_hbm, vbuf)]
        + [(wq_hbm.at[pl.ds(local, 2)], wq), (kv_hbm, kv)]
        + [(grads_hbm.at[pl.ds(0, 2)], pbuf.at[pl.ds(0, 2)])]
        + [(n_hbm.at[0], normed), (x_hbm, x), (dm_hbm, dm)],
        lsem,
    )
    greet([flip("c"), flip("zl", "zh")] + around(("x", "y")))
    mlp_rings = [
        Ring(link, "y", lambda i, h: sa_ref.at[0, i, mlp_halves[h]], ma0, ma1),
        Ring(link, "x", lambda i, h: sb_ref.at[0, i, mlp_halves[h]], mb0, mb1),
        Ring(link, "y", lambda i, h: sa_ref.at[1, i, mlp_halves[h]], mc0, mc1),
        Ring(link, "x", lambda i, h: sb_ref.at[1, i, mlp_halves[h]], md0, md1),
    ]
    for ring in mlp_rings:
        ring.start()
    dgk[...] = jnp.zeros_like(dgk)
    dgg[...] = jnp.zeros_like(dgg)

    def spread(s):
        rows = slice(PAD * s, PAD * s + PAD)
        spread_rows = mm(places(mbuf[s], 0, base), pbuf[s]).astype(BF16)
        dr[0, rows] = spread_rows[:PAD]
        dr[1, rows] = spread_rows[PAD:]

    def outward(first):
        group = slice(PAD * first, PAD * first + 2 * PAD)
        for e in range(2):
            grad = sum(
                mm(
                    dr[e, group, 512 * k : 512 * k + 512],
                    wo[e, :, :, rq * k : rq * k + rq].reshape(FF, 512),
                    NT,
                )
                for k in range(3)
            )
            attended = abuf_[e, group].astype(F32)
            grad_gate = jnp.sum(attended * grad, axis=1, keepdims=True)
            gate = jnp.concatenate(
                [slot_gate(mbuf[first + n], gbuf[first + n], 0, base + e) for n in range(2)], axis=0
            )
            for n in range(2):
                s = first + n
                (dgg if s % 2 else dgk)[s // 2, 0:2] += token_sums(
                    mbuf[s], 0, base + e, grad_gate[PAD * n : PAD * n + PAD]
                )
            ag[e, group] = (gate * attended).astype(BF16)
            da[e, group] = (gate * grad).astype(BF16)

    scale = HD ** (-0.5)
    masks, q_masks = head_masks(), head_masks(scale)
    collect = Collect(
        link, pbuf.at[0], pbuf.at[1], pbuf.at[2], pbuf.at[3], abuf, bbuf, fbuf, rbuf
    )

    def scores_back(s):
        rows = slice(PAD * s, PAD * s + PAD)
        dk[...] = jnp.zeros_like(dk)
        dv[...] = jnp.zeros_like(dv)
        columns = mbuf[s].astype(F32).T
        for pair in range(4):
            cols = slice(128 * pair, 128 * pair + 128)
            kt[cols] = kbuf[s, :, cols].astype(F32).T.astype(BF16)

        def block(e, carry):
            allowed = slot_mask(columns, base + e)
            turned = []
            for pair in range(4):
                cols = slice(128 * pair, 128 * pair + 128)
                q = two_heads(qbuf[e, rows, cols], q_masks)
                grad = two_heads(da[e, rows, cols], masks)
                scores = mm(kbuf[s, :, cols], q, NT)
                probs = [
                    jnp.exp(masked(scores, allowed, h) - lse_ref[e, s, 2 * pair + h : 2 * pair + h + 1])
                    for h in range(2)
                ]
                grad_probs = mm(vbuf[s, :, cols], grad, NT)
                grad_scores = []
                for h in range(2):
                    gp = grad_probs[:, PAD * h : PAD * h + PAD]
                    inner = jnp.sum(gp * probs[h], axis=0, keepdims=True)
                    grad_scores.append((probs[h] * (gp - inner)).astype(BF16))
                probs = jnp.concatenate([p.astype(BF16) for p in probs], axis=1)
                grad_scores = jnp.concatenate(grad_scores, axis=1)
                dv[:, cols] += mm(probs, grad)
                dk[:, cols] += mm(grad_scores, q)
                turned.append(own_lanes(mm(kt[cols], grad_scores)) * scale)
            depth = slot_depth(mbuf[s], base + e)
            dq[e, rows] = turn(jnp.concatenate(turned, axis=1), depth, -1.0).astype(BF16)
            return carry

        lax.fori_loop(0, 2, block, 0)
        depth = as_column(mbuf[s, 7:8].astype(F32))
        tokens = slice(TOK * s, TOK * s + TOK)
        dkv_ref[tokens, 0:QW] = turn(dk[...], depth, -1.0).astype(BF16)
        dkv_ref[tokens, QW:] = dv[...].astype(BF16)

    def rows_back(first):
        group = slice(PAD * first, PAD * first + 2 * PAD)
        for e in range(2):
            moved[e] = mm(dq[e, group], wq[e], NT).astype(BF16)
        for n in (1, 0):
            s = first + n
            both = jnp.concatenate([moved[e, PAD * n : PAD * n + PAD] for e in range(2)], axis=0)
            total = mm(places(mbuf[s], 0, base), both, TN)
            tokens = slice(TOK * s, TOK * s + TOK)
            pbuf[s] = (total + mm(dkv_ref[tokens], kv[...], NT)).astype(BF16)
            if s == 3:
                collect.send_far_mate()
            if s == 1:
                collect.send_mate()

    load[0].wait()
    spread(3)
    spread(2)
    for copy in load[1:5]:
        copy.wait()
    outward(2)
    for copy in load[5:10]:
        copy.wait()
    scores_back(3)
    for ring in mlp_rings:
        ring.middle()
    scores_back(2)
    rows_back(2)
    collect.forward()

    load[10].wait()
    spread(1)
    spread(0)
    outward(0)
    pairs = Pairs(link, dgk, dgg, gpair, gmid, gfar)
    o_rings = [
        Ring(link, "x", lambda i, h: ogrid.at[0, i, :, halves[h]], a0, a1),
        Ring(link, "y", lambda i, h: ogrid.at[1, :, i, halves[h]], b0, b1),
    ]
    q_rings = [
        Ring(link, "x", lambda i, h: wo.at[0, i, :, halves[h]], qa0, qa1),
        Ring(link, "y", lambda i, h: wo.at[1, :, i, halves[h]], qb0, qb1),
    ]
    wide, narrow = D // nx, FF // nx
    for e in range(2):
        for t in range(nx):
            block = mm(ag[e, :, narrow * t : narrow * t + narrow], dr[e], TN).astype(BF16)
            for k in range(3):
                ogrid[e, t, :, rq * k : rq * k + rq] = block[:, 512 * k : 512 * k + 512].reshape(
                    ny, rq, 512
                )
        o_rings[e].start()
    saved = []

    def save(source, target):
        copy = pltpu.make_async_copy(source, target, lsem.at[17 + len(saved)])
        copy.start()
        saved.append(copy)

    rows_load = pltpu.make_async_copy(r_hbm, dr, lsem.at[16])
    rows_load.start()
    pairs.forward()
    scores_back(1)
    for n, ring in enumerate(mlp_rings):
        ring.end(keeper(tm, (mlp_halves, mlp_later)[n % 2], n // 2))
    save(tm, tm_hbm)
    for ring in o_rings:
        ring.middle()
    scores_back(0)
    save(dkv_ref, dkv_hbm)
    rows_back(0)

    rows_load.wait()
    for e in range(2):
        for t in range(nx):
            block = mm(dr[e, :, wide * t : wide * t + wide], dq[e], TN)
            wo[e, t] = block.astype(BF16).reshape(ny, r, QW)
        q_rings[e].start()
    o_halves = [slice(r + s.start, r + s.stop) for s in halves]
    for ring, out in zip(o_rings, (oa_ref, ob_ref)):
        ring.end(keeper(out, o_halves))

    for copy in load[11:14]:
        copy.wait()
    logits = logit_grads(mbuf[0], 0, gbuf[0], pairs.total())
    router_grad_ref[...] = mm(logits, normed[...])
    gain_grad_ref[...] = jnp.zeros_like(gain_grad_ref)
    for j in range(CHUNKS):
        if j == CHUNKS - 1:
            for ring in q_rings:
                ring.middle()
        grad = collect.total(j) + mm(logits[:, part(j)], router_ref[...], TN)
        own = x[part(j)].astype(F32)
        inverse = lax.rsqrt(jnp.mean(own * own, axis=-1, keepdims=True) + EPS)
        gain_grad_ref[...] += jnp.sum(grad * (own * inverse), axis=0, keepdims=True)
        weighted = grad * gain_ref[...].reshape(1, D)
        inner = jnp.mean(weighted * own, axis=-1, keepdims=True)
        input_grad[part(j)] = (
            dm[part(j)] + inverse * weighted - own * (inverse * inverse * inverse * inner)
        ).astype(BF16)
    save(input_grad, input_grad_hbm)
    for ring, out in zip(q_rings, (oa_ref, ob_ref)):
        ring.end(keeper(out, halves))
    pairs.close()
    collect.close()
    for ring in mlp_rings + o_rings + q_rings:
        ring.close()
    for copy in saved:
        copy.wait()


def attn_back_call(nx, ny, *operands):
    r, rq = expert_block(nx, ny)
    mlp_block, block = 2 * r + 3 * rq, r
    copies = 4 * CHUNKS + 2 + 8 * 6
    narrow = pltpu.VMEM((2, 4 * PAD, QW), BF16)
    grid = pltpu.VMEM((2, nx, ny, block, 512), BF16)
    return pl.pallas_call(
        partial(attn_back_kernel, nx, ny),
        out_shape=(
            jax.ShapeDtypeStruct((1, D), F32),
            jax.ShapeDtypeStruct((8, D), F32),
            jax.ShapeDtypeStruct((ny, r + 3 * rq, 512), BF16),
            jax.ShapeDtypeStruct((nx, r + 3 * rq, 512), BF16),
            jax.ShapeDtypeStruct((4 * TOK, 2 * QW), BF16),
            jax.ShapeDtypeStruct((2, mlp_block, 512), F32),
            jax.ShapeDtypeStruct((TOK, D), BF16),
        ),
        in_specs=[VSPEC] * 7 + [ANY] * 12,
        out_specs=(VSPEC,) * 4 + (ANY,) * 3,
        scratch_shapes=[
            pltpu.VMEM((4 * TOK, 2 * QW), BF16),
            pltpu.VMEM((2, mlp_block, 512), F32),
            ROWS_BUF,
            pltpu.VMEM((4, TOK, D), BF16),
            pltpu.VMEM((4, TOK, QW), BF16),
            pltpu.VMEM((4, TOK, QW), BF16),
            pltpu.VMEM((QW, TOK), BF16),
            narrow,
            narrow,
            pltpu.VMEM((2, D, QW), BF16),
            grid,
            pltpu.VMEM((D, 2 * QW), BF16),
            pltpu.VMEM((2, 4 * PAD, D), BF16),
            narrow,
            narrow,
            narrow,
            pltpu.VMEM((TOK, QW), F32),
            pltpu.VMEM((TOK, QW), F32),
            ROWS_BUF,
            pltpu.VMEM((TOK, D), F32),
            ROWS_BUF,
            pltpu.VMEM((2, 2 * PAD, D), BF16),
        ]
        + [ROWS_BUF] * 4
        + [
            pltpu.VMEM((2, 8, TOK), F32),
            pltpu.VMEM((2, 8, TOK), F32),
            pltpu.VMEM((2, 8, TOK), F32),
            pltpu.VMEM((8, TOK), F32),
            pltpu.VMEM((8, TOK), F32),
            grid,
        ]
        + (ring_buffers((ny,), block) + ring_buffers((nx,), block)) * 2
        + ring_buffers((), mlp_block // 2) * 4
        + [
            pltpu.SemaphoreType.DMA((20,)),
            pltpu.SemaphoreType.DMA((copies,)),
            pltpu.SemaphoreType.DMA((copies,)),
        ],
        compiler_params=remote_params(63, 3),
        cost_estimate=pl.CostEstimate(flops=10**9, bytes_accessed=300 * 10**6, transcendentals=0),
        name="attention_backward",
    )(*operands)


def last_kernel(nx, ny, *refs):
    (
        small_a, small_b, small_c, small_d, sa_ref, sb_ref, tm_hbm, middle_hbm, keep_hbm, give_hbm, n_hbm,
        dkv_hbm,
    ) = refs[:12]
    outs = refs[12:22]
    (
        output_ref, kv_ref, first_ref, second_ref, norm_ref, gate_ref, up_ref, down_ref, query_ref, out_ref,
        nb, dkv, tm, middle_ref, kblock, ga, gb, kf, ko, la, lb, fb, lr, kgrid, kgive, kback, sgrid,
        ka0, ka1, kb0, kb1, s0, s1, tka, tkb, ts,
        aa0, aa1, ab0, ab1, kka0, kka1, kkb0, kkb1, ss0, ss1, tt, tk, tsm,
        zsend, zrecv, y, csend, crecv, pieces, landed, lsem, osem, ssem, rsem,
    ) = refs[22:]
    zl, core, zh = lax.axis_index("zl"), lax.axis_index("c"), lax.axis_index("zh")
    r, rq = expert_block(nx, ny)
    halves, k_halves, s_halves = split(r + 3 * rq), split(r // 2), split(r)
    link = Link(ssem, rsem)
    load = fetch(
        [(give_hbm.at[1], ga), (give_hbm.at[0], gb), (keep_hbm.at[1], kf), (n_hbm, nb), (dkv_hbm, dkv)]
        + [(tm_hbm, tm), (keep_hbm.at[0], ko), (middle_hbm, middle_ref)],
        lsem,
    )
    saved = []

    def save(*numbers):
        for n in numbers:
            copy = pltpu.make_async_copy(refs[22 + n], outs[n], osem.at[n])
            copy.start()
            saved.append(copy)

    mate, far = flip("c"), flip("zl", "zh")
    column = ["c"], ["zl"], ["zh"], ["c", "zl"], ["c", "zh"], ["zl", "zh"], ["c", "zl", "zh"]
    greet([flip(*axes) for axes in column] + around(("x", "y")))
    seconds = [
        Ring(link, "y", lambda i, h: sa_ref.at[i, halves[h]], aa0, aa1),
        Ring(link, "x", lambda i, h: sb_ref.at[i, halves[h]], ab0, ab1),
    ]
    k_rings = [
        Ring(link, "x", lambda i, h: kgrid.at[0, i, :, k_halves[h]], ka0, ka1),
        Ring(link, "y", lambda i, h: kgrid.at[1, :, i, k_halves[h]], kb0, kb1),
    ]
    s_ring = Ring(link, "x", lambda i, h: sgrid.at[i, :, s_halves[h]], s0, s1)
    for ring in seconds:
        ring.start()
    load[0].wait()
    load[1].wait()
    late_first = link.copy(ga, la, mate)
    late_second = link.copy(gb, lb, mate)
    for copy in load[2:5]:
        copy.wait()

    wide = D // nx

    def project(t):
        kblock[...] = sum(
            mm(nb[s, :, wide * t : wide * t + wide], dkv[TOK * s : TOK * s + TOK], TN)
            for s in range(4)
        ).astype(BF16)
        for side, target in ((1 - core, kgive), (core, kgrid)):
            columns = pl.ds(pl.multiple_of(side * QW, QW), QW)
            block = kblock[:, columns].reshape(ny, 2, r // 2, QW)
            for h in range(2):
                target[h, t] = block[:, h]

    pieces[...] = jnp.zeros_like(pieces)
    project(0)
    late_first.wait_recv()
    fb[...] = (kf[...].astype(F32) + la[...].astype(F32)).astype(BF16)
    late_third = link.copy(fb, lr, far)
    for t in range(1, nx):
        project(t)
    k_copy = link.copy(kgive, kback, mate)
    for ring in seconds:
        ring.middle()
    row = iota((8, 1), 0)
    norms = jnp.where(row == 0, small_c[...], jnp.where(row == 1, small_d[...], 0.0))
    small = jnp.concatenate(
        [small_a[...], small_b[...], norms, jnp.zeros((104, D), F32)], axis=0
    ).T
    sgrid[...] = small.astype(BF16).reshape(nx, ny, r, 128)
    s_ring.start()
    k_copy.wait_recv()
    kgrid[...] = (kgrid[...].astype(F32) + kback[...].astype(F32)).astype(BF16)
    for ring in k_rings:
        ring.start()
    for e in range(2):
        seconds[e].end(keeper(tt, halves, e))
    s_ring.middle()
    for copy in load[5:]:
        copy.wait()

    fields = [(tm, 0, r), (tm, r, r)] + [(tm, 2 * r + rq * k, rq) for k in range(3)]
    fields += [(tt, 0, r)] + [(tt, r + rq * k, rq) for k in range(3)]
    to_zl = flip("zl")
    halves_to_send(fields, zsend, zl)
    z_copy = link.copy(zsend, zrecv, to_zl)
    s_ring.end(keeper(ts, s_halves))
    s_second = Ring(link, "y", lambda i, h: ts.at[i, s_halves[h]], ss0, ss1)
    s_second.start()
    for ring in k_rings:
        ring.middle()
    z_copy.wait_recv()
    add_halves(fields, zrecv, y, zl)
    quarters_to_send(fields, y, csend, core)
    c_copy = link.copy(csend, crecv, mate)
    s_second.middle()
    k_seconds = [
        Ring(link, "y", lambda i, h: tka.at[i, k_halves[h]], kka0, kka1),
        Ring(link, "x", lambda i, h: tkb.at[i, k_halves[h]], kkb0, kkb1),
    ]
    for e in range(2):
        k_rings[e].end(keeper((tka, tkb)[e], k_halves))
        k_seconds[e].start()
    c_copy.wait_recv()
    targets = [(gate_ref, None), (up_ref, None)] + [(down_ref, k) for k in range(3)]
    targets += [(query_ref, None)] + [(out_ref, k) for k in range(3)]
    place_quarters(fields, targets, y, crecv, core)
    save(5, 6, 7, 8, 9)
    for ring in k_seconds:
        ring.middle()

    def store_small(h, value):
        tsm[s_halves[h]] = value

    s_second.end(store_small)
    for e in range(2):
        k_seconds[e].end(keeper(tk, k_halves, e))

    piece = r // 8
    for p in range(8):
        rows = slice(piece * (p % 4), piece * (p % 4) + piece)
        pieces[p, 0:piece, 0:QW] = tk[p // 4, rows]
        pieces[p, 0:piece, QW:] = tsm[piece * p : piece * p + piece]

    def other(m):
        return (
            lax.rem(zl + m // 4, 2), lax.rem(core + m // 2 % 2, 2), lax.rem(zh + m % 2, 2)
        )

    p_copies = []
    for m in range(1, 8):
        at = other(m)
        p_copies.append(
            link.copy(
                pieces.at[4 * at[0] + 2 * at[1] + at[2]],
                landed.at[m],
                {"zl": at[0], "c": at[1], "zh": at[2]},
            )
        )
    late_second.wait_recv()
    late_third.wait_recv()
    for j in range(CHUNKS):
        output_ref[part(j)] = (
            middle_ref[part(j)]
            + ko[part(j)].astype(F32)
            + lb[part(j)].astype(F32)
            + lr[part(j)].astype(F32)
        ).astype(BF16)
    save(0)
    for copy in p_copies:
        copy.wait_recv()
    mine = pieces[4 * zl + 2 * core + zh]
    own_half = mine + landed[1] + landed[4] + landed[5]
    other_half = landed[2] + landed[3] + landed[6] + landed[7]
    first = core == 0
    kv_ref[:, 0:QW] = jnp.where(first, own_half, other_half)[0:piece, 0:QW]
    kv_ref[:, QW:] = jnp.where(first, other_half, own_half)[0:piece, 0:QW]
    total = (own_half + other_half)[:, QW:]
    total = total.T
    first_ref[...] = total[0:8, 0:piece]
    second_ref[...] = total[8:16, 0:piece]
    norm_ref[...] = total[16:24, 0:piece]
    save(1, 2, 3, 4)
    for ring in seconds + k_rings + [s_ring] + k_seconds + [s_second]:
        ring.close()
    for copy in [late_first, late_second, late_third, k_copy, z_copy, c_copy] + p_copies:
        copy.wait_send()
    for copy in saved:
        copy.wait()


def last_call(nx, ny, *operands):
    r, rq = expert_block(nx, ny)
    block, mlp_block, k_block = r + 3 * rq, 2 * r + 3 * rq, r // 2
    zrows = (block + mlp_block) // 2

    def small_buffers(lead):
        return [pltpu.VMEM((3,) + lead + (s.stop - s.start, 128), BF16) for s in split(r)]

    copies = 4 * 12 + 13
    results = [
        ((TOK, D), BF16),
        ((r // 8, 2 * QW), F32),
        ((8, r // 8), F32),
        ((8, r // 8), F32),
        ((8, r // 8), F32),
        ((4, r // 4, FF), F32),
        ((4, r // 4, FF), F32),
        ((4, rq // 4, D), F32),
        ((4, r // 4, QW), F32),
        ((4, rq // 4, D), F32),
    ]
    return pl.pallas_call(
        partial(last_kernel, nx, ny),
        out_shape=tuple(jax.ShapeDtypeStruct(*a) for a in results),
        in_specs=[VSPEC] * 6 + [ANY] * 6,
        out_specs=(ANY,) * len(results),
        scratch_shapes=[pltpu.VMEM(*a) for a in results]
        + [
            pltpu.VMEM((4, TOK, D), BF16),
            pltpu.VMEM((4 * TOK, 2 * QW), BF16),
            pltpu.VMEM((2, mlp_block, 512), F32),
            pltpu.VMEM((TOK, D), F32),
            pltpu.VMEM((D // nx, 2 * QW), BF16),
        ]
        + [ROWS_BUF] * 8
        + [
            pltpu.VMEM((2, nx, ny, k_block, 512), BF16),
            pltpu.VMEM((2, nx, ny, k_block, 512), BF16),
            pltpu.VMEM((2, nx, ny, k_block, 512), BF16),
            pltpu.VMEM((nx, ny, r, 128), BF16),
        ]
        + ring_buffers((ny,), k_block)
        + ring_buffers((nx,), k_block)
        + small_buffers((ny,))
        + [
            pltpu.VMEM((ny, k_block, 512), BF16),
            pltpu.VMEM((nx, k_block, 512), BF16),
            pltpu.VMEM((ny, r, 128), BF16),
        ]
        + ring_buffers((), block) * 2
        + ring_buffers((), k_block) * 2
        + small_buffers(())
        + [
            pltpu.VMEM((2, block, 512), F32),
            pltpu.VMEM((2, k_block, 512), F32),
            pltpu.VMEM((r, 128), F32),
            pltpu.VMEM((2, zrows, 512), BF16),
            pltpu.VMEM((2, zrows, 512), BF16),
            pltpu.VMEM((2, zrows, 512), F32),
            pltpu.VMEM((2, zrows // 2, 512), F32),
            pltpu.VMEM((2, zrows // 2, 512), F32),
            pltpu.VMEM((8, (r // 8 + 7) // 8 * 8, QW + 128), F32),
            pltpu.VMEM((8, (r // 8 + 7) // 8 * 8, QW + 128), F32),
            pltpu.SemaphoreType.DMA((8,)),
            pltpu.SemaphoreType.DMA((len(results),)),
            pltpu.SemaphoreType.DMA((copies,)),
            pltpu.SemaphoreType.DMA((copies,)),
        ],
        compiler_params=remote_params(60, 4),
        cost_estimate=pl.CostEstimate(flops=10**9, bytes_accessed=150 * 10**6, transcendentals=0),
        name="last_sums",
    )(*operands)


def copy_kernel(norms_ref, *refs):
    n = (len(refs) - 6) // 3
    sources, targets, vectors = refs[:n], refs[n : 2 * n], refs[2 * n : 2 * n + 2]
    bufs, held = refs[2 * n + 2 : 3 * n + 2], refs[3 * n + 2 : 3 * n + 4]
    came = fetch(list(zip(sources, bufs)), refs[-2])
    left = []

    def leave(source, target):
        copy = pltpu.make_async_copy(source, target, refs[-1].at[len(left)])
        copy.start()
        left.append(copy)

    for k in range(2):
        held[k][...] = norms_ref[1 - k]
        leave(held[k], vectors[k])
    for k in range(n):
        came[k].wait()
        leave(bufs[k], targets[k])
    for copy in left:
        copy.wait()


def copy_call(norms, *arrays):
    count, n = norms.shape[1], len(arrays)
    return pl.pallas_call(
        copy_kernel,
        out_shape=tuple(jax.ShapeDtypeStruct(a.shape, a.dtype) for a in arrays)
        + (jax.ShapeDtypeStruct((count,), F32),) * 2,
        in_specs=[VSPEC] + [ANY] * n,
        out_specs=(ANY,) * (n + 2),
        scratch_shapes=[pltpu.VMEM(a.shape, a.dtype) for a in arrays]
        + [pltpu.VMEM((count,), F32)] * 2
        + [pltpu.SemaphoreType.DMA((n,)), pltpu.SemaphoreType.DMA((n + 2,))],
        compiler_params=params(60),
        name="results",
    )(norms, *arrays)


def per_device(
    inputs, cotangent, norm_one, kv_weight, attn_router, query_experts, out_experts, norm_two,
    mlp_router, gate_experts, up_experts, down_experts, attn_routes, mlp_routes, slot_order,
    seg_lengths, seg_parents,
):
    nx, ny = lax.axis_size("x"), lax.axis_size("y")
    router_one, router_two = attn_router.T, mlp_router.T
    normed, keys, values, rows, q, attended, normed_twos, cots, gates, metas, middle, lse = forward_call(
        seg_lengths, seg_parents, slot_order, jnp.swapaxes(attn_routes, 2, 3),
        jnp.swapaxes(mlp_routes, 2, 3), inputs, norm_one, norm_two,
        router_one, cotangent, kv_weight, query_experts, out_experts,
    )
    r, rq = expert_block(nx, ny)
    grad_norm_two, grad_router_two, sums_a, sums_b, grads_in, keep_out, give_out, grad_middle = mlp_call(
        nx, ny, metas, router_two, norm_two, normed_twos, cotangent, cots, middle,
        gate_experts.reshape(4, nx, ny, r, FF), up_experts.reshape(4, nx, ny, r, FF),
        down_experts.reshape(4, nx, ny, rq, D),
    )
    grad_norm_one, grad_router_one, sums_a, sums_b, grad_kv, sums_mlp, input_grad = attn_back_call(
        nx, ny, metas, gates, lse, router_one, norm_one, sums_a, sums_b, inputs, grad_middle, normed,
        grads_in, keys, values, q, attended, query_experts, out_experts.reshape(4, nx, ny, rq, D),
        kv_weight, rows,
    )
    output, kv, router_one_grad, router_two_grad, norms, gate, up, down, query, out = last_call(
        nx, ny, grad_router_one, grad_router_two, grad_norm_two, grad_norm_one, sums_a, sums_b, sums_mlp,
        middle, keep_out, give_out, normed, grad_kv,
    )
    (
        output, input_grad, kv, router_one_grad, query, out, router_two_grad, gate, up, down, norm_one_grad,
        norm_two_grad,
    ) = copy_call(
        norms, output, input_grad, kv, router_one_grad, query, out, router_two_grad, gate, up, down
    )
    return (
        output, input_grad, norm_one_grad, kv, router_one_grad.T, query, out, norm_two_grad,
        router_two_grad.T, gate, up, down,
    )


def solution(mesh):
    total = mesh.devices.size
    grid = mesh.devices.reshape(4, total // 32, 2, 2, 2)
    fine = Mesh(grid, ("x", "y", "zl", "c", "zh"))
    copies = ("x", "y", "zl", "c")
    every = copies + ("zh",)
    weight = P("zh", None, None)
    placed = (
        P(every, None),
        P(every, None),
        P(),
        P(),
        P(),
        weight,
        weight,
        P(),
        P(),
        weight,
        weight,
        weight,
        P(copies, None, None, None),
        P(copies, None, None, None),
        P(copies, None, None, None),
        P(copies, None, None),
        P(copies, None, None),
    )
    grad = P("zh", copies, None)
    return jax.shard_map(
        per_device,
        mesh=fine,
        in_specs=placed,
        out_specs=(
            P(every, None),
            P(every, None),
            P(every),
            P(every, None),
            P(every, None),
            grad,
            grad,
            P(every),
            P(every, None),
            grad,
            grad,
            grad,
        ),
        check_vma=False,
    )
```
